512 devices in a mesh: gx: 128 (over x, z, y_hi), gy: 4 (over y_lo, core).
Axes of the slice: x: 4, y: 8 (y_hi: 4, y_lo: 2; y = y_hi * 2 + y_lo), z: 8, core: 2. Of those that a mesh axis runs over, the one named last changes fastest.
Arguments:
- positions: float32 [3, 65536], P(None, ('gx', 'gy')), may hold values from 0 to 2
- velocities: float32 [3, 65536], P(None, ('gx', 'gy')), may hold values from -6 to 6
- forces: float32 [3, 65536], P(None, ('gx', 'gy')), may hold values from -6 to 6
- species: int32 [65536], P(('gx', 'gy')), may hold values from 0 to 4
- inv_mass: float32 [5], replicated, may hold values from 0.5 to 2
- xface_list: int32 [32768], P(('gx', 'gy')), may hold values from 0 to 127
- yface_list: int32 [65536], P(('gx', 'gy')), may hold values from 0 to 191
- edge_center: int32 [131072], P(('gx', 'gy')), may hold values from 0 to 127
- edge_neighbor: int32 [131072], P(('gx', 'gy')), may hold values from 0 to 319, as said below
- edge_count: int32 [512], P(('gx', 'gy')), may hold values from 192 to 256, as said below
- migrants: int32 [4096, 8], P(('gx', 'gy')), may hold values from -1 to 127, as said below
- embed_center: float32 [5, 128], replicated, may hold values from -6 to 6
- embed_neighbor: float32 [5, 128], replicated, may hold values from -6 to 6
- radial_weight: float32 [8, 128], replicated, may hold values from -2 to 2
- tensor_one: float32 [128, 128], replicated, may hold values from -0.5 to 0.5
- mix_one: float32 [384, 128], replicated, may hold values from -0.3125 to 0.3125
- tensor_two: float32 [128, 128], replicated, may hold values from -0.5 to 0.5
- mix_two: float32 [384, 128], replicated, may hold values from -0.3125 to 0.3125
- final_weight: float32 [128, 128], replicated, may hold values from -0.5 to 0.5
- energy_out: float32 [128], replicated, may hold values from -0.5 to 0.5
Outputs:
- new_positions: float32 [3, 65536], P(None, ('gx', 'gy'))
- new_velocities: float32 [3, 65536], P(None, ('gx', 'gy'))
- new_forces: float32 [3, 65536], P(None, ('gx', 'gy'))
- arrivals: float32 [384, 12, 64], P('gx', 'gy')
The draws below stay inside these ranges and needn't reach their ends.
Inputs may be any that keep to these rules, and one draw needn't show every extreme that they name: `edge_neighbor`: the first 192 slots of each brick name every ghost atom once. `edge_count`: some brick is full and some brick holds exactly 192. `migrants`: an atom is listed at most once per brick; live slots come first in each list, at least half of each list is live, and some list is full.
All inputs are finite; a program needn't handle non-finite values.
Results may differ from the reference program's by a relative error of at most 0.0003.
Values sent between devices are 32-bit elements; how exact they have to be, the bound alone decides.
A program may use at most 64 MiB of HBM per device.

```python
import math
import jax
import jax.numpy as jnp
from jax import lax

A_DEV = 128
XFACE = 32
YFACE = 64
L_DEV = 320
E_DEV = 256
MIGD = 8
ATOMS = 65536
H = 128
TC = 128
NSPEC = 5
NB = 8
STEPS = 1
N_GX = 128
N_GY = 4


def draw_edge_neighbor(key, part):
    key = jax.random.fold_in(key, 11)
    device_count = N_GX * N_GY
    ghost_total = 2 * XFACE + 2 * YFACE

    def per_device(device_key):
        key_cover, key_rest = jax.random.split(device_key)
        covering = A_DEV + jax.random.permutation(key_cover, ghost_total)
        remaining = jax.random.randint(key_rest, (E_DEV - ghost_total,), 0, L_DEV)
        return jnp.concatenate([covering.astype(jnp.int32), remaining.astype(jnp.int32)])
    return jax.vmap(per_device)(jax.random.split(key, device_count)).reshape(-1)


def draw_edge_count(key, part):
    key = jax.random.fold_in(key, 12)
    device_count = N_GX * N_GY
    key_draw, key_pick = jax.random.split(key)
    least = 3 * E_DEV // 4
    counts = jax.random.randint(key_draw, (device_count,), least, E_DEV + 1)
    ordering = jax.random.permutation(key_pick, device_count)
    counts = counts.at[ordering[0]].set(E_DEV).at[ordering[1]].set(least)
    return counts.astype(jnp.int32)


def draw_migrants(key, part):
    key = jax.random.fold_in(key, 13)
    device_count = N_GX * N_GY
    key_perm, key_fill, key_full = jax.random.split(key, 3)

    def per_device(device_key):
        return jax.random.permutation(device_key, A_DEV)[:8 * MIGD].reshape(8, MIGD)
    chosen = jax.vmap(per_device)(jax.random.split(key_perm, device_count)).reshape(device_count * 8, MIGD)
    filled = jax.random.randint(key_fill, (device_count * 8, 1), MIGD // 2, MIGD + 1)
    full_row = jax.random.randint(key_full, (), 0, device_count * 8)
    row_ids = jnp.arange(device_count * 8, dtype=jnp.int32)[:, None]
    filled = jnp.where(row_ids == full_row, MIGD, filled)
    slot_ids = jnp.arange(MIGD, dtype=jnp.int32)[None, :]
    return jnp.where(slot_ids < filled, chosen, -1).astype(jnp.int32)


def with_ends(values, key, low, largest):
    dims = values.shape
    spot = [jax.random.randint(jax.random.fold_in(key, axis), (), 0, dims[axis]) for axis in range(len(dims))]
    values = values.at[tuple(spot)].set(low)
    longest = dims.index(max(dims))
    spot[longest] = (spot[longest] + 1) % dims[longest]
    return values.at[tuple(spot)].set(largest)


def level_of(key, extent, cuts, low, high):
    def one(axis_at, blocks):
        draws = jax.random.uniform(jax.random.fold_in(jax.random.fold_in(key, 6), axis_at), (blocks,), jnp.float32, low / len(cuts), high / len(cuts))
        return jnp.repeat(jnp.exp(draws), extent[axis_at] // blocks).reshape((-1,) + (1,) * (len(extent) - axis_at - 1))

    factor_of = one(*cuts[0])
    for cut in cuts[1:]:
        factor_of = factor_of * one(*cut)
    return factor_of


def normal_values(key, extent, spread, most, cuts=(), kind=jnp.bfloat16):
    values = jax.random.normal(key, extent, jnp.float32) * spread
    if len(cuts) > 0:
        values = level_of(key, extent, cuts, -0.22, 0.18) * values
    return jnp.clip(values, min=-most, max=most).astype(kind)


def setup_inputs(seed: int = 0) -> dict:
    key_list = jax.random.split(jax.random.key(seed), 21)
    return {
        "positions": jnp.clip(2.0 * jax.random.uniform(key_list[0], (3, ATOMS), jnp.float32) ** level_of(key_list[0], (3, ATOMS), ((1, 512),), -0.2, 0.2), 0.0, 2.0),
        "velocities": normal_values(key_list[1], (3, ATOMS), 1.0, 6.0, ((1, 512),), jnp.float32),
        "forces": normal_values(key_list[2], (3, ATOMS), 1.0, 6.0, ((1, 512),), jnp.float32),
        "species": with_ends(jax.random.randint(key_list[3], (ATOMS,), 0, NSPEC), jax.random.fold_in(key_list[3], 1), 0, NSPEC - 1).astype(jnp.int32),
        "inv_mass": jnp.clip(jnp.exp(jax.random.uniform(key_list[4], (NSPEC,), jnp.float32, math.log(0.5), math.log(2.0))), 0.5, 2.0),
        "xface_list": with_ends(jax.random.randint(key_list[5], (N_GX * N_GY * 2 * XFACE,), 0, A_DEV), jax.random.fold_in(key_list[5], 1), 0, A_DEV - 1).astype(jnp.int32),
        "yface_list": with_ends(jax.random.randint(key_list[6], (N_GX * N_GY * 2 * YFACE,), 0, A_DEV + 2 * XFACE), jax.random.fold_in(key_list[6], 1), 0, (A_DEV + 2 * XFACE) - 1).astype(jnp.int32),
        "edge_center": with_ends(jax.random.randint(key_list[7], (N_GX * N_GY * E_DEV,), 0, A_DEV), jax.random.fold_in(key_list[7], 1), 0, A_DEV - 1).astype(jnp.int32),
        "edge_neighbor": draw_edge_neighbor(jax.random.fold_in(key_list[20], 71), 0),
        "edge_count": draw_edge_count(jax.random.fold_in(key_list[20], 71), 0),
        "migrants": draw_migrants(jax.random.fold_in(key_list[20], 71), 0),
        "embed_center": normal_values(key_list[11], (NSPEC, H), 1.0, 6.0, (), jnp.float32),
        "embed_neighbor": normal_values(key_list[12], (NSPEC, H), 1.0, 6.0, (), jnp.float32),
        "radial_weight": normal_values(key_list[13], (NB, H), NB ** -0.5, 2.0, (), jnp.float32),
        "tensor_one": normal_values(key_list[14], (H, TC), H ** -0.5, 0.5, (), jnp.float32),
        "mix_one": normal_values(key_list[15], (3 * TC, H), (3 * TC) ** -0.5, 0.3125, (), jnp.float32),
        "tensor_two": normal_values(key_list[16], (H, TC), H ** -0.5, 0.5, (), jnp.float32),
        "mix_two": normal_values(key_list[17], (3 * TC, H), (3 * TC) ** -0.5, 0.3125, (), jnp.float32),
        "final_weight": normal_values(key_list[18], (H, H), H ** -0.5, 0.5, (), jnp.float32),
        "energy_out": normal_values(key_list[19], (H,), H ** -0.5, 0.5, (), jnp.float32),
    }


BOX_SIDE = 2.0
CUTOFF = 2.0
TIME_STEP = 0.05
WIDTHS = tuple((0.1 * 20.0 ** (k / 7.0) for k in range(8)))

def product(left, right):
    return jnp.dot(left, right, precision=lax.Precision.HIGHEST, preferred_element_type=jnp.float32)

def harmonics(offset_vec):
    along_x, along_y, along_z = (offset_vec[0], offset_vec[1], offset_vec[2])
    constant = jnp.ones_like(along_x)
    return jnp.stack([constant, along_x, along_y, along_z, along_x * along_y, along_y * along_z, along_z * along_x, 0.5 * (along_x * along_x - along_y * along_y), (2.0 * along_z * along_z - along_x * along_x - along_y * along_y) * 0.28867513459481287], axis=1)

def brick_energy(coords, ext_species, edge_center, edge_neighbor, edge_count, weights_all, owned_count):
    embed_center, embed_neighbor, radial_weight, tensor_one, mix_one, tensor_two, mix_two, final_weight, energy_out = weights_all
    species_ids = jnp.arange(embed_center.shape[0], dtype=jnp.int32)
    offset_vec = (jnp.take(coords, edge_neighbor, axis=1) - jnp.take(coords, edge_center, axis=1)) / CUTOFF
    squared = lax.optimization_barrier(jnp.sum(offset_vec * offset_vec, axis=0))
    radial = jnp.exp(-squared[:, None] / jnp.asarray(WIDTHS, dtype=jnp.float32)[None, :])
    center_hot = (jnp.take(ext_species, edge_center)[:, None] == species_ids[None, :]).astype(jnp.float32)
    neighbor_hot = (jnp.take(ext_species, edge_neighbor)[:, None] == species_ids[None, :]).astype(jnp.float32)
    hidden = jax.nn.silu(product(radial, radial_weight) + product(center_hot, embed_center) + product(neighbor_hot, embed_neighbor))
    harmonic = harmonics(offset_vec)
    live_mask = (jnp.arange(edge_center.shape[0], dtype=jnp.int32) < edge_count[0]).astype(jnp.float32)
    for tensor_w, mix_w in ((tensor_one, mix_one), (tensor_two, mix_two)):
        weight = product(hidden, tensor_w) * live_mask[:, None]
        outer_prod = harmonic[:, :, None] * weight[:, None, :]
        environment = jax.ops.segment_sum(outer_prod, edge_center, num_segments=owned_count)
        projected = jnp.take(environment, edge_center, axis=0) * harmonic[:, :, None]
        invariants = jnp.concatenate([projected[:, 0], lax.optimization_barrier(jnp.sum(projected[:, 1:4], axis=1)), lax.optimization_barrier(jnp.sum(projected[:, 4:9], axis=1))], axis=1)
        hidden = hidden + jax.nn.silu(product(invariants, mix_w))
    edge_energy = product(jax.nn.silu(product(hidden, final_weight)), energy_out)
    return jnp.sum(edge_energy * live_mask)

def extend_bricks(record, xface_all, yface_all):
    row_count = record.shape[2]
    x_shift = jnp.zeros((row_count, 1), jnp.float32).at[0, 0].set(BOX_SIDE)
    y_shift = jnp.zeros((row_count, 1), jnp.float32).at[1, 0].set(BOX_SIDE)
    xface_width = xface_all.shape[-1] // 2
    yface_width = yface_all.shape[-1] // 2
    send_x = jnp.take_along_axis(record, jnp.broadcast_to(xface_all[:, :, None, :], record.shape[:3] + xface_all.shape[-1:]), axis=3)
    extended = jnp.concatenate([record, jnp.roll(send_x[..., xface_width:], 1, axis=0) - x_shift, jnp.roll(send_x[..., :xface_width], -1, axis=0) + x_shift], axis=3)
    send_y = jnp.take_along_axis(extended, jnp.broadcast_to(yface_all[:, :, None, :], extended.shape[:3] + yface_all.shape[-1:]), axis=3)
    return jnp.concatenate([extended, jnp.roll(send_y[..., yface_width:], 1, axis=1) - y_shift, jnp.roll(send_y[..., :yface_width], -1, axis=1) + y_shift], axis=3)

def reference(positions, velocities, forces, species, inv_mass, xface_list, yface_list, edge_center, edge_neighbor, edge_count, migrants, embed_center, embed_neighbor, radial_weight, tensor_one, mix_one, tensor_two, mix_two, final_weight, energy_out):
    weights_all = (embed_center, embed_neighbor, radial_weight, tensor_one, mix_one, tensor_two, mix_two, final_weight, energy_out)
    device_count = N_GX * N_GY
    group_count = device_count // 8

    def to_bricks(field):
        return field.reshape(3, N_GX, N_GY, A_DEV).transpose(1, 2, 0, 3)
    species_float = species.reshape(N_GX, N_GY, A_DEV).astype(jnp.float32)
    xface_all = xface_list.reshape(N_GX, N_GY, 2 * XFACE)
    yface_all = yface_list.reshape(N_GX, N_GY, 2 * YFACE)
    centers = edge_center.reshape(group_count, 8, E_DEV)
    neighbors = edge_neighbor.reshape(group_count, 8, E_DEV)
    counts = edge_count.reshape(group_count, 8, 1)

    def group_energy(group_args):
        ext_group, cen_group, nbr_group, cnt_group = group_args

        def single(ext_one, cen_one, nbr_one, cnt_one):
            return brick_energy(ext_one[:3], lax.stop_gradient(ext_one[3]).astype(jnp.int32), cen_one, nbr_one, cnt_one, weights_all, A_DEV)
        return jnp.sum(jax.vmap(single)(ext_group, cen_group, nbr_group, cnt_group))

    def total_energy(coords_b):
        record = jnp.concatenate([coords_b, species_float[:, :, None, :]], axis=2)
        complete = extend_bricks(record, xface_all, yface_all).reshape(group_count, 8, 4, L_DEV)
        return jnp.sum(lax.map(jax.checkpoint(group_energy), (complete, centers, neighbors, counts)))
    gradient_fn = jax.grad(total_energy)
    species_ids = jnp.arange(NSPEC, dtype=jnp.int32)
    atom_inv = lax.optimization_barrier(jnp.sum((species[:, None] == species_ids[None, :]).astype(jnp.float32) * inv_mass[None, :], axis=1))
    atom_inv = atom_inv.reshape(N_GX, N_GY, 1, A_DEV)
    coords_b = to_bricks(positions)
    veloc_b = to_bricks(velocities)
    force_b = to_bricks(forces)
    for step_index in range(STEPS):
        halfway = veloc_b + 0.5 * TIME_STEP * force_b * atom_inv
        coords_b = coords_b + TIME_STEP * halfway
        force_b = -gradient_fn(coords_b)
        veloc_b = halfway + 0.5 * TIME_STEP * force_b * atom_inv
    fields = jnp.concatenate([coords_b, veloc_b, species_float[:, :, None, :], jnp.ones_like(species_float)[:, :, None, :]], axis=2)
    slot_lists = migrants.reshape(N_GX, N_GY, 8, MIGD)
    cell_list = []
    for cell_index in range(9):
        if cell_index == 4:
            cell_list.append(jnp.zeros((N_GX, N_GY, 8, MIGD), jnp.float32))
            continue
        list_row = cell_index if cell_index < 4 else cell_index - 1
        slot_index = slot_lists[:, :, list_row, :]
        valid_mask = (slot_index >= 0).astype(jnp.float32)
        picked = jnp.take_along_axis(fields, jnp.broadcast_to(jnp.maximum(slot_index, 0)[:, :, None, :], (N_GX, N_GY, 8, MIGD)), axis=3)
        moved = jnp.zeros((8, 1), jnp.float32).at[0, 0].set((cell_index // 3 - 1) * BOX_SIDE).at[1, 0].set((cell_index % 3 - 1) * BOX_SIDE)
        cell_list.append((picked - moved) * valid_mask[:, :, None, :])
    outgoing = jnp.stack(cell_list, axis=2).reshape(N_GX, N_GY, 3, 3, 8 * MIGD)
    arrived_rows = []
    for row_a in range(3):
        arrived_cols = []
        for col_b in range(3):
            arrived_cols.append(jnp.roll(outgoing[:, :, row_a, col_b], (row_a - 1, col_b - 1), axis=(0, 1)))
        arrived_rows.append(jnp.stack(arrived_cols, axis=2))
    arrivals = jnp.stack(arrived_rows, axis=2).transpose(0, 2, 1, 3, 4).reshape(3 * N_GX, 3 * N_GY, 8 * MIGD)

    def from_bricks(field):
        return field.transpose(2, 0, 1, 3).reshape(3, ATOMS)
    return (from_bricks(coords_b), from_bricks(veloc_b), from_bricks(force_b), arrivals)
```

```python
import math

import jax
import jax.numpy as jnp
from jax import lax
from jax.experimental import pallas as pl
from jax.experimental.pallas import tpu as pltpu
from jax.sharding import PartitionSpec as P

BOX_SIDE = 2.0
CUTOFF = 2.0
TIME_STEP = 0.05
WIDTHS = tuple((0.1 * 20.0 ** (k / 7.0) for k in range(8)))
Y20 = 0.28867513459481287
MESH = pl.DeviceIdType.MESH
F32 = jnp.float32
BF16 = jnp.bfloat16

MOVES = tuple((a, b) for a in (-1, 0, 1) for b in (-1, 0, 1) if (a, b) != (0, 0))


def cell(dx, dy):
    return (dx + 1) * 3 + dy + 1


def iota(shape, dim):
    return lax.broadcasted_iota(jnp.int32, shape, dim)


def halves(value):
    high = value.astype(BF16)
    low = (value - high.astype(F32)).astype(BF16)
    return high, low


def halves_f32(value):
    high = value.astype(BF16).astype(F32)
    return high, value - high


def dot(left, right, contract=(1, 0)):
    return lax.dot_general(
        left, right, (((contract[0],), (contract[1],)), ((), ())), preferred_element_type=F32
    )


def lanes_at(tile, index):
    return jnp.take_along_axis(
        tile, jnp.broadcast_to(index, tile.shape), axis=1, mode="promise_in_bounds"
    )


def sigmoid(value):
    return 0.5 + 0.5 * jnp.tanh(0.5 * value)


def row_const(values, shape):
    rows = iota(shape, 0)
    result = jnp.zeros(shape, F32)
    for index, value in enumerate(values):
        result = jnp.where(rows == index, F32(value), result)
    return result


def kernel(
    n_gx,
    n_gy,
    pos_ref,
    vel_ref,
    frc_ref,
    spec_ref,
    inv_mass_ref,
    xface_ref,
    yface_ref,
    center_ref,
    neighbor_ref,
    count_ref,
    migrants_ref,
    emb_c_ref,
    emb_n_ref,
    radial_ref,
    tensor1_ref,
    mix1_ref,
    tensor2_ref,
    mix2_ref,
    final_ref,
    eout_ref,
    new_pos_ref,
    new_vel_ref,
    new_frc_ref,
    arr_ref,
    send_x,
    send_y,
    recv_a,
    send_w,
    send_z,
    send_d,
    recv_c,
    send_m,
    recv_m,
    sems_out,
    sems_in,
):
    gx = lax.axis_index("gx")
    gy = lax.axis_index("gy")

    def place(dx, dy):
        return (lax.rem(gx + (dx + n_gx), n_gx), lax.rem(gy + (dy + n_gy), n_gy))

    def copy(phase, move, source, target):
        slot = cell(*move)
        return pltpu.make_async_remote_copy(
            src_ref=source,
            dst_ref=target.at[slot],
            send_sem=sems_out.at[phase, slot],
            recv_sem=sems_in.at[phase, slot],
            device_id=place(*move),
            device_id_type=MESH,
        )

    barrier = pltpu.get_barrier_semaphore()
    for move in MOVES:
        pl.semaphore_signal(barrier, inc=1, device_id=place(*move), device_id_type=MESH)

    lane = iota((1, 128), 1)
    rows = iota((8, 128), 0)
    low_x = (lane % 64) < 32
    low_y = lane < 64

    species = spec_ref[...].reshape(1, 128)
    inv_mass = jnp.zeros((1, 128), F32)
    for k in range(inv_mass_ref.shape[0]):
        inv_mass = jnp.where(species == k, inv_mass_ref[k], inv_mass)
    halfway = vel_ref[...] + 0.5 * TIME_STEP * frc_ref[...] * inv_mass
    coords = pos_ref[...] + TIME_STEP * halfway
    new_pos_ref[...] = coords
    species_row = species.astype(F32)
    minus = jnp.full((1, 128), -1.0, F32)
    record = jnp.concatenate([coords, species_row, minus, jnp.zeros((3, 128), F32)], axis=0)

    xface = xface_ref[...].reshape(1, 64)
    xface2 = jnp.concatenate([xface, xface], axis=1)
    yface = yface_ref[...].reshape(1, 128)
    y_owned = yface < 128
    send_x[...] = lanes_at(record, xface2)
    send_y[...] = jnp.where(
        rows == 4, yface.astype(F32), lanes_at(record, jnp.where(y_owned, yface, 0))
    )
    pl.semaphore_wait(barrier, len(MOVES))
    first = [copy(0, m, send_y if m[0] == 0 else send_x, recv_a) for m in MOVES]
    for c in first:
        c.start()

    neighbor = neighbor_ref[...].reshape(1, 256)
    center = center_ref[...].reshape(1, 256)
    live = iota((1, 256), 1) < count_ref[0]
    place_n = jnp.where(
        neighbor < 128,
        neighbor,
        jnp.where(neighbor < 192, ((neighbor - 128) ^ 32) + 128, ((neighbor - 192) ^ 64) + 256),
    )
    hot_n = (iota((384, 256), 0) == place_n).astype(F32).astype(BF16)
    hot_c = (iota((128, 256), 0) == center).astype(F32).astype(BF16)
    face_rows = jnp.concatenate([jnp.where(y_owned, yface, -1), xface2], axis=1)
    hot_f = (iota((128, 256), 0) == face_rows).astype(F32).astype(BF16)
    c_live = center.astype(F32)
    rows_e = iota((8, 256), 0)
    left_c = jnp.where(rows_e == 0, jnp.where(live, c_live, -1.0), jnp.where(rows_e == 1, 1.0, 0.0))
    right_c = jnp.where(rows_e == 0, 1.0, jnp.where(rows_e == 1, jnp.where(live, -c_live, 2.0), 0.0))
    same = dot(left_c.astype(BF16), right_c.astype(BF16), (0, 0)) == 0.0
    k0 = same.astype(F32).astype(BF16)

    def merged(tensor_ref, mix_ref):
        tensor = tensor_ref[...]
        width = tensor.shape[1]
        high, low = halves(
            jnp.concatenate(
                [
                    lax.dot_general(
                        tensor,
                        mix_ref[pl.ds(width * deg, width), :],
                        (((1,), (0,)), ((), ())),
                        precision=lax.Precision.HIGHEST,
                        preferred_element_type=F32,
                    )
                    for deg in range(3)
                ],
                axis=1,
            )
        )
        return high, low

    layers = (merged(tensor1_ref, mix1_ref), merged(tensor2_ref, mix2_ref))
    final_h, final_l = halves(final_ref[...])
    pad3 = jnp.zeros((3, 128), F32)
    table = jnp.concatenate([radial_ref[...], emb_c_ref[...], pad3, emb_n_ref[...], pad3], axis=0)
    table_h, table_l = halves_f32(table)
    table_cat = jnp.concatenate(
        [table_h, table_l, table_h[:8], jnp.zeros((8, 128), F32)], axis=0
    ).astype(BF16)
    rad_h, rad_l = table_h[:8], table_l[:8]
    rad_cat = jnp.concatenate([rad_h, rad_l], axis=0).astype(BF16)

    for c in first:
        c.wait_recv()

    def pick4(tiles):
        quarter = lane // 32
        result = tiles[3]
        for q in (2, 1, 0):
            result = jnp.where(quarter == q, tiles[q], result)
        return result

    x_shift = jnp.where(rows == 0, jnp.where(low_x, BOX_SIDE, -BOX_SIDE), 0.0)
    y_shift = jnp.where(rows == 1, jnp.where(low_y, BOX_SIDE, -BOX_SIDE), 0.0)
    ghost_x = jnp.where(low_x, recv_a[cell(-1, 0)], recv_a[cell(1, 0)]) + x_shift
    far_x = (
        pick4(
            [recv_a[cell(-1, -1)], recv_a[cell(1, -1)], recv_a[cell(-1, 1)], recv_a[cell(1, 1)]]
        )
        + x_shift
    )
    ghost_y = jnp.where(low_y, recv_a[cell(0, -1)], recv_a[cell(0, 1)])
    listed = ghost_y[4:5].astype(jnp.int32)
    via_x = listed >= 128
    far_lane = jnp.where(via_x, ((listed - 128) ^ 32) + jnp.where(low_y, 0, 64), 0)
    ghost_y = jnp.where(via_x, lanes_at(far_x, far_lane), ghost_y) + y_shift
    ghost_y = jnp.where(rows == 4, jnp.where(via_x, far_lane.astype(F32), -1.0), ghost_y)

    def edge_side(tiles, index):
        parts = []
        for half in range(2):
            at = index[:, 128 * half : 128 * half + 128]
            result = lanes_at(tiles[0], at & 127)
            for number in range(1, len(tiles)):
                result = jnp.where(
                    at >= 128 * number, lanes_at(tiles[number], at & 127), result
                )
            parts.append(result)
        return jnp.concatenate(parts, axis=1)

    near = edge_side([record, ghost_x, ghost_y], place_n)
    own = edge_side([record], center)
    hot_far = (iota((128, 256), 0) == near[4:5].astype(jnp.int32)).astype(F32).astype(BF16)

    offset = (near - own) * (1.0 / CUTOFF)
    ux, uy, uz = offset[0:1], offset[1:2], offset[2:3]
    squared = ux * ux + uy * uy + uz * uz
    tees = jnp.concatenate(
        [
            ux,
            uy,
            uz,
            ux * uy,
            uy * uz,
            uz * ux,
            0.5 * (ux * ux - uy * uy),
            (2.0 * uz * uz - ux * ux - uy * uy) * Y20,
        ],
        axis=0,
    )
    minus_inv_w = row_const([-1.0 / w for w in WIDTHS], (8, 256))
    radial = jnp.exp(squared * minus_inv_w)
    hot_sc = (rows_e == own[3:4].astype(jnp.int32)).astype(F32)
    hot_sn = (rows_e == near[3:4].astype(jnp.int32)).astype(F32)
    radial_h, radial_l = halves_f32(radial)
    features = jnp.concatenate(
        [radial_h, hot_sc, hot_sn, radial_h, hot_sc, hot_sn, radial_l, jnp.zeros((8, 256), F32)],
        axis=0,
    ).astype(BF16)
    hidden_pre = dot(features, table_cat, (0, 0))

    tees_h, tees_l = halves_f32(tees)
    tees_r = jnp.concatenate([tees_h, tees_l, tees_h, jnp.zeros((8, 256), F32)], axis=0).astype(BF16)

    def degree(mask):
        left = jnp.concatenate([tees_h, tees_h, tees_l, jnp.zeros((8, 256), F32)], axis=0)
        left = jnp.where(mask, left, 0.0).astype(BF16)
        return halves(jnp.where(same, dot(left, tees_r, (0, 0)), 0.0))

    row32 = iota((32, 256), 0) % 8
    k1_h, k1_l = degree(row32 < 3)
    k2_h, k2_l = degree(row32 >= 3)

    k_wide = jnp.concatenate([k0, k1_h, k2_h], axis=1)
    k_wide_l = jnp.concatenate([k1_l, k2_l], axis=1)
    k_tall = jnp.concatenate([k0, k1_h, k2_h], axis=0)
    k_tall_l = jnp.concatenate([k1_l, k2_l], axis=0)

    sig = sigmoid(hidden_pre)
    hidden = hidden_pre * sig
    slope0 = sig * (1.0 + hidden_pre * (1.0 - sig))
    slopes, values = [], []
    for high, low in layers:
        hid_h, hid_l = halves(hidden)
        value = dot(
            jnp.concatenate([hid_h, hid_l, hid_h], axis=1),
            jnp.concatenate([high, high, low], axis=0),
        )
        val_h, val_l = halves(value)
        values.append((val_h, val_l))
        both = dot(
            k_wide,
            jnp.concatenate(
                [
                    jnp.concatenate([val_h[:, 128 * d : 128 * d + 128], val_l[:, 128 * d : 128 * d + 128]], axis=1)
                    for d in range(3)
                ],
                axis=0,
            ),
        )
        rest = dot(k_wide_l, jnp.concatenate([val_h[:, 128:256], val_h[:, 256:384]], axis=0))
        pre = both[:, :128] + both[:, 128:] + rest
        sig = sigmoid(pre)
        hidden = hidden + pre * sig
        slopes.append(sig * (1.0 + pre * (1.0 - sig)))

    hid_h, hid_l = halves(hidden)
    pre = dot(
        jnp.concatenate([hid_h, hid_l, hid_h], axis=1),
        jnp.concatenate([final_h, final_h, final_l], axis=0),
    )
    sig = sigmoid(pre)
    back = eout_ref[...].reshape(1, 128) * (sig * (1.0 + pre * (1.0 - sig)))
    back_h, back_l = halves(back)
    grad = dot(
        jnp.concatenate([back_h, back_l, back_h], axis=1),
        jnp.concatenate([final_h, final_h, final_l], axis=1),
        (1, 1),
    )
    downs = []
    for index in (1, 0):
        high, low = layers[index]
        down_h, down_l = halves(grad * slopes[index])
        downs.append((down_h, down_l))
        both = dot(k_tall, jnp.concatenate([down_h, down_l], axis=1))
        rest = dot(k_tall_l, down_h)
        parts = [both[:256, :128] + both[:256, 128:]]
        for d in (1, 2):
            at = slice(256 * d, 256 * d + 256)
            parts.append(both[at, :128] + both[at, 128:] + rest[256 * d - 256 : 256 * d])
        dv_h, dv_l = halves(jnp.concatenate(parts, axis=1))
        grad = grad + dot(
            jnp.concatenate([dv_h, dv_l, dv_h], axis=1),
            jnp.concatenate([high, high, low], axis=1),
            (1, 1),
        )
    (d2_h, d2_l), (d1_h, d1_l) = downs
    (v1_h, v1_l), (v2_h, v2_l) = values
    outer_left = jnp.concatenate([d1_h, d2_h, d1_l, d2_l, d1_h, d2_h], axis=1)
    moved = []
    for d in (1, 2):
        at = slice(128 * d, 128 * d + 128)
        outer = dot(
            outer_left,
            jnp.concatenate(
                [v1_h[:, at], v2_h[:, at], v1_h[:, at], v2_h[:, at], v1_l[:, at], v2_l[:, at]],
                axis=1,
            ),
            (1, 1),
        )
        out_h, out_l = halves(jnp.where(same, outer, 0.0))
        pair = jnp.concatenate([tees_h, tees_l], axis=0).astype(BF16)
        high_t = tees_h.astype(BF16)
        first_part = dot(pair, out_h) + dot(pair, out_h, (1, 1))
        second_part = dot(high_t, out_l) + dot(high_t, out_l, (1, 1))
        moved.append(first_part[:8] + first_part[8:] + second_part)
    d_tees = jnp.where(rows_e < 3, moved[0], moved[1])

    g_h, g_l = halves(grad * slope0)
    d_radial = dot(rad_cat, g_h, (1, 1))
    d_radial = d_radial[:8] + d_radial[8:] + dot(rad_cat[:8], g_l, (1, 1))
    d_squared = 2.0 * jnp.sum(d_radial * radial * minus_inv_w, axis=0, keepdims=True)
    dxy, dyz, dzx = d_tees[3:4], d_tees[4:5], d_tees[5:6]
    dxx, dzz = d_tees[6:7], (2.0 * Y20) * d_tees[7:8]
    dux = d_tees[0:1] + ux * (d_squared + dxx - dzz) + uy * dxy + uz * dzx
    duy = d_tees[1:2] + uy * (d_squared - dxx - dzz) + ux * dxy + uz * dyz
    duz = d_tees[2:3] + uz * (d_squared + 2.0 * dzz) + uy * dyz + ux * dzx
    d_edge = jnp.concatenate([dux, duy, duz, jnp.zeros((5, 256), F32)], axis=0)
    d_edge = jnp.where(live, d_edge * (1.0 / CUTOFF), 0.0)
    d_edge_h, d_edge_l = halves_f32(d_edge)
    d_pair = jnp.concatenate([d_edge_h, d_edge_l], axis=0).astype(BF16)

    def spread(hot):
        result = dot(d_pair, hot, (1, 1))
        return result[:8] + result[8:]

    on_ghosts = spread(hot_n[128:])
    send_z[...] = on_ghosts[:, :128]
    send_w[...] = on_ghosts[:, 128:]
    send_d[...] = spread(hot_far)
    second = [
        copy(1, m, send_w if m[0] == 0 else send_z if m[1] == 0 else send_d, recv_c) for m in MOVES
    ]
    for c in second:
        c.start()
    on_owned = spread(hot_n[:128]) - spread(hot_c)

    slots = migrants_ref[...]
    slots = jnp.concatenate([slots] * 16, axis=1)

    for c in second:
        c.wait_recv()
    from_y = jnp.where(low_y, recv_c[cell(0, 1)], recv_c[cell(0, -1)])
    from_x = jnp.where(low_x, recv_c[cell(1, 0)], recv_c[cell(-1, 0)])
    from_far = pick4(
        [recv_c[cell(1, 1)], recv_c[cell(-1, 1)], recv_c[cell(1, -1)], recv_c[cell(-1, -1)]]
    )
    from_x = jnp.where(low_y, from_x, 0.0) + from_far
    back_h, back_l = halves_f32(jnp.concatenate([from_y, from_x], axis=1))
    back = dot(jnp.concatenate([back_h, back_l], axis=0).astype(BF16), hot_f, (1, 1))
    force = -(on_owned + back[:8] + back[8:])[:3]
    veloc = halfway + 0.5 * TIME_STEP * force * inv_mass
    new_frc_ref[...] = force
    new_vel_ref[...] = veloc

    valid = slots >= 0
    at = jnp.where(valid, slots, 0)
    fields = [coords[0:1], coords[1:2], coords[2:3], veloc[0:1], veloc[1:2], veloc[2:3], species_row]
    field = lane // 8
    out = jnp.where(field == 7, 1.0, jnp.zeros((8, 128), F32))
    for number, value in enumerate(fields):
        out = jnp.where(field == number, lanes_at(jnp.broadcast_to(value, (8, 128)), at), out)
    dx_col = row_const([BOX_SIDE * m[0] for m in MOVES], (8, 128))
    dy_col = row_const([BOX_SIDE * m[1] for m in MOVES], (8, 128))
    out = out - jnp.where(field == 0, dx_col, jnp.where(field == 1, dy_col, 0.0))
    send_m[...] = jnp.where(valid, out, 0.0)
    third = [copy(2, m, send_m, recv_m) for m in MOVES]
    for c in third:
        c.start()
    for c in third:
        c.wait_recv()
    for a in range(3):
        arr_ref[a] = jnp.concatenate(
            [
                jnp.zeros((1, 64), F32)
                if (a, b) == (1, 1)
                else recv_m[3 * a + b, MOVES.index((a - 1, b - 1)), 0:64].reshape(1, 64)
                for b in range(3)
            ],
            axis=0,
        )
    for c in first + second + third:
        c.wait_send()


def solution(mesh):
    n_gx, n_gy = mesh.shape["gx"], mesh.shape["gy"]
    vmem = pl.BlockSpec(memory_space=pltpu.VMEM)
    smem = pl.BlockSpec(memory_space=pltpu.SMEM)

    def body(*args):
        def whole(*refs):
            kernel(n_gx, n_gy, *refs)

        atoms = jax.ShapeDtypeStruct(args[0].shape, F32)
        tile = pltpu.VMEM((8, 128), F32)
        tiles = pltpu.VMEM((9, 8, 128), F32)
        return pl.pallas_call(
            whole,
            out_shape=(atoms, atoms, atoms, jax.ShapeDtypeStruct((3, 3, 64), F32)),
            in_specs=[smem if i in (4, 9) else vmem for i in range(len(args))],
            out_specs=(vmem,) * 4,
            scratch_shapes=[
                tile,
                tile,
                tiles,
                tile,
                tile,
                tile,
                tiles,
                tile,
                tiles,
                pltpu.SemaphoreType.DMA((3, 9)),
                pltpu.SemaphoreType.DMA((3, 9)),
            ],
            compiler_params=pltpu.CompilerParams(
                collective_id=0, has_side_effects=True, vmem_limit_bytes=32 * 1024 * 1024
            ),
        )(*args)

    bricks = ("gx", "gy")
    atoms_spec = P(None, bricks)
    in_specs = (
        (atoms_spec,) * 3
        + (P(bricks), P())
        + (P(bricks),) * 5
        + (P(bricks, None),)
        + (P(),) * 9
    )
    return jax.shard_map(
        body,
        mesh=mesh,
        in_specs=in_specs,
        out_specs=(atoms_spec,) * 3 + (P("gx", "gy", None),),
        check_vma=False,
    )
```

```python
import jax
import jax.numpy as jnp
from jax import lax
from jax.experimental import pallas as pl
from jax.experimental.pallas import tpu as pltpu
from jax.sharding import PartitionSpec as P

BOX_SIDE = 2.0
CUTOFF = 2.0
TIME_STEP = 0.05
WIDTHS = tuple((0.1 * 20.0 ** (k / 7.0) for k in range(8)))
Y20 = 0.28867513459481287
MESH = pl.DeviceIdType.MESH
F32 = jnp.float32
BF16 = jnp.bfloat16
VMEM_BYTES = 32 * 1024 * 1024

MOVES = tuple((a, b) for a in (-1, 0, 1) for b in (-1, 0, 1) if (a, b) != (0, 0))
FAR_FIRST = tuple(sorted(MOVES, key=lambda move: -abs(move[0])))


INPUTS = (
    "pos",
    "vel",
    "frc",
    "spec",
    "inv_mass",
    "xface",
    "yface",
    "center",
    "neighbor",
    "count",
    "migrants",
    "emb_c",
    "emb_n",
    "radial",
    "tensor1",
    "mix1",
    "tensor2",
    "mix2",
    "final",
    "eout",
)
FIRST = ("spec", "inv_mass", "frc", "vel", "pos", "xface", "yface")
LOAD_ORDER = FIRST + tuple(name for name in INPUTS if name not in FIRST and name != "count")


def cell(dx, dy):
    return (dx + 1) * 3 + dy + 1


def iota(shape, dim):
    return lax.broadcasted_iota(jnp.int32, shape, dim)


def halves(value):
    high = value.astype(BF16)
    low = (value - high.astype(F32)).astype(BF16)
    return high, low


def halves_f32(value):
    high = value.astype(BF16).astype(F32)
    return high, value - high


def dot(left, right, contract=(1, 0)):
    return lax.dot_general(
        left, right, (((contract[0],), (contract[1],)), ((), ())), preferred_element_type=F32
    )


def lanes_at(tile, index):
    return jnp.take_along_axis(
        tile, jnp.broadcast_to(index, tile.shape), axis=1, mode="promise_in_bounds"
    )


def sigmoid(value):
    return 0.5 + 0.5 * jnp.tanh(0.5 * value)


def row_const(values, shape):
    rows = iota(shape, 0)
    result = jnp.zeros(shape, F32)
    for index, value in enumerate(values):
        result = jnp.where(rows == index, F32(value), result)
    return result


def kernel(n_gx, n_gy, *refs):
    count = len(INPUTS)
    sources, refs = refs[:count], refs[count:]
    (new_pos_ref, new_vel_ref, new_frc_ref, arr_ref), refs = refs[:4], refs[4:]
    local, refs = refs[:count], refs[count:]
    send_x, send_y, recv_a, send_m, recv_m, send_c, recv_c, load_sems, sems_out, sems_in = refs
    loads = {
        name: pltpu.make_async_copy(sources[i], local[i], load_sems.at[i])
        for i, name in enumerate(INPUTS)
        if name != "count"
    }
    refs_of = dict(zip(INPUTS, local))
    count_ref = sources[INPUTS.index("count")]
    for name in LOAD_ORDER:
        loads[name].start()

    def loaded(*wanted):
        for name in wanted:
            loads[name].wait()
        return [refs_of[name] for name in wanted]

    gx = lax.axis_index("gx")
    gy = lax.axis_index("gy")

    def place(dx, dy):
        return (lax.rem(gx + (dx + n_gx), n_gx), lax.rem(gy + (dy + n_gy), n_gy))

    def copy(phase, move, source, target, slot):
        return pltpu.make_async_remote_copy(
            src_ref=source,
            dst_ref=target,
            send_sem=sems_out.at[phase, slot],
            recv_sem=sems_in.at[phase, slot],
            device_id=place(*move),
            device_id_type=MESH,
        )

    barrier = pltpu.get_barrier_semaphore()
    for move in MOVES:
        pl.semaphore_signal(barrier, inc=1, device_id=place(*move), device_id_type=MESH)

    lane = iota((1, 128), 1)
    rows = iota((8, 128), 0)
    low_x = (lane % 64) < 32
    low_y = lane < 64

    spec_ref, inv_mass_ref, frc_ref, vel_ref, pos_ref, xface_ref, yface_ref = loaded(*FIRST)
    species = spec_ref[...].reshape(1, 128)
    inv_mass = jnp.zeros((1, 128), F32)
    for k in range(inv_mass_ref.shape[0]):
        inv_mass = jnp.where(species == k, inv_mass_ref[k], inv_mass)
    halfway = vel_ref[...] + 0.5 * TIME_STEP * frc_ref[...] * inv_mass
    coords = pos_ref[...] + TIME_STEP * halfway
    new_pos_ref[...] = coords
    species_row = species.astype(F32)
    minus = jnp.full((1, 128), -1.0, F32)
    record = jnp.concatenate([coords, species_row, minus, jnp.zeros((3, 128), F32)], axis=0)

    xface = xface_ref[...].reshape(1, 64)
    xface2 = jnp.concatenate([xface, xface], axis=1)
    yface = yface_ref[...].reshape(1, 128)
    y_owned = yface < 128
    lists = jnp.concatenate(
        [
            jnp.zeros((4, 128), F32),
            yface.astype(F32),
            xface2.astype(F32),
            jnp.where(y_owned, yface, -1).astype(F32),
            jnp.zeros((1, 128), F32),
        ],
        axis=0,
    )
    send_x[...] = jnp.where(rows < 5, lanes_at(record, xface2), lists)
    send_y[...] = jnp.where(rows < 4, lanes_at(record, jnp.where(y_owned, yface, 0)), lists)
    pl.semaphore_wait(barrier, len(MOVES))
    first = [
        copy(0, m, send_y if m[0] == 0 else send_x, recv_a.at[cell(*m)], cell(*m)) for m in FAR_FIRST
    ]
    for c in first:
        c.start()

    (migrants_ref,) = loaded("migrants")
    slots = jnp.concatenate([migrants_ref[...]] * 16, axis=1)
    valid = slots >= 0
    at = jnp.where(valid, slots, 0)
    field = lane // 8
    gain = 0.5 * TIME_STEP * inv_mass
    out = jnp.where(field == 7, 1.0, jnp.zeros((8, 128), F32))
    fields = [coords[0:1], coords[1:2], coords[2:3]]
    fields += [halfway[0:1], halfway[1:2], halfway[2:3], species_row, None, gain]
    for number, value in enumerate(fields):
        if value is not None:
            out = jnp.where(field == number, lanes_at(jnp.broadcast_to(value, (8, 128)), at), out)
    dx_col = row_const([BOX_SIDE * m[0] for m in MOVES], (8, 128))
    dy_col = row_const([BOX_SIDE * m[1] for m in MOVES], (8, 128))
    out = out - jnp.where(field == 0, dx_col, jnp.where(field == 1, dy_col, 0.0))
    out = jnp.where(valid, out, 0.0)
    send_m[...] = jnp.where(field == 9, slots.astype(F32), out)
    leave = [copy(1, m, send_m, recv_m.at[cell(*m)], cell(*m)) for m in MOVES]
    for c in leave:
        c.start()

    neighbor_ref, center_ref = loaded("neighbor", "center")
    neighbor = neighbor_ref[...].reshape(1, 256)
    center = center_ref[...].reshape(1, 256)
    live = iota((1, 256), 1) < count_ref[0]
    place_n = jnp.where(
        neighbor < 128,
        neighbor,
        jnp.where(neighbor < 192, ((neighbor - 128) ^ 32) + 128, ((neighbor - 192) ^ 64) + 256),
    )
    hot_n = (iota((384, 256), 0) == place_n).astype(F32)
    hot_c = (iota((128, 256), 0) == center).astype(F32)
    hot_owned = (hot_n[:128] - hot_c).astype(BF16)
    hot_ghosts = hot_n[128:].astype(BF16)
    face_rows = jnp.concatenate([jnp.where(y_owned, yface, -1), xface2], axis=1)
    hot_f = (iota((128, 256), 0) == face_rows).astype(F32).astype(BF16)
    c_live = center.astype(F32)
    rows_e = iota((8, 256), 0)
    left_c = jnp.where(rows_e == 0, jnp.where(live, c_live, -1.0), jnp.where(rows_e == 1, 1.0, 0.0))
    right_c = jnp.where(rows_e == 0, 1.0, jnp.where(rows_e == 1, jnp.where(live, -c_live, 2.0), 0.0))
    same = dot(left_c.astype(BF16), right_c.astype(BF16), (0, 0)) == 0.0
    k0 = same.astype(F32).astype(BF16)

    def merged(tensor_ref, mix_ref):
        tensor = tensor_ref[...]
        width = tensor.shape[1]
        high, low = halves(
            jnp.concatenate(
                [
                    lax.dot_general(
                        tensor,
                        mix_ref[pl.ds(width * deg, width), :],
                        (((1,), (0,)), ((), ())),
                        precision=lax.Precision.HIGHEST,
                        preferred_element_type=F32,
                    )
                    for deg in range(3)
                ],
                axis=1,
            )
        )
        return high, low

    tensor1_ref, mix1_ref, tensor2_ref, mix2_ref = loaded("tensor1", "mix1", "tensor2", "mix2")
    final_ref, radial_ref, emb_c_ref, emb_n_ref = loaded("final", "radial", "emb_c", "emb_n")
    (eout_ref,) = loaded("eout")
    layers = (merged(tensor1_ref, mix1_ref), merged(tensor2_ref, mix2_ref))
    final_h, final_l = halves(final_ref[...])
    pad3 = jnp.zeros((3, 128), F32)
    table = jnp.concatenate([radial_ref[...], emb_c_ref[...], pad3, emb_n_ref[...], pad3], axis=0)
    table_h, table_l = halves_f32(table)
    table_cat = jnp.concatenate(
        [table_h, table_l, table_h[:8], jnp.zeros((8, 128), F32)], axis=0
    ).astype(BF16)
    rad_h, rad_l = table_h[:8], table_l[:8]
    rad_cat = jnp.concatenate([rad_h, rad_l], axis=0).astype(BF16)

    for c in first:
        c.wait_recv()

    def pick4(tiles):
        quarter = lane // 32
        result = tiles[3]
        for q in (2, 1, 0):
            result = jnp.where(quarter == q, tiles[q], result)
        return result

    x_shift = jnp.where(rows == 0, jnp.where(low_x, BOX_SIDE, -BOX_SIDE), 0.0)
    y_shift = jnp.where(rows == 1, jnp.where(low_y, BOX_SIDE, -BOX_SIDE), 0.0)
    ghost_x = jnp.where(low_x, recv_a[cell(-1, 0)], recv_a[cell(1, 0)]) + x_shift
    far_x = (
        pick4(
            [recv_a[cell(-1, -1)], recv_a[cell(1, -1)], recv_a[cell(-1, 1)], recv_a[cell(1, 1)]]
        )
        + x_shift
    )
    ghost_y = jnp.where(low_y, recv_a[cell(0, -1)], recv_a[cell(0, 1)])
    listed = ghost_y[4:5].astype(jnp.int32)
    via_x = listed >= 128
    far_lane = jnp.where(via_x, ((listed - 128) ^ 32) + jnp.where(low_y, 0, 64), 0)
    ghost_y = jnp.where(via_x, lanes_at(far_x, far_lane), ghost_y) + y_shift
    ghost_y = jnp.where(rows == 4, jnp.where(via_x, far_lane.astype(F32), -1.0), ghost_y)

    def edge_side(tiles, index):
        parts = []
        for half in range(2):
            at = index[:, 128 * half : 128 * half + 128]
            result = lanes_at(tiles[0], at & 127)
            for number in range(1, len(tiles)):
                result = jnp.where(
                    at >= 128 * number, lanes_at(tiles[number], at & 127), result
                )
            parts.append(result)
        return jnp.concatenate(parts, axis=1)

    near = edge_side([record, ghost_x, ghost_y], place_n)
    own = edge_side([record], center)
    hot_far = (iota((128, 256), 0) == near[4:5].astype(jnp.int32)).astype(F32).astype(BF16)

    offset = (near - own) * (1.0 / CUTOFF)
    ux, uy, uz = offset[0:1], offset[1:2], offset[2:3]
    squared = ux * ux + uy * uy + uz * uz
    tees = jnp.concatenate(
        [
            ux,
            uy,
            uz,
            ux * uy,
            uy * uz,
            uz * ux,
            0.5 * (ux * ux - uy * uy),
            (2.0 * uz * uz - ux * ux - uy * uy) * Y20,
        ],
        axis=0,
    )
    minus_inv_w = row_const([-1.0 / w for w in WIDTHS], (8, 256))
    radial = jnp.exp(squared * minus_inv_w)
    hot_sc = (rows_e == own[3:4].astype(jnp.int32)).astype(F32)
    hot_sn = (rows_e == near[3:4].astype(jnp.int32)).astype(F32)
    radial_h, radial_l = halves_f32(radial)
    features = jnp.concatenate(
        [radial_h, hot_sc, hot_sn, radial_h, hot_sc, hot_sn, radial_l, jnp.zeros((8, 256), F32)],
        axis=0,
    ).astype(BF16)
    hidden_pre = dot(features, table_cat, (0, 0))

    tees_h, tees_l = halves_f32(tees)
    tees_r = jnp.concatenate([tees_h, tees_l, tees_h, jnp.zeros((8, 256), F32)], axis=0).astype(BF16)

    def degree(mask):
        left = jnp.concatenate([tees_h, tees_h, tees_l, jnp.zeros((8, 256), F32)], axis=0)
        left = jnp.where(mask, left, 0.0).astype(BF16)
        return halves(jnp.where(same, dot(left, tees_r, (0, 0)), 0.0))

    row32 = iota((32, 256), 0) % 8
    k1_h, k1_l = degree(row32 < 3)
    k2_h, k2_l = degree(row32 >= 3)

    k_wide = jnp.concatenate([k0, k1_h, k2_h], axis=1)
    k_wide_l = jnp.concatenate([k1_l, k2_l], axis=1)
    k_tall = jnp.concatenate([k0, k1_h, k2_h], axis=0)
    k_tall_l = jnp.concatenate([k1_l, k2_l], axis=0)

    sig = sigmoid(hidden_pre)
    hidden = hidden_pre * sig
    slope0 = sig * (1.0 + hidden_pre * (1.0 - sig))
    slopes, values = [], []
    for high, low in layers:
        hid_h, hid_l = halves(hidden)
        value = dot(
            jnp.concatenate([hid_h, hid_l, hid_h], axis=1),
            jnp.concatenate([high, high, low], axis=0),
        )
        val_h, val_l = halves(value)
        values.append((val_h, val_l))
        both = dot(
            k_wide,
            jnp.concatenate(
                [
                    jnp.concatenate([val_h[:, 128 * d : 128 * d + 128], val_l[:, 128 * d : 128 * d + 128]], axis=1)
                    for d in range(3)
                ],
                axis=0,
            ),
        )
        rest = dot(k_wide_l, jnp.concatenate([val_h[:, 128:256], val_h[:, 256:384]], axis=0))
        pre = both[:, :128] + both[:, 128:] + rest
        sig = sigmoid(pre)
        hidden = hidden + pre * sig
        slopes.append(sig * (1.0 + pre * (1.0 - sig)))

    hid_h, hid_l = halves(hidden)
    pre = dot(
        jnp.concatenate([hid_h, hid_l, hid_h], axis=1),
        jnp.concatenate([final_h, final_h, final_l], axis=0),
    )
    sig = sigmoid(pre)
    back = eout_ref[...].reshape(1, 128) * (sig * (1.0 + pre * (1.0 - sig)))
    back_h, back_l = halves(back)
    grad = dot(
        jnp.concatenate([back_h, back_l, back_h], axis=1),
        jnp.concatenate([final_h, final_h, final_l], axis=1),
        (1, 1),
    )
    downs = []
    for index in (1, 0):
        high, low = layers[index]
        down_h, down_l = halves(grad * slopes[index])
        downs.append((down_h, down_l))
        both = dot(k_tall, jnp.concatenate([down_h, down_l], axis=1))
        rest = dot(k_tall_l, down_h)
        parts = [both[:256, :128] + both[:256, 128:]]
        for d in (1, 2):
            at = slice(256 * d, 256 * d + 256)
            parts.append(both[at, :128] + both[at, 128:] + rest[256 * d - 256 : 256 * d])
        dv_h, dv_l = halves(jnp.concatenate(parts, axis=1))
        grad = grad + dot(
            jnp.concatenate([dv_h, dv_l, dv_h], axis=1),
            jnp.concatenate([high, high, low], axis=1),
            (1, 1),
        )
    (d2_h, d2_l), (d1_h, d1_l) = downs
    (v1_h, v1_l), (v2_h, v2_l) = values
    outer_left = jnp.concatenate([d1_h, d2_h, d1_l, d2_l, d1_h, d2_h], axis=1)
    moved = []
    for d in (1, 2):
        at = slice(128 * d, 128 * d + 128)
        outer = dot(
            outer_left,
            jnp.concatenate(
                [v1_h[:, at], v2_h[:, at], v1_h[:, at], v2_h[:, at], v1_l[:, at], v2_l[:, at]],
                axis=1,
            ),
            (1, 1),
        )
        out_h, out_l = halves(jnp.where(same, outer, 0.0))
        pair = jnp.concatenate([tees_h, tees_l], axis=0).astype(BF16)
        high_t = tees_h.astype(BF16)
        first_part = dot(pair, out_h) + dot(pair, out_h, (1, 1))
        second_part = dot(high_t, out_l) + dot(high_t, out_l, (1, 1))
        moved.append(first_part[:8] + first_part[8:] + second_part)
    d_tees = jnp.where(rows_e < 3, moved[0], moved[1])

    g_h, g_l = halves(grad * slope0)
    d_radial = dot(rad_cat, g_h, (1, 1))
    d_radial = d_radial[:8] + d_radial[8:] + dot(rad_cat[:8], g_l, (1, 1))
    d_squared = 2.0 * jnp.sum(d_radial * radial * minus_inv_w, axis=0, keepdims=True)
    dxy, dyz, dzx = d_tees[3:4], d_tees[4:5], d_tees[5:6]
    dxx, dzz = d_tees[6:7], (2.0 * Y20) * d_tees[7:8]
    dux = d_tees[0:1] + ux * (d_squared + dxx - dzz) + uy * dxy + uz * dzx
    duy = d_tees[1:2] + uy * (d_squared - dxx - dzz) + ux * dxy + uz * dyz
    duz = d_tees[2:3] + uz * (d_squared + 2.0 * dzz) + uy * dyz + ux * dzx
    d_edge = jnp.concatenate([dux, duy, duz, dux, duy, duz, jnp.zeros((2, 256), F32)], axis=0)
    d_edge = jnp.where(live, d_edge * (1.0 / CUTOFF), 0.0)
    d_edge_h, d_edge_l = halves_f32(d_edge)
    d_pair = jnp.concatenate([d_edge_h, d_edge_l], axis=0).astype(BF16)

    spread = dot(d_pair, jnp.concatenate([hot_owned, hot_ghosts, hot_far], axis=0), (1, 1))
    spread = spread[:8] + spread[8:]
    own_y = jnp.where(rows < 3, spread[:, :128], spread[:, 256:384])
    far_x = jnp.where(rows < 3, spread[:, 384:], spread[:, 128:256])
    send_c[0] = own_y
    send_c[1] = far_x

    def seat(ox, oy):
        return (ox + 2) * n_gy + oy % n_gy

    second = []
    for mx in (-2, 2, -1, 1, 0):
        for my in (2, -1, 1, 0):
            if (mx, my) != (0, 0):
                slot = seat(-mx, -my)
                pair = (send_c, recv_c.at[slot])
                if abs(mx) == 2:
                    pair = (send_c.at[1], recv_c.at[slot, 1])
                second.append(copy(2, (mx, my), *pair, slot))
    for c in second:
        c.start()

    for c in leave:
        c.wait_recv()
    arriving = jnp.zeros((8, 128), F32)
    for c, m in enumerate(MOVES):
        arriving = jnp.where(rows == c, recv_m[cell(*m)], arriving)
    slot_lane = lane % 8
    gains = lanes_at(arriving, 64 + slot_lane)
    listed = lanes_at(arriving, 72 + slot_lane)
    listed_row = jnp.sum(jnp.where(rows == field, listed, 0.0), axis=0, keepdims=True)
    listed_at = jnp.maximum(listed_row, 0.0).astype(jnp.int32)
    spots = iota((64, 128), 0)
    arriving_lists = jnp.where(field == 9, arriving, 0.0).astype(BF16)
    from_source = (iota((64, 8), 0) // 8 == iota((64, 8), 1)).astype(F32).astype(BF16)
    listed_col = jnp.sum(
        jnp.where(
            iota((64, 128), 1) == 72 + spots % 8, dot(from_source, arriving_lists), 0.0
        ),
        axis=1,
        keepdims=True,
    )
    spot_source = iota((64, 256), 0) // 8
    hot_spots = []
    for c, m in enumerate(MOVES):
        tile = recv_a[cell(*m)]
        faces = jnp.concatenate([tile[6:7], tile[5:6]], axis=1)
        hit = jnp.where(spot_source == c, faces, -2.0) == listed_col
        hot_spots.append(hit.astype(F32).astype(BF16))
    hot_spots = jnp.concatenate(hot_spots, axis=1)

    for c in second:
        c.wait_recv()

    def part(ox, oy, tile):
        if (ox, oy) == (0, 0):
            return (own_y, far_x)[tile]
        return recv_c[seat(ox, oy), tile]

    def inward(bx, by):
        from_y = jnp.where(low_y, part(bx, by - 1, 0), part(bx, by + 1, 0))
        from_x = jnp.where(low_x, part(bx - 1, by, 1), part(bx + 1, by, 1))
        from_far = pick4(
            [part(bx + sx, by + sy, 1) for sx, sy in ((-1, -1), (1, -1), (-1, 1), (1, 1))]
        )
        both = jnp.concatenate(
            [jnp.where(rows < 3, 0.0, from_y), jnp.where(rows < 3, from_far, from_x)], axis=1
        )
        return jnp.concatenate(halves_f32(both), axis=0).astype(BF16)

    def force_of(owned, back):
        back = back[:8] + back[8:]
        return -(owned[:3] + back[:3] + back[3:6])

    force = force_of(own_y, dot(inward(0, 0), hot_f, (1, 1)))
    new_frc_ref[...] = force
    new_vel_ref[...] = halfway + gain * force

    owned = jnp.zeros((8, 128), F32)
    for c, m in enumerate(MOVES):
        owned = jnp.where(field == c, lanes_at(part(-m[0], -m[1], 0), listed_at), owned)
    back = dot(
        jnp.concatenate([inward(-m[0], -m[1]) for m in MOVES], axis=1), hot_spots, (1, 1)
    )
    back = jnp.concatenate([back, jnp.zeros((16, 64), F32)], axis=1)
    arriving_force = force_of(owned, back)
    push = jnp.zeros((8, 128), F32)
    for axis in range(3):
        value = jnp.broadcast_to(arriving_force[axis : axis + 1], (8, 128))
        push = jnp.where(field == 3 + axis, lanes_at(value, rows * 8 + slot_lane), push)
    result = arriving + gains * push
    for a in range(3):
        arr_ref[a] = jnp.concatenate(
            [
                jnp.zeros((1, 64), F32)
                if (a, b) == (1, 1)
                else result[MOVES.index((a - 1, b - 1)), 0:64].reshape(1, 64)
                for b in range(3)
            ],
            axis=0,
        )
    for c in first + leave + second:
        c.wait_send()


def store(*refs):
    copies = [pltpu.make_async_copy(refs[i], refs[4 + i], refs[8].at[i]) for i in range(4)]
    for c in copies:
        c.start()
    for c in copies:
        c.wait()


def solution(mesh):
    n_gx, n_gy = mesh.shape["gx"], mesh.shape["gy"]
    vmem = pl.BlockSpec(memory_space=pltpu.VMEM)
    smem = pl.BlockSpec(memory_space=pltpu.SMEM)
    hbm = pl.BlockSpec(memory_space=pltpu.HBM)

    def hold(name, arg):
        return arg if name == "count" else pltpu.with_memory_space_constraint(arg, pltpu.HBM)

    def body(*args):
        def whole(*refs):
            kernel(n_gx, n_gy, *refs)

        atoms = jax.ShapeDtypeStruct(args[0].shape, F32)
        outs = (atoms, atoms, atoms, jax.ShapeDtypeStruct((3, 3, 64), F32))
        tile = pltpu.VMEM((8, 128), F32)
        tiles = pltpu.VMEM((9, 8, 128), F32)
        scalars = ("inv_mass", "count")
        results = pl.pallas_call(
            whole,
            out_shape=outs,
            in_specs=[smem if name == "count" else hbm for name in INPUTS],
            out_specs=(vmem,) * 4,
            scratch_shapes=[
                (pltpu.SMEM if name in scalars else pltpu.VMEM)(arg.shape, arg.dtype)
                for name, arg in zip(INPUTS, args)
            ]
            + [tile, tile, tiles, tile, tiles]
            + [
                pltpu.VMEM((2, 8, 128), F32),
                pltpu.VMEM((5 * n_gy, 2, 8, 128), F32),
                pltpu.SemaphoreType.DMA((len(args),)),
                pltpu.SemaphoreType.DMA((3, 5 * n_gy)),
                pltpu.SemaphoreType.DMA((3, 5 * n_gy)),
            ],
            compiler_params=pltpu.CompilerParams(
                collective_id=0, has_side_effects=True, vmem_limit_bytes=VMEM_BYTES
            ),
        )(*(hold(name, arg) for name, arg in zip(INPUTS, args)))
        return pl.pallas_call(
            store,
            out_shape=outs,
            in_specs=[vmem] * 4,
            out_specs=(hbm,) * 4,
            scratch_shapes=[pltpu.SemaphoreType.DMA((4,))],
            compiler_params=pltpu.CompilerParams(vmem_limit_bytes=VMEM_BYTES),
        )(*results)

    bricks = ("gx", "gy")
    atoms_spec = P(None, bricks)
    in_specs = (
        (atoms_spec,) * 3
        + (P(bricks), P())
        + (P(bricks),) * 5
        + (P(bricks, None),)
        + (P(),) * 9
    )
    return jax.shard_map(
        body,
        mesh=mesh,
        in_specs=in_specs,
        out_specs=(atoms_spec,) * 3 + (P("gx", "gy", None),),
        check_vma=False,
    )
```

```python
import jax
import jax.numpy as jnp
from jax import lax
from jax.experimental import pallas as pl
from jax.experimental.pallas import tpu as pltpu
from jax.sharding import PartitionSpec as P

BOX_SIDE = 2.0
CUTOFF = 2.0
TIME_STEP = 0.05
WIDTHS = tuple((0.1 * 20.0 ** (k / 7.0) for k in range(8)))
Y20 = 0.28867513459481287
MESH = pl.DeviceIdType.MESH
F32 = jnp.float32
BF16 = jnp.bfloat16
VMEM_BYTES = 32 * 1024 * 1024

MOVES = tuple((a, b) for a in (-1, 0, 1) for b in (-1, 0, 1) if (a, b) != (0, 0))
ROW = 32
RELAY = 3
FAR_FIRST = tuple(sorted(MOVES, key=lambda move: -abs(move[0])))


INPUTS = (
    "pos",
    "vel",
    "frc",
    "spec",
    "inv_mass",
    "xface",
    "yface",
    "center",
    "neighbor",
    "count",
    "migrants",
    "emb_c",
    "emb_n",
    "radial",
    "tensor1",
    "mix1",
    "tensor2",
    "mix2",
    "final",
    "eout",
)
FIRST = ("spec", "inv_mass", "frc", "vel", "pos", "xface", "yface")
LOAD_ORDER = FIRST + tuple(name for name in INPUTS if name not in FIRST and name != "count")


def cell(dx, dy):
    return (dx + 1) * 3 + dy + 1


def iota(shape, dim):
    return lax.broadcasted_iota(jnp.int32, shape, dim)


def halves(value):
    high = value.astype(BF16)
    low = (value - high.astype(F32)).astype(BF16)
    return high, low


def halves_f32(value):
    high = value.astype(BF16).astype(F32)
    return high, value - high


def dot(left, right, contract=(1, 0)):
    return lax.dot_general(
        left, right, (((contract[0],), (contract[1],)), ((), ())), preferred_element_type=F32
    )


def lanes_at(tile, index):
    return jnp.take_along_axis(
        tile, jnp.broadcast_to(index, tile.shape), axis=1, mode="promise_in_bounds"
    )


def sigmoid(value):
    return 0.5 + 0.5 * jnp.tanh(0.5 * value)


def row_const(values, shape):
    rows = iota(shape, 0)
    result = jnp.zeros(shape, F32)
    for index, value in enumerate(values):
        result = jnp.where(rows == index, F32(value), result)
    return result


def kernel(n_gx, n_gy, *refs):
    count = len(INPUTS)
    sources, refs = refs[:count], refs[count:]
    (new_pos_ref, new_vel_ref, new_frc_ref, arr_ref), refs = refs[:4], refs[4:]
    local, refs = refs[:count], refs[count:]
    send_x, send_y, recv_a, send_m, recv_m, send_c, recv_c, load_sems, sems_out, sems_in = refs[:10]
    relay_sem, known_sem = refs[10:]
    gx = lax.axis_index("gx")
    gy = lax.axis_index("gy")
    row = lax.rem(gx, ROW)

    def place(dx, dy):
        return (lax.rem(gx + (dx + n_gx), n_gx), lax.rem(gy + (dy + n_gy), n_gy))

    def signal(semaphore, target):
        pl.semaphore_signal(semaphore, inc=1, device_id=target, device_id_type=MESH)

    barrier = pltpu.get_barrier_semaphore()

    @pl.when(row == RELAY)
    def _():
        signal(barrier, place(ROW - 1 - RELAY, 0))
        for dy in (-1, 0, 1):
            signal(barrier, place(ROW - RELAY, dy))

    @pl.when(row < ROW - 1)
    def _():
        for dy in (-1, 0, 1):
            signal(barrier, place(1, dy))

    for move in FAR_FIRST:
        if move[0] != 1:
            signal(barrier, place(*move))

    loads = {
        name: pltpu.make_async_copy(sources[i], local[i], load_sems.at[i])
        for i, name in enumerate(INPUTS)
        if name != "count"
    }
    refs_of = dict(zip(INPUTS, local))
    count_ref = sources[INPUTS.index("count")]
    for name in LOAD_ORDER:
        loads[name].start()

    def loaded(*wanted):
        for name in wanted:
            loads[name].wait()
        return [refs_of[name] for name in wanted]

    def copy(phase, source, target, out_slot, in_slot, device):
        return pltpu.make_async_remote_copy(
            src_ref=source,
            dst_ref=target,
            send_sem=sems_out.at[phase, out_slot],
            recv_sem=sems_in.at[phase, in_slot],
            device_id=device,
            device_id_type=MESH,
        )

    lane = iota((1, 128), 1)
    rows = iota((8, 128), 0)
    low_x = (lane % 64) < 32
    low_y = lane < 64

    spec_ref, inv_mass_ref, frc_ref, vel_ref, pos_ref, xface_ref, yface_ref = loaded(*FIRST)
    species = spec_ref[...].reshape(1, 128)
    inv_mass = jnp.zeros((1, 128), F32)
    for k in range(inv_mass_ref.shape[0]):
        inv_mass = jnp.where(species == k, inv_mass_ref[k], inv_mass)
    halfway = vel_ref[...] + 0.5 * TIME_STEP * frc_ref[...] * inv_mass
    coords = pos_ref[...] + TIME_STEP * halfway
    new_pos_ref[...] = coords
    species_row = species.astype(F32)
    minus = jnp.full((1, 128), -1.0, F32)
    record = jnp.concatenate([coords, species_row, minus, jnp.zeros((3, 128), F32)], axis=0)

    xface = xface_ref[...].reshape(1, 64)
    xface2 = jnp.concatenate([xface, xface], axis=1)
    yface = yface_ref[...].reshape(1, 128)
    y_owned = yface < 128
    lists = jnp.concatenate(
        [
            jnp.zeros((4, 128), F32),
            yface.astype(F32),
            xface2.astype(F32),
            jnp.where(y_owned, yface, -1).astype(F32),
            jnp.zeros((1, 128), F32),
        ],
        axis=0,
    )
    send_x[...] = jnp.where(rows < 5, lanes_at(record, xface2), lists)
    send_y[...] = jnp.where(rows < 4, lanes_at(record, jnp.where(y_owned, yface, 0)), lists)
    pl.semaphore_wait(barrier, len(MOVES) + row // (ROW - 1))

    @pl.when(row == ROW - 1)
    def _():
        signal(relay_sem, place(RELAY + 1 - ROW, 0))

    at_start = 1 - (row + (ROW - 1)) // ROW
    first, first_in = [], []
    for m in FAR_FIRST:
        source, slot = send_y if m[0] == 0 else send_x, cell(*m)
        first_in.append(copy(0, source, recv_a.at[slot], slot, slot, place(*m)))
        if m[0] == -1:
            there = slot + at_start * (10 + m[1] - slot)
            target = place(-1 - at_start * (ROW - 1 - RELAY), m[1])
            first.append(copy(0, source, recv_a.at[there], slot, there, target))
        else:
            first.append(first_in[-1])
    for c in first:
        c.start()

    relays, relays_in = [], []
    for dy in (-1, 0, 1):
        here, there = 10 + dy, cell(-1, dy)
        last = place(ROW - 1 - RELAY, 0)
        relays_in.append(copy(0, send_x, recv_a.at[here], here, here, last))
        relays.append(copy(0, recv_a.at[here], recv_a.at[there], here, there, last))

    (migrants_ref,) = loaded("migrants")
    slots = jnp.concatenate([migrants_ref[...]] * 16, axis=1)
    valid = slots >= 0
    at = jnp.where(valid, slots, 0)
    field = lane // 8
    gain = 0.5 * TIME_STEP * inv_mass
    out = jnp.where(field == 7, 1.0, jnp.zeros((8, 128), F32))
    fields = [coords[0:1], coords[1:2], coords[2:3]]
    fields += [halfway[0:1], halfway[1:2], halfway[2:3], species_row, None, gain]
    for number, value in enumerate(fields):
        if value is not None:
            out = jnp.where(field == number, lanes_at(jnp.broadcast_to(value, (8, 128)), at), out)
    dx_col = row_const([BOX_SIDE * m[0] for m in MOVES], (8, 128))
    dy_col = row_const([BOX_SIDE * m[1] for m in MOVES], (8, 128))
    out = out - jnp.where(field == 0, dx_col, jnp.where(field == 1, dy_col, 0.0))
    out = jnp.where(valid, out, 0.0)
    send_m[...] = jnp.where(field == 9, slots.astype(F32), out)
    leave = [copy(1, send_m, recv_m.at[cell(*m)], cell(*m), cell(*m), place(*m)) for m in MOVES]
    for m, c in zip(MOVES, leave):
        if m[0] == -1:
            pl.when(row > 0)(c.start)
        else:
            c.start()

    neighbor_ref, center_ref = loaded("neighbor", "center")
    neighbor = neighbor_ref[...].reshape(1, 256)
    center = center_ref[...].reshape(1, 256)
    live = iota((1, 256), 1) < count_ref[0]
    place_n = jnp.where(
        neighbor < 128,
        neighbor,
        jnp.where(neighbor < 192, ((neighbor - 128) ^ 32) + 128, ((neighbor - 192) ^ 64) + 256),
    )
    hot_n = (iota((384, 256), 0) == place_n).astype(F32)
    hot_c = (iota((128, 256), 0) == center).astype(F32)
    hot_owned = (hot_n[:128] - hot_c).astype(BF16)
    hot_ghosts = hot_n[128:].astype(BF16)
    face_rows = jnp.concatenate([jnp.where(y_owned, yface, -1), xface2], axis=1)
    hot_f = (iota((128, 256), 0) == face_rows).astype(F32).astype(BF16)
    c_live = center.astype(F32)
    rows_e = iota((8, 256), 0)
    left_c = jnp.where(rows_e == 0, jnp.where(live, c_live, -1.0), jnp.where(rows_e == 1, 1.0, 0.0))
    right_c = jnp.where(rows_e == 0, 1.0, jnp.where(rows_e == 1, jnp.where(live, -c_live, 2.0), 0.0))
    same = dot(left_c.astype(BF16), right_c.astype(BF16), (0, 0)) == 0.0
    k0 = same.astype(F32).astype(BF16)

    def merged(tensor_ref, mix_ref):
        tensor = tensor_ref[...]
        width = tensor.shape[1]
        high, low = halves(
            jnp.concatenate(
                [
                    lax.dot_general(
                        tensor,
                        mix_ref[pl.ds(width * deg, width), :],
                        (((1,), (0,)), ((), ())),
                        precision=lax.Precision.HIGHEST,
                        preferred_element_type=F32,
                    )
                    for deg in range(3)
                ],
                axis=1,
            )
        )
        return high, low

    tensor1_ref, mix1_ref, tensor2_ref, mix2_ref = loaded("tensor1", "mix1", "tensor2", "mix2")
    final_ref, radial_ref, emb_c_ref, emb_n_ref = loaded("final", "radial", "emb_c", "emb_n")
    (eout_ref,) = loaded("eout")
    layers = (merged(tensor1_ref, mix1_ref), merged(tensor2_ref, mix2_ref))
    final_h, final_l = halves(final_ref[...])
    pad3 = jnp.zeros((3, 128), F32)
    table = jnp.concatenate([radial_ref[...], emb_c_ref[...], pad3, emb_n_ref[...], pad3], axis=0)
    table_h, table_l = halves_f32(table)
    table_cat = jnp.concatenate(
        [table_h, table_l, table_h[:8], jnp.zeros((8, 128), F32)], axis=0
    ).astype(BF16)
    rad_h, rad_l = table_h[:8], table_l[:8]
    rad_cat = jnp.concatenate([rad_h, rad_l], axis=0).astype(BF16)

    @pl.when(row == RELAY)
    def _():
        for c in relays_in:
            c.wait_recv()
        pl.semaphore_wait(relay_sem, 1)
        for c in relays:
            c.start()

    for c in first_in:
        c.wait_recv()

    @pl.when(row == 0)
    def _():
        signal(known_sem, place(1, 0))
        signal(known_sem, place(1, 1))
        for m, c in zip(MOVES, leave):
            if m[0] == -1:
                c.start()

    def pick4(tiles):
        quarter = lane // 32
        result = tiles[3]
        for q in (2, 1, 0):
            result = jnp.where(quarter == q, tiles[q], result)
        return result

    x_shift = jnp.where(rows == 0, jnp.where(low_x, BOX_SIDE, -BOX_SIDE), 0.0)
    y_shift = jnp.where(rows == 1, jnp.where(low_y, BOX_SIDE, -BOX_SIDE), 0.0)
    ghost_x = jnp.where(low_x, recv_a[cell(-1, 0)], recv_a[cell(1, 0)]) + x_shift
    far_x = (
        pick4(
            [recv_a[cell(-1, -1)], recv_a[cell(1, -1)], recv_a[cell(-1, 1)], recv_a[cell(1, 1)]]
        )
        + x_shift
    )
    ghost_y = jnp.where(low_y, recv_a[cell(0, -1)], recv_a[cell(0, 1)])
    listed = ghost_y[4:5].astype(jnp.int32)
    via_x = listed >= 128
    far_lane = jnp.where(via_x, ((listed - 128) ^ 32) + jnp.where(low_y, 0, 64), 0)
    ghost_y = jnp.where(via_x, lanes_at(far_x, far_lane), ghost_y) + y_shift
    ghost_y = jnp.where(rows == 4, jnp.where(via_x, far_lane.astype(F32), -1.0), ghost_y)

    def edge_side(tiles, index):
        parts = []
        for half in range(2):
            at = index[:, 128 * half : 128 * half + 128]
            result = lanes_at(tiles[0], at & 127)
            for number in range(1, len(tiles)):
                result = jnp.where(
                    at >= 128 * number, lanes_at(tiles[number], at & 127), result
                )
            parts.append(result)
        return jnp.concatenate(parts, axis=1)

    near = edge_side([record, ghost_x, ghost_y], place_n)
    own = edge_side([record], center)
    hot_far = (iota((128, 256), 0) == near[4:5].astype(jnp.int32)).astype(F32).astype(BF16)

    offset = (near - own) * (1.0 / CUTOFF)
    ux, uy, uz = offset[0:1], offset[1:2], offset[2:3]
    squared = ux * ux + uy * uy + uz * uz
    tees = jnp.concatenate(
        [
            ux,
            uy,
            uz,
            ux * uy,
            uy * uz,
            uz * ux,
            0.5 * (ux * ux - uy * uy),
            (2.0 * uz * uz - ux * ux - uy * uy) * Y20,
        ],
        axis=0,
    )
    minus_inv_w = row_const([-1.0 / w for w in WIDTHS], (8, 256))
    radial = jnp.exp(squared * minus_inv_w)
    hot_sc = (rows_e == own[3:4].astype(jnp.int32)).astype(F32)
    hot_sn = (rows_e == near[3:4].astype(jnp.int32)).astype(F32)
    radial_h, radial_l = halves_f32(radial)
    features = jnp.concatenate(
        [radial_h, hot_sc, hot_sn, radial_h, hot_sc, hot_sn, radial_l, jnp.zeros((8, 256), F32)],
        axis=0,
    ).astype(BF16)
    hidden_pre = dot(features, table_cat, (0, 0))

    tees_h, tees_l = halves_f32(tees)
    tees_r = jnp.concatenate([tees_h, tees_l, tees_h, jnp.zeros((8, 256), F32)], axis=0).astype(BF16)

    def degree(mask):
        left = jnp.concatenate([tees_h, tees_h, tees_l, jnp.zeros((8, 256), F32)], axis=0)
        left = jnp.where(mask, left, 0.0).astype(BF16)
        return halves(jnp.where(same, dot(left, tees_r, (0, 0)), 0.0))

    row32 = iota((32, 256), 0) % 8
    k1_h, k1_l = degree(row32 < 3)
    k2_h, k2_l = degree(row32 >= 3)

    k_wide = jnp.concatenate([k0, k1_h, k2_h], axis=1)
    k_wide_l = jnp.concatenate([k1_l, k2_l], axis=1)
    k_tall = jnp.concatenate([k0, k1_h, k2_h], axis=0)
    k_tall_l = jnp.concatenate([k1_l, k2_l], axis=0)

    sig = sigmoid(hidden_pre)
    hidden = hidden_pre * sig
    slope0 = sig * (1.0 + hidden_pre * (1.0 - sig))
    slopes, values = [], []
    for high, low in layers:
        hid_h, hid_l = halves(hidden)
        value = dot(
            jnp.concatenate([hid_h, hid_l, hid_h], axis=1),
            jnp.concatenate([high, high, low], axis=0),
        )
        val_h, val_l = halves(value)
        values.append((val_h, val_l))
        both = dot(
            k_wide,
            jnp.concatenate(
                [
                    jnp.concatenate([val_h[:, 128 * d : 128 * d + 128], val_l[:, 128 * d : 128 * d + 128]], axis=1)
                    for d in range(3)
                ],
                axis=0,
            ),
        )
        rest = dot(k_wide_l, jnp.concatenate([val_h[:, 128:256], val_h[:, 256:384]], axis=0))
        pre = both[:, :128] + both[:, 128:] + rest
        sig = sigmoid(pre)
        hidden = hidden + pre * sig
        slopes.append(sig * (1.0 + pre * (1.0 - sig)))

    hid_h, hid_l = halves(hidden)
    pre = dot(
        jnp.concatenate([hid_h, hid_l, hid_h], axis=1),
        jnp.concatenate([final_h, final_h, final_l], axis=0),
    )
    sig = sigmoid(pre)
    back = eout_ref[...].reshape(1, 128) * (sig * (1.0 + pre * (1.0 - sig)))
    back_h, back_l = halves(back)
    grad = dot(
        jnp.concatenate([back_h, back_l, back_h], axis=1),
        jnp.concatenate([final_h, final_h, final_l], axis=1),
        (1, 1),
    )
    downs = []
    for index in (1, 0):
        high, low = layers[index]
        down_h, down_l = halves(grad * slopes[index])
        downs.append((down_h, down_l))
        both = dot(k_tall, jnp.concatenate([down_h, down_l], axis=1))
        rest = dot(k_tall_l, down_h)
        parts = [both[:256, :128] + both[:256, 128:]]
        for d in (1, 2):
            at = slice(256 * d, 256 * d + 256)
            parts.append(both[at, :128] + both[at, 128:] + rest[256 * d - 256 : 256 * d])
        dv_h, dv_l = halves(jnp.concatenate(parts, axis=1))
        grad = grad + dot(
            jnp.concatenate([dv_h, dv_l, dv_h], axis=1),
            jnp.concatenate([high, high, low], axis=1),
            (1, 1),
        )
    (d2_h, d2_l), (d1_h, d1_l) = downs
    (v1_h, v1_l), (v2_h, v2_l) = values
    outer_left = jnp.concatenate([d1_h, d2_h, d1_l, d2_l, d1_h, d2_h], axis=1)
    moved = []
    for d in (1, 2):
        at = slice(128 * d, 128 * d + 128)
        outer = dot(
            outer_left,
            jnp.concatenate(
                [v1_h[:, at], v2_h[:, at], v1_h[:, at], v2_h[:, at], v1_l[:, at], v2_l[:, at]],
                axis=1,
            ),
            (1, 1),
        )
        out_h, out_l = halves(jnp.where(same, outer, 0.0))
        pair = jnp.concatenate([tees_h, tees_l], axis=0).astype(BF16)
        high_t = tees_h.astype(BF16)
        first_part = dot(pair, out_h) + dot(pair, out_h, (1, 1))
        second_part = dot(high_t, out_l) + dot(high_t, out_l, (1, 1))
        moved.append(first_part[:8] + first_part[8:] + second_part)
    d_tees = jnp.where(rows_e < 3, moved[0], moved[1])

    g_h, g_l = halves(grad * slope0)
    d_radial = dot(rad_cat, g_h, (1, 1))
    d_radial = d_radial[:8] + d_radial[8:] + dot(rad_cat[:8], g_l, (1, 1))
    d_squared = 2.0 * jnp.sum(d_radial * radial * minus_inv_w, axis=0, keepdims=True)
    dxy, dyz, dzx = d_tees[3:4], d_tees[4:5], d_tees[5:6]
    dxx, dzz = d_tees[6:7], (2.0 * Y20) * d_tees[7:8]
    dux = d_tees[0:1] + ux * (d_squared + dxx - dzz) + uy * dxy + uz * dzx
    duy = d_tees[1:2] + uy * (d_squared - dxx - dzz) + ux * dxy + uz * dyz
    duz = d_tees[2:3] + uz * (d_squared + 2.0 * dzz) + uy * dyz + ux * dzx
    d_edge = jnp.concatenate([dux, duy, duz, dux, duy, duz, jnp.zeros((2, 256), F32)], axis=0)
    d_edge = jnp.where(live, d_edge * (1.0 / CUTOFF), 0.0)
    d_edge_h, d_edge_l = halves_f32(d_edge)
    d_pair = jnp.concatenate([d_edge_h, d_edge_l], axis=0).astype(BF16)

    spread = dot(d_pair, jnp.concatenate([hot_owned, hot_ghosts, hot_far], axis=0), (1, 1))
    spread = spread[:8] + spread[8:]
    own_y = jnp.where(rows < 3, spread[:, :128], spread[:, 256:384])
    far_x = jnp.where(rows < 3, spread[:, 384:], spread[:, 128:256])
    send_c[0] = own_y
    send_c[1] = far_x

    def seat(ox, oy):
        return (ox + 2) * n_gy + oy % n_gy

    second = []
    for mx in (-2, 2, -1, 1, 0):
        for my in (2, -1, 1, 0):
            if (mx, my) != (0, 0):
                slot = seat(-mx, -my)
                pair = (send_c, recv_c.at[slot])
                if abs(mx) == 2:
                    pair = (send_c.at[1], recv_c.at[slot, 1])
                c = copy(2, *pair, slot, slot, place(mx, my))
                second.append(c)
                if mx == -2:
                    pl.when(row != 1)(c.start)
                else:
                    c.start()

    @pl.when(row == 1)
    def _():
        pl.semaphore_wait(known_sem, 2)
        for c in second[:n_gy]:
            c.start()

    for c in leave:
        c.wait_recv()
    arriving = jnp.zeros((8, 128), F32)
    for c, m in enumerate(MOVES):
        arriving = jnp.where(rows == c, recv_m[cell(*m)], arriving)
    slot_lane = lane % 8
    gains = lanes_at(arriving, 64 + slot_lane)
    listed = lanes_at(arriving, 72 + slot_lane)
    listed_row = jnp.sum(jnp.where(rows == field, listed, 0.0), axis=0, keepdims=True)
    listed_at = jnp.maximum(listed_row, 0.0).astype(jnp.int32)
    spots = iota((64, 128), 0)
    arriving_lists = jnp.where(field == 9, arriving, 0.0).astype(BF16)
    from_source = (iota((64, 8), 0) // 8 == iota((64, 8), 1)).astype(F32).astype(BF16)
    listed_col = jnp.sum(
        jnp.where(
            iota((64, 128), 1) == 72 + spots % 8, dot(from_source, arriving_lists), 0.0
        ),
        axis=1,
        keepdims=True,
    )
    spot_source = iota((64, 256), 0) // 8
    hot_spots = []
    for c, m in enumerate(MOVES):
        tile = recv_a[cell(*m)]
        faces = jnp.concatenate([tile[6:7], tile[5:6]], axis=1)
        hit = jnp.where(spot_source == c, faces, -2.0) == listed_col
        hot_spots.append(hit.astype(F32).astype(BF16))
    hot_spots = jnp.concatenate(hot_spots, axis=1)

    for c in second:
        c.wait_recv()

    def part(ox, oy, tile):
        if (ox, oy) == (0, 0):
            return (own_y, far_x)[tile]
        return recv_c[seat(ox, oy), tile]

    def inward(bx, by):
        from_y = jnp.where(low_y, part(bx, by - 1, 0), part(bx, by + 1, 0))
        from_x = jnp.where(low_x, part(bx - 1, by, 1), part(bx + 1, by, 1))
        from_far = pick4(
            [part(bx + sx, by + sy, 1) for sx, sy in ((-1, -1), (1, -1), (-1, 1), (1, 1))]
        )
        both = jnp.concatenate(
            [jnp.where(rows < 3, 0.0, from_y), jnp.where(rows < 3, from_far, from_x)], axis=1
        )
        return jnp.concatenate(halves_f32(both), axis=0).astype(BF16)

    def force_of(owned, back):
        back = back[:8] + back[8:]
        return -(owned[:3] + back[:3] + back[3:6])

    force = force_of(own_y, dot(inward(0, 0), hot_f, (1, 1)))
    new_frc_ref[...] = force
    new_vel_ref[...] = halfway + gain * force

    owned = jnp.zeros((8, 128), F32)
    for c, m in enumerate(MOVES):
        owned = jnp.where(field == c, lanes_at(part(-m[0], -m[1], 0), listed_at), owned)
    back = dot(
        jnp.concatenate([inward(-m[0], -m[1]) for m in MOVES], axis=1), hot_spots, (1, 1)
    )
    back = jnp.concatenate([back, jnp.zeros((16, 64), F32)], axis=1)
    arriving_force = force_of(owned, back)
    push = jnp.zeros((8, 128), F32)
    for axis in range(3):
        value = jnp.broadcast_to(arriving_force[axis : axis + 1], (8, 128))
        push = jnp.where(field == 3 + axis, lanes_at(value, rows * 8 + slot_lane), push)
    result = arriving + gains * push
    for a in range(3):
        arr_ref[a] = jnp.concatenate(
            [
                jnp.zeros((1, 64), F32)
                if (a, b) == (1, 1)
                else result[MOVES.index((a - 1, b - 1)), 0:64].reshape(1, 64)
                for b in range(3)
            ],
            axis=0,
        )
    for c in first + leave + second:
        c.wait_send()

    @pl.when(row == RELAY)
    def _():
        for c in relays:
            c.wait_send()


def store(*refs):
    copies = [pltpu.make_async_copy(refs[i], refs[4 + i], refs[8].at[i]) for i in range(4)]
    for c in copies:
        c.start()
    for c in copies:
        c.wait()


def solution(mesh):
    n_gx, n_gy = mesh.shape["gx"], mesh.shape["gy"]
    vmem = pl.BlockSpec(memory_space=pltpu.VMEM)
    smem = pl.BlockSpec(memory_space=pltpu.SMEM)
    hbm = pl.BlockSpec(memory_space=pltpu.HBM)

    def hold(name, arg):
        return arg if name == "count" else pltpu.with_memory_space_constraint(arg, pltpu.HBM)

    def body(*args):
        def whole(*refs):
            kernel(n_gx, n_gy, *refs)

        atoms = jax.ShapeDtypeStruct(args[0].shape, F32)
        outs = (atoms, atoms, atoms, jax.ShapeDtypeStruct((3, 3, 64), F32))
        tile = pltpu.VMEM((8, 128), F32)
        tiles = pltpu.VMEM((9, 8, 128), F32)
        scalars = ("inv_mass", "count")
        results = pl.pallas_call(
            whole,
            out_shape=outs,
            in_specs=[smem if name == "count" else hbm for name in INPUTS],
            out_specs=(vmem,) * 4,
            scratch_shapes=[
                (pltpu.SMEM if name in scalars else pltpu.VMEM)(arg.shape, arg.dtype)
                for name, arg in zip(INPUTS, args)
            ]
            + [tile, tile, pltpu.VMEM((12, 8, 128), F32), tile, tiles]
            + [
                pltpu.VMEM((2, 8, 128), F32),
                pltpu.VMEM((5 * n_gy, 2, 8, 128), F32),
                pltpu.SemaphoreType.DMA((len(args),)),
                pltpu.SemaphoreType.DMA((3, 5 * n_gy)),
                pltpu.SemaphoreType.DMA((3, 5 * n_gy)),
                pltpu.SemaphoreType.REGULAR,
                pltpu.SemaphoreType.REGULAR,
            ],
            compiler_params=pltpu.CompilerParams(
                collective_id=0, has_side_effects=True, vmem_limit_bytes=VMEM_BYTES
            ),
        )(*(hold(name, arg) for name, arg in zip(INPUTS, args)))
        return pl.pallas_call(
            store,
            out_shape=outs,
            in_specs=[vmem] * 4,
            out_specs=(hbm,) * 4,
            scratch_shapes=[pltpu.SemaphoreType.DMA((4,))],
            compiler_params=pltpu.CompilerParams(vmem_limit_bytes=VMEM_BYTES),
        )(*results)

    bricks = ("gx", "gy")
    atoms_spec = P(None, bricks)
    in_specs = (
        (atoms_spec,) * 3
        + (P(bricks), P())
        + (P(bricks),) * 5
        + (P(bricks, None),)
        + (P(),) * 9
    )
    return jax.shard_map(
        body,
        mesh=mesh,
        in_specs=in_specs,
        out_specs=(atoms_spec,) * 3 + (P("gx", "gy", None),),
        check_vma=False,
    )
```

```python
import jax
import jax.numpy as jnp
from jax import lax
from jax.experimental import pallas as pl
from jax.experimental.pallas import tpu as pltpu
from jax.sharding import PartitionSpec as P

BOX_SIDE = 2.0
CUTOFF = 2.0
TIME_STEP = 0.05
WIDTHS = tuple((0.1 * 20.0 ** (k / 7.0) for k in range(8)))
Y20 = 0.28867513459481287
MESH = pl.DeviceIdType.MESH
F32 = jnp.float32
BF16 = jnp.bfloat16
VMEM_BYTES = 32 * 1024 * 1024

MOVES = tuple((a, b) for a in (-1, 0, 1) for b in (-1, 0, 1) if (a, b) != (0, 0))
ROW = 32
RELAY = 3
FAR_FIRST = tuple(sorted(MOVES, key=lambda move: -abs(move[0])))


INPUTS = (
    "pos",
    "vel",
    "frc",
    "spec",
    "inv_mass",
    "xface",
    "yface",
    "center",
    "neighbor",
    "count",
    "migrants",
    "emb_c",
    "emb_n",
    "radial",
    "tensor1",
    "mix1",
    "tensor2",
    "mix2",
    "final",
    "eout",
)
FIRST = ("spec", "inv_mass", "frc", "vel", "pos", "xface", "yface")
LOAD_ORDER = FIRST + tuple(name for name in INPUTS if name not in FIRST and name != "count")


def cell(dx, dy):
    return (dx + 1) * 3 + dy + 1


def iota(shape, dim):
    return lax.broadcasted_iota(jnp.int32, shape, dim)


def halves(value):
    high = value.astype(BF16)
    low = (value - high.astype(F32)).astype(BF16)
    return high, low


def halves_f32(value):
    high = value.astype(BF16).astype(F32)
    return high, value - high


def doubled(high, low):
    return (
        jnp.concatenate([jnp.concatenate([high, low], axis=1)] * 2, axis=0),
        jnp.concatenate([jnp.concatenate([high] * 2, axis=1), jnp.concatenate([low] * 2, axis=1)], axis=0),
    )


def dot(left, right, contract=(1, 0)):
    return lax.dot_general(
        left, right, (((contract[0],), (contract[1],)), ((), ())), preferred_element_type=F32
    )


def lanes_at(tile, index):
    return jnp.take_along_axis(
        tile, jnp.broadcast_to(index, tile.shape), axis=1, mode="promise_in_bounds"
    )


def sigmoid(value):
    return 0.5 + 0.5 * jnp.tanh(0.5 * value)


def row_const(values, shape):
    rows = iota(shape, 0)
    result = jnp.zeros(shape, F32)
    for index, value in enumerate(values):
        result = jnp.where(rows == index, F32(value), result)
    return result


def kernel(n_gx, n_gy, *refs):
    count = len(INPUTS)
    sources, refs = refs[:count], refs[count:]
    (new_pos_ref, new_vel_ref, new_frc_ref, arr_ref), refs = refs[:4], refs[4:]
    local, refs = refs[:count], refs[count:]
    send_x, send_y, recv_a, send_m, recv_m, send_c, recv_c, load_sems, sems_out, sems_in = refs[:10]
    relay_sem, known_sem = refs[10:]
    gx = lax.axis_index("gx")
    gy = lax.axis_index("gy")
    row = lax.rem(gx, ROW)

    def place(dx, dy):
        return (lax.rem(gx + (dx + n_gx), n_gx), lax.rem(gy + (dy + n_gy), n_gy))

    def signal(semaphore, target):
        pl.semaphore_signal(semaphore, inc=1, device_id=target, device_id_type=MESH)

    barrier = pltpu.get_barrier_semaphore()

    @pl.when(row == RELAY)
    def _():
        signal(barrier, place(ROW - 1 - RELAY, 0))
        for dy in (-1, 0, 1):
            signal(barrier, place(ROW - RELAY, dy))

    @pl.when(row < ROW - 1)
    def _():
        for dy in (-1, 0, 1):
            signal(barrier, place(1, dy))

    for move in FAR_FIRST:
        if move[0] != 1:
            signal(barrier, place(*move))

    loads = {
        name: pltpu.make_async_copy(sources[i], local[i], load_sems.at[i])
        for i, name in enumerate(INPUTS)
        if name != "count"
    }
    refs_of = dict(zip(INPUTS, local))
    count_ref = sources[INPUTS.index("count")]
    for name in LOAD_ORDER:
        loads[name].start()

    def loaded(*wanted):
        for name in wanted:
            loads[name].wait()
        return [refs_of[name] for name in wanted]

    def copy(phase, source, target, device, arrive=None):
        return pltpu.make_async_remote_copy(
            src_ref=source,
            dst_ref=target,
            send_sem=sems_out.at[phase],
            recv_sem=sems_in.at[phase if arrive is None else arrive],
            device_id=device,
            device_id_type=MESH,
        )

    def all_of(phase, ref, tiles):
        whole = ref.at[pl.ds(0, tiles)]
        return copy(phase, whole, whole, place(1, 0))

    lane = iota((1, 128), 1)
    rows = iota((8, 128), 0)
    low_x = (lane % 64) < 32
    low_y = lane < 64

    spec_ref, inv_mass_ref, frc_ref, vel_ref, pos_ref, xface_ref, yface_ref = loaded(*FIRST)
    species = spec_ref[...].reshape(1, 128)
    inv_mass = jnp.zeros((1, 128), F32)
    for k in range(inv_mass_ref.shape[0]):
        inv_mass = jnp.where(species == k, inv_mass_ref[k], inv_mass)
    halfway = vel_ref[...] + 0.5 * TIME_STEP * frc_ref[...] * inv_mass
    coords = pos_ref[...] + TIME_STEP * halfway
    new_pos_ref[...] = coords
    species_row = species.astype(F32)
    minus = jnp.full((1, 128), -1.0, F32)
    record = jnp.concatenate([coords, species_row, minus, jnp.zeros((3, 128), F32)], axis=0)

    xface = xface_ref[...].reshape(1, 64)
    xface2 = jnp.concatenate([xface, xface], axis=1)
    yface = yface_ref[...].reshape(1, 128)
    y_owned = yface < 128
    lists = jnp.concatenate(
        [
            jnp.zeros((4, 128), F32),
            yface.astype(F32),
            xface2.astype(F32),
            jnp.where(y_owned, yface, -1).astype(F32),
            jnp.zeros((1, 128), F32),
        ],
        axis=0,
    )
    send_x[...] = jnp.where(rows < 5, lanes_at(record, xface2), lists)
    send_y[...] = jnp.where(rows < 4, lanes_at(record, jnp.where(y_owned, yface, 0)), lists)
    pl.semaphore_wait(barrier, len(MOVES) + row // (ROW - 1))

    @pl.when(row == ROW - 1)
    def _():
        signal(relay_sem, place(RELAY + 1 - ROW, 0))

    at_start = 1 - (row + (ROW - 1)) // ROW
    last = place(ROW - 1 - RELAY, 0)
    for m in FAR_FIRST:
        source, slot = send_y if m[0] == 0 else send_x, cell(*m)
        if m[0] == -1:
            there = slot + at_start * (10 + m[1] - slot)
            target = place(-1 - at_start * (ROW - 1 - RELAY), m[1])
            copy(0, source, recv_a.at[there], target, 3 * at_start).start()
        else:
            copy(0, source, recv_a.at[slot], place(*m)).start()

    (migrants_ref,) = loaded("migrants")
    slots = jnp.concatenate([migrants_ref[...]] * 16, axis=1)
    valid = slots >= 0
    at = jnp.where(valid, slots, 0)
    field = lane // 8
    gain = 0.5 * TIME_STEP * inv_mass
    out = jnp.where(field == 7, 1.0, jnp.zeros((8, 128), F32))
    fields = [coords[0:1], coords[1:2], coords[2:3]]
    fields += [halfway[0:1], halfway[1:2], halfway[2:3], species_row, None, gain]
    for number, value in enumerate(fields):
        if value is not None:
            out = jnp.where(field == number, lanes_at(jnp.broadcast_to(value, (8, 128)), at), out)
    dx_col = row_const([BOX_SIDE * m[0] for m in MOVES], (8, 128))
    dy_col = row_const([BOX_SIDE * m[1] for m in MOVES], (8, 128))
    out = out - jnp.where(field == 0, dx_col, jnp.where(field == 1, dy_col, 0.0))
    out = jnp.where(valid, out, 0.0)
    send_m[...] = jnp.where(field == 9, slots.astype(F32), out)
    leave = [copy(1, send_m, recv_m.at[cell(*m)], place(*m)) for m in MOVES]
    for m, c in zip(MOVES, leave):
        if m[0] == -1:
            pl.when(row > 0)(c.start)
        else:
            c.start()

    neighbor_ref, center_ref = loaded("neighbor", "center")
    neighbor = neighbor_ref[...].reshape(1, 256)
    center = center_ref[...].reshape(1, 256)
    live = iota((1, 256), 1) < count_ref[0]
    place_n = jnp.where(
        neighbor < 128,
        neighbor,
        jnp.where(neighbor < 192, ((neighbor - 128) ^ 32) + 128, ((neighbor - 192) ^ 64) + 256),
    )
    hot_n = (iota((384, 256), 0) == place_n).astype(F32)
    hot_c = (iota((128, 256), 0) == center).astype(F32)
    hot_owned = (hot_n[:128] - hot_c).astype(BF16)
    hot_ghosts = hot_n[128:].astype(BF16)
    face_rows = jnp.concatenate([jnp.where(y_owned, yface, -1), xface2], axis=1)
    hot_f = (iota((128, 256), 0) == face_rows).astype(F32).astype(BF16)
    c_live = center.astype(F32)
    rows_e = iota((8, 256), 0)
    left_c = jnp.where(rows_e == 0, jnp.where(live, c_live, -1.0), jnp.where(rows_e == 1, 1.0, 0.0))
    right_c = jnp.where(rows_e == 0, 1.0, jnp.where(rows_e == 1, jnp.where(live, -c_live, 2.0), 0.0))
    same = dot(left_c.astype(BF16), right_c.astype(BF16), (0, 0)) == 0.0
    k0 = same.astype(F32).astype(BF16)

    def merged(tensor_ref, mix_ref):
        tensor = tensor_ref[...]
        width = tensor.shape[1]
        high, low = halves(
            jnp.concatenate(
                [
                    lax.dot_general(
                        tensor,
                        mix_ref[pl.ds(width * deg, width), :],
                        (((1,), (0,)), ((), ())),
                        precision=lax.Precision.HIGHEST,
                        preferred_element_type=F32,
                    )
                    for deg in range(3)
                ],
                axis=1,
            )
        )
        return doubled(high, low)

    tensor1_ref, mix1_ref, tensor2_ref, mix2_ref = loaded("tensor1", "mix1", "tensor2", "mix2")
    final_ref, radial_ref, emb_c_ref, emb_n_ref = loaded("final", "radial", "emb_c", "emb_n")
    (eout_ref,) = loaded("eout")
    layers = (merged(tensor1_ref, mix1_ref), merged(tensor2_ref, mix2_ref))
    final_forward, final_backward = doubled(*halves(final_ref[...]))
    pad3 = jnp.zeros((3, 128), F32)
    table = jnp.concatenate([radial_ref[...], emb_c_ref[...], pad3, emb_n_ref[...], pad3], axis=0)
    table_h, table_l = halves_f32(table)
    table_cat = jnp.concatenate(
        [table_h, table_l, table_h[:8], jnp.zeros((8, 128), F32)], axis=0
    ).astype(BF16)
    rad_h, rad_l = table_h[:8], table_l[:8]
    rad_cat = jnp.concatenate([rad_h, rad_l], axis=0).astype(BF16)

    @pl.when(row == RELAY)
    def _():
        all_of(3, recv_a, 3).wait_recv()
        pl.semaphore_wait(relay_sem, 1)
        for dy in (-1, 0, 1):
            copy(3, recv_a.at[10 + dy], recv_a.at[cell(-1, dy)], last, 0).start()

    all_of(0, recv_a, 8).wait_recv()

    @pl.when(row == 0)
    def _():
        signal(known_sem, place(1, 0))
        signal(known_sem, place(1, 1))
        for m, c in zip(MOVES, leave):
            if m[0] == -1:
                c.start()

    def pick4(tiles):
        quarter = lane // 32
        result = tiles[3]
        for q in (2, 1, 0):
            result = jnp.where(quarter == q, tiles[q], result)
        return result

    x_shift = jnp.where(rows == 0, jnp.where(low_x, BOX_SIDE, -BOX_SIDE), 0.0)
    y_shift = jnp.where(rows == 1, jnp.where(low_y, BOX_SIDE, -BOX_SIDE), 0.0)
    ghost_x = jnp.where(low_x, recv_a[cell(-1, 0)], recv_a[cell(1, 0)]) + x_shift
    far_x = (
        pick4(
            [recv_a[cell(-1, -1)], recv_a[cell(1, -1)], recv_a[cell(-1, 1)], recv_a[cell(1, 1)]]
        )
        + x_shift
    )
    ghost_y = jnp.where(low_y, recv_a[cell(0, -1)], recv_a[cell(0, 1)])
    listed = ghost_y[4:5].astype(jnp.int32)
    via_x = listed >= 128
    far_lane = jnp.where(via_x, ((listed - 128) ^ 32) + jnp.where(low_y, 0, 64), 0)
    ghost_y = jnp.where(via_x, lanes_at(far_x, far_lane), ghost_y) + y_shift
    ghost_y = jnp.where(rows == 4, jnp.where(via_x, far_lane.astype(F32), -1.0), ghost_y)

    def edge_side(tiles, index):
        parts = []
        for half in range(2):
            at = index[:, 128 * half : 128 * half + 128]
            result = lanes_at(tiles[0], at & 127)
            for number in range(1, len(tiles)):
                result = jnp.where(
                    at >= 128 * number, lanes_at(tiles[number], at & 127), result
                )
            parts.append(result)
        return jnp.concatenate(parts, axis=1)

    near = edge_side([record, ghost_x, ghost_y], place_n)
    own = edge_side([record], center)
    hot_far = (iota((128, 256), 0) == near[4:5].astype(jnp.int32)).astype(F32).astype(BF16)

    offset = (near - own) * (1.0 / CUTOFF)
    ux, uy, uz = offset[0:1], offset[1:2], offset[2:3]
    squared = ux * ux + uy * uy + uz * uz
    tees = jnp.concatenate(
        [
            ux,
            uy,
            uz,
            ux * uy,
            uy * uz,
            uz * ux,
            0.5 * (ux * ux - uy * uy),
            (2.0 * uz * uz - ux * ux - uy * uy) * Y20,
        ],
        axis=0,
    )
    minus_inv_w = row_const([-1.0 / w for w in WIDTHS], (8, 256))
    radial = jnp.exp(squared * minus_inv_w)
    hot_sc = (rows_e == own[3:4].astype(jnp.int32)).astype(F32)
    hot_sn = (rows_e == near[3:4].astype(jnp.int32)).astype(F32)
    radial_h, radial_l = halves_f32(radial)
    features = jnp.concatenate(
        [radial_h, hot_sc, hot_sn, radial_h, hot_sc, hot_sn, radial_l, jnp.zeros((8, 256), F32)],
        axis=0,
    ).astype(BF16)
    hidden_pre = dot(features, table_cat, (0, 0))

    tees_h, tees_l = halves_f32(tees)
    tees_r = jnp.concatenate([tees_h, tees_l, tees_h, jnp.zeros((8, 256), F32)], axis=0).astype(BF16)

    def degree(mask):
        left = jnp.concatenate([tees_h, tees_h, tees_l, jnp.zeros((8, 256), F32)], axis=0)
        left = jnp.where(mask, left, 0.0).astype(BF16)
        return halves(jnp.where(same, dot(left, tees_r, (0, 0)), 0.0))

    row32 = iota((32, 256), 0) % 8
    k1_h, k1_l = degree(row32 < 3)
    k2_h, k2_l = degree(row32 >= 3)

    k_wide = jnp.concatenate([k0, k1_h, k2_h], axis=1)
    k_wide_l = jnp.concatenate([k1_l, k2_l], axis=1)
    k_tall = jnp.concatenate([k0, k1_h, k2_h], axis=0)
    k_tall_l = jnp.concatenate([k1_l, k2_l], axis=0)

    sig = sigmoid(hidden_pre)
    hidden = hidden_pre * sig
    slope0 = sig * (1.0 + hidden_pre * (1.0 - sig))
    slopes, values = [], []
    for forward, _ in layers:
        hid_h, hid_l = halves(hidden)
        pair = dot(jnp.concatenate([hid_h, hid_l], axis=1), forward)
        value = pair[:, :384] + pair[:, 384:]
        val_h, val_l = halves(value)
        values.append((val_h, val_l))
        both = dot(
            k_wide,
            jnp.concatenate(
                [
                    jnp.concatenate([val_h[:, 128 * d : 128 * d + 128], val_l[:, 128 * d : 128 * d + 128]], axis=1)
                    for d in range(3)
                ],
                axis=0,
            ),
        )
        rest = dot(k_wide_l, jnp.concatenate([val_h[:, 128:256], val_h[:, 256:384]], axis=0))
        pre = both[:, :128] + both[:, 128:] + rest
        sig = sigmoid(pre)
        hidden = hidden + pre * sig
        slopes.append(sig * (1.0 + pre * (1.0 - sig)))

    hid_h, hid_l = halves(hidden)
    pre = dot(jnp.concatenate([hid_h, hid_l], axis=1), final_forward)
    pre = pre[:, :128] + pre[:, 128:]
    sig = sigmoid(pre)
    back = eout_ref[...].reshape(1, 128) * (sig * (1.0 + pre * (1.0 - sig)))
    back_h, back_l = halves(back)
    grad = dot(jnp.concatenate([back_h, back_l], axis=1), final_backward, (1, 1))
    grad = grad[:, :128] + grad[:, 128:]
    downs = []
    for index in (1, 0):
        _, backward = layers[index]
        down_h, down_l = halves(grad * slopes[index])
        downs.append((down_h, down_l))
        both = dot(k_tall, jnp.concatenate([down_h, down_l], axis=1))
        rest = dot(k_tall_l, down_h)
        parts = [both[:256, :128] + both[:256, 128:]]
        for d in (1, 2):
            at = slice(256 * d, 256 * d + 256)
            parts.append(both[at, :128] + both[at, 128:] + rest[256 * d - 256 : 256 * d])
        dv_h, dv_l = halves(jnp.concatenate(parts, axis=1))
        both = dot(jnp.concatenate([dv_h, dv_l], axis=1), backward, (1, 1))
        grad = grad + (both[:, :128] + both[:, 128:])
    (d2_h, d2_l), (d1_h, d1_l) = downs
    (v1_h, v1_l), (v2_h, v2_l) = values
    outer_left = jnp.concatenate([d1_h, d2_h, d1_l, d2_l, d1_h, d2_h], axis=1)
    moved = []
    for d in (1, 2):
        at = slice(128 * d, 128 * d + 128)
        outer = dot(
            outer_left,
            jnp.concatenate(
                [v1_h[:, at], v2_h[:, at], v1_h[:, at], v2_h[:, at], v1_l[:, at], v2_l[:, at]],
                axis=1,
            ),
            (1, 1),
        )
        out_h, out_l = halves(jnp.where(same, outer, 0.0))
        pair = jnp.concatenate([tees_h, tees_l], axis=0).astype(BF16)
        high_t = tees_h.astype(BF16)
        first_part = dot(pair, out_h) + dot(pair, out_h, (1, 1))
        second_part = dot(high_t, out_l) + dot(high_t, out_l, (1, 1))
        moved.append(first_part[:8] + first_part[8:] + second_part)
    d_tees = jnp.where(rows_e < 3, moved[0], moved[1])

    g_h, g_l = halves(grad * slope0)
    d_radial = dot(rad_cat, g_h, (1, 1))
    d_radial = d_radial[:8] + d_radial[8:] + dot(rad_cat[:8], g_l, (1, 1))
    d_squared = 2.0 * jnp.sum(d_radial * radial * minus_inv_w, axis=0, keepdims=True)
    dxy, dyz, dzx = d_tees[3:4], d_tees[4:5], d_tees[5:6]
    dxx, dzz = d_tees[6:7], (2.0 * Y20) * d_tees[7:8]
    dux = d_tees[0:1] + ux * (d_squared + dxx - dzz) + uy * dxy + uz * dzx
    duy = d_tees[1:2] + uy * (d_squared - dxx - dzz) + ux * dxy + uz * dyz
    duz = d_tees[2:3] + uz * (d_squared + 2.0 * dzz) + uy * dyz + ux * dzx
    d_edge = jnp.concatenate([dux, duy, duz, dux, duy, duz, jnp.zeros((2, 256), F32)], axis=0)
    d_edge = jnp.where(live, d_edge * (1.0 / CUTOFF), 0.0)
    d_edge_h, d_edge_l = halves_f32(d_edge)
    d_pair = jnp.concatenate([d_edge_h, d_edge_l], axis=0).astype(BF16)

    spread = dot(d_pair, jnp.concatenate([hot_owned, hot_ghosts, hot_far], axis=0), (1, 1))
    spread = spread[:8] + spread[8:]
    own_y = jnp.where(rows < 3, spread[:, :128], spread[:, 256:384])
    far_x = jnp.where(rows < 3, spread[:, 384:], spread[:, 128:256])
    send_c[0] = own_y
    send_c[1] = far_x

    def seat(ox, oy):
        return (ox + 2) * n_gy + oy % n_gy

    second = []
    for mx in (2, 1, -2, -1, 0):
        for my in (2, -1, 1, 0):
            if (mx, my) != (0, 0):
                slot = seat(-mx, -my)
                pair = (send_c, recv_c.at[slot])
                if abs(mx) == 2:
                    pair = (send_c.at[1], recv_c.at[slot, 1])
                c = copy(2, *pair, place(mx, my))
                second.append(c)
                if mx == -2:
                    pl.when(row != 1)(c.start)
                else:
                    c.start()

    @pl.when(row == 1)
    def _():
        pl.semaphore_wait(known_sem, 2)
        for c in second[2 * n_gy : 3 * n_gy]:
            c.start()

    all_of(1, recv_m, 8).wait_recv()
    arriving = jnp.zeros((8, 128), F32)
    for c, m in enumerate(MOVES):
        arriving = jnp.where(rows == c, recv_m[cell(*m)], arriving)
    slot_lane = lane % 8
    gains = lanes_at(arriving, 64 + slot_lane)
    listed = lanes_at(arriving, 72 + slot_lane)
    listed_row = jnp.sum(jnp.where(rows == field, listed, 0.0), axis=0, keepdims=True)
    listed_at = jnp.maximum(listed_row, 0.0).astype(jnp.int32)
    spots = iota((64, 128), 0)
    arriving_lists = jnp.where(field == 9, arriving, 0.0).astype(BF16)
    from_source = (iota((64, 8), 0) // 8 == iota((64, 8), 1)).astype(F32).astype(BF16)
    listed_col = jnp.sum(
        jnp.where(
            iota((64, 128), 1) == 72 + spots % 8, dot(from_source, arriving_lists), 0.0
        ),
        axis=1,
        keepdims=True,
    )
    spot_source = iota((64, 256), 0) // 8
    hot_spots = []
    for c, m in enumerate(MOVES):
        tile = recv_a[cell(*m)]
        faces = jnp.concatenate([tile[6:7], tile[5:6]], axis=1)
        hit = jnp.where(spot_source == c, faces, -2.0) == listed_col
        hot_spots.append(hit.astype(F32).astype(BF16))
    hot_spots = jnp.concatenate(hot_spots, axis=1)

    all_of(2, recv_c, 5 * n_gy - 5).wait_recv()

    def part(ox, oy, tile):
        if (ox, oy) == (0, 0):
            return (own_y, far_x)[tile]
        return recv_c[seat(ox, oy), tile]

    def inward(bx, by):
        from_y = jnp.where(low_y, part(bx, by - 1, 0), part(bx, by + 1, 0))
        from_x = jnp.where(low_x, part(bx - 1, by, 1), part(bx + 1, by, 1))
        from_far = pick4(
            [part(bx + sx, by + sy, 1) for sx, sy in ((-1, -1), (1, -1), (-1, 1), (1, 1))]
        )
        both = jnp.concatenate(
            [jnp.where(rows < 3, 0.0, from_y), jnp.where(rows < 3, from_far, from_x)], axis=1
        )
        return jnp.concatenate(halves_f32(both), axis=0).astype(BF16)

    def force_of(owned, back):
        back = back[:8] + back[8:]
        return -(owned[:3] + back[:3] + back[3:6])

    force = force_of(own_y, dot(inward(0, 0), hot_f, (1, 1)))
    new_frc_ref[...] = force
    new_vel_ref[...] = halfway + gain * force

    owned = jnp.zeros((8, 128), F32)
    for c, m in enumerate(MOVES):
        owned = jnp.where(field == c, lanes_at(part(-m[0], -m[1], 0), listed_at), owned)
    back = dot(
        jnp.concatenate([inward(-m[0], -m[1]) for m in MOVES], axis=1), hot_spots, (1, 1)
    )
    back = jnp.concatenate([back, jnp.zeros((16, 64), F32)], axis=1)
    arriving_force = force_of(owned, back)
    push = jnp.zeros((8, 128), F32)
    for axis in range(3):
        value = jnp.broadcast_to(arriving_force[axis : axis + 1], (8, 128))
        push = jnp.where(field == 3 + axis, lanes_at(value, rows * 8 + slot_lane), push)
    result = arriving + gains * push
    for a in range(3):
        arr_ref[a] = jnp.concatenate(
            [
                jnp.zeros((1, 64), F32)
                if (a, b) == (1, 1)
                else result[MOVES.index((a - 1, b - 1)), 0:64].reshape(1, 64)
                for b in range(3)
            ],
            axis=0,
        )
    all_of(0, recv_a, 8).wait_send()
    all_of(1, recv_m, 8).wait_send()
    all_of(2, recv_c, 5 * n_gy - 5).wait_send()

    @pl.when(row == RELAY)
    def _():
        all_of(3, recv_a, 3).wait_send()


def store(*refs):
    copies = [pltpu.make_async_copy(refs[i], refs[4 + i], refs[8].at[i]) for i in range(4)]
    for c in copies:
        c.start()
    for c in copies:
        c.wait()


def solution(mesh):
    n_gx, n_gy = mesh.shape["gx"], mesh.shape["gy"]
    vmem = pl.BlockSpec(memory_space=pltpu.VMEM)
    smem = pl.BlockSpec(memory_space=pltpu.SMEM)
    hbm = pl.BlockSpec(memory_space=pltpu.HBM)

    def hold(name, arg):
        return arg if name == "count" else pltpu.with_memory_space_constraint(arg, pltpu.HBM)

    def body(*args):
        def whole(*refs):
            kernel(n_gx, n_gy, *refs)

        atoms = jax.ShapeDtypeStruct(args[0].shape, F32)
        outs = (atoms, atoms, atoms, jax.ShapeDtypeStruct((3, 3, 64), F32))
        tile = pltpu.VMEM((8, 128), F32)
        tiles = pltpu.VMEM((9, 8, 128), F32)
        scalars = ("inv_mass", "count")
        results = pl.pallas_call(
            whole,
            out_shape=outs,
            in_specs=[smem if name == "count" else hbm for name in INPUTS],
            out_specs=(vmem,) * 4,
            scratch_shapes=[
                (pltpu.SMEM if name in scalars else pltpu.VMEM)(arg.shape, arg.dtype)
                for name, arg in zip(INPUTS, args)
            ]
            + [tile, tile, pltpu.VMEM((12, 8, 128), F32), tile, tiles]
            + [
                pltpu.VMEM((2, 8, 128), F32),
                pltpu.VMEM((5 * n_gy, 2, 8, 128), F32),
                pltpu.SemaphoreType.DMA((len(args),)),
                pltpu.SemaphoreType.DMA((4,)),
                pltpu.SemaphoreType.DMA((4,)),
                pltpu.SemaphoreType.REGULAR,
                pltpu.SemaphoreType.REGULAR,
            ],
            compiler_params=pltpu.CompilerParams(
                collective_id=0, has_side_effects=True, vmem_limit_bytes=VMEM_BYTES
            ),
        )(*(hold(name, arg) for name, arg in zip(INPUTS, args)))
        return pl.pallas_call(
            store,
            out_shape=outs,
            in_specs=[vmem] * 4,
            out_specs=(hbm,) * 4,
            scratch_shapes=[pltpu.SemaphoreType.DMA((4,))],
            compiler_params=pltpu.CompilerParams(vmem_limit_bytes=VMEM_BYTES),
        )(*results)

    bricks = ("gx", "gy")
    atoms_spec = P(None, bricks)
    in_specs = (
        (atoms_spec,) * 3
        + (P(bricks), P())
        + (P(bricks),) * 5
        + (P(bricks, None),)
        + (P(),) * 9
    )
    return jax.shard_map(
        body,
        mesh=mesh,
        in_specs=in_specs,
        out_specs=(atoms_spec,) * 3 + (P("gx", "gy", None),),
        check_vma=False,
    )
```

```python
import jax
import jax.numpy as jnp
from jax import lax
from jax.experimental import pallas as pl
from jax.experimental.pallas import tpu as pltpu
from jax.sharding import PartitionSpec as P

BOX_SIDE = 2.0
CUTOFF = 2.0
TIME_STEP = 0.05
WIDTHS = tuple((0.1 * 20.0 ** (k / 7.0) for k in range(8)))
Y20 = 0.28867513459481287
MESH = pl.DeviceIdType.MESH
F32 = jnp.float32
BF16 = jnp.bfloat16
VMEM_BYTES = 32 * 1024 * 1024

MOVES = tuple((a, b) for a in (-1, 0, 1) for b in (-1, 0, 1) if (a, b) != (0, 0))
ROW = 32
RELAY = 3
FAR_FIRST = tuple(sorted(MOVES, key=lambda move: -abs(move[0])))


INPUTS = (
    "pos",
    "vel",
    "frc",
    "spec",
    "inv_mass",
    "xface",
    "yface",
    "center",
    "neighbor",
    "count",
    "migrants",
    "emb_c",
    "emb_n",
    "radial",
    "tensor1",
    "mix1",
    "tensor2",
    "mix2",
    "final",
    "eout",
)
FIRST = ("spec", "inv_mass", "frc", "vel", "pos", "xface", "yface")
LOAD_ORDER = FIRST + tuple(name for name in INPUTS if name not in FIRST and name != "count")


def cell(dx, dy):
    return (dx + 1) * 3 + dy + 1


def iota(shape, dim):
    return lax.broadcasted_iota(jnp.int32, shape, dim)


def halves(value):
    high = value.astype(BF16)
    low = (value - high.astype(F32)).astype(BF16)
    return high, low


def halves_f32(value):
    high = value.astype(BF16).astype(F32)
    return high, value - high


def doubled(high, low):
    return (
        jnp.concatenate([jnp.concatenate([high, low], axis=1)] * 2, axis=0),
        jnp.concatenate([jnp.concatenate([high] * 2, axis=1), jnp.concatenate([low] * 2, axis=1)], axis=0),
    )


def dot(left, right, contract=(1, 0)):
    return lax.dot_general(
        left, right, (((contract[0],), (contract[1],)), ((), ())), preferred_element_type=F32
    )


def lanes_at(tile, index):
    return jnp.take_along_axis(
        tile, jnp.broadcast_to(index, tile.shape), axis=1, mode="promise_in_bounds"
    )


def sigmoid(value):
    return 0.5 + 0.5 * jnp.tanh(0.5 * value)


def row_const(values, shape):
    rows = iota(shape, 0)
    result = jnp.zeros(shape, F32)
    for index, value in enumerate(values):
        result = jnp.where(rows == index, F32(value), result)
    return result


def kernel(n_gx, n_gy, *refs):
    count = len(INPUTS)
    sources, refs = refs[:count], refs[count:]
    (new_pos_ref, new_vel_ref, new_frc_ref, arr_ref), refs = refs[:4], refs[4:]
    local, refs = refs[:count], refs[count:]
    send_x, send_y, recv_a, send_m, recv_m, send_c, recv_c, load_sems, sems_out, sems_in = refs[:10]
    relay_sem, known_sem = refs[10:]
    gx = lax.axis_index("gx")
    gy = lax.axis_index("gy")
    row = lax.rem(gx, ROW)

    def place(dx, dy):
        return (lax.rem(gx + (dx + n_gx), n_gx), lax.rem(gy + (dy + n_gy), n_gy))

    def signal(semaphore, target):
        pl.semaphore_signal(semaphore, inc=1, device_id=target, device_id_type=MESH)

    barrier = pltpu.get_barrier_semaphore()

    @pl.when(row == RELAY)
    def _():
        signal(barrier, place(ROW - 1 - RELAY, 0))
        for dy in (-1, 0, 1):
            signal(barrier, place(ROW - RELAY, dy))

    @pl.when(row < ROW - 1)
    def _():
        for dy in (-1, 0, 1):
            signal(barrier, place(1, dy))

    for move in FAR_FIRST:
        if move[0] != 1:
            signal(barrier, place(*move))

    loads = {
        name: pltpu.make_async_copy(sources[i], local[i], load_sems.at[i])
        for i, name in enumerate(INPUTS)
        if name != "count"
    }
    refs_of = dict(zip(INPUTS, local))
    count_ref = sources[INPUTS.index("count")]
    for name in LOAD_ORDER:
        loads[name].start()

    def loaded(*wanted):
        for name in wanted:
            loads[name].wait()
        return [refs_of[name] for name in wanted]

    def copy(phase, source, target, device, arrive=None):
        return pltpu.make_async_remote_copy(
            src_ref=source,
            dst_ref=target,
            send_sem=sems_out.at[phase],
            recv_sem=sems_in.at[phase if arrive is None else arrive],
            device_id=device,
            device_id_type=MESH,
        )

    def all_of(phase, ref, tiles):
        whole = ref.at[pl.ds(0, tiles)]
        return copy(phase, whole, whole, place(1, 0))

    lane = iota((1, 128), 1)
    rows = iota((8, 128), 0)
    low_x = (lane % 64) < 32
    low_y = lane < 64

    spec_ref, inv_mass_ref, frc_ref, vel_ref, pos_ref, xface_ref, yface_ref = loaded(*FIRST)
    species = spec_ref[...].reshape(1, 128)
    inv_mass = jnp.zeros((1, 128), F32)
    for k in range(inv_mass_ref.shape[0]):
        inv_mass = jnp.where(species == k, inv_mass_ref[k], inv_mass)
    halfway = vel_ref[...] + 0.5 * TIME_STEP * frc_ref[...] * inv_mass
    coords = pos_ref[...] + TIME_STEP * halfway
    new_pos_ref[...] = coords
    species_row = species.astype(F32)
    minus = jnp.full((1, 128), -1.0, F32)
    record = jnp.concatenate([coords, species_row, minus, jnp.zeros((3, 128), F32)], axis=0)

    xface = xface_ref[...].reshape(1, 64)
    xface2 = jnp.concatenate([xface, xface], axis=1)
    yface = yface_ref[...].reshape(1, 128)
    y_owned = yface < 128
    blank = jnp.full((1, 32), -1, jnp.int32)
    lower = jnp.concatenate([xface[:, :32]] * 3 + [blank], axis=1)
    upper = jnp.concatenate([xface[:, 32:]] * 3 + [blank], axis=1)
    owned_y = jnp.where(y_owned, yface, -1)
    lists = jnp.concatenate(
        [
            jnp.zeros((4, 128), F32),
            yface.astype(F32),
            owned_y.astype(F32),
            lower.astype(F32),
            upper.astype(F32),
        ],
        axis=0,
    )
    send_x[...] = jnp.where(rows < 5, lanes_at(record, xface2), lists)
    send_y[...] = jnp.where(rows < 4, lanes_at(record, jnp.where(y_owned, yface, 0)), lists)
    pl.semaphore_wait(barrier, len(MOVES) + row // (ROW - 1))

    @pl.when(row == ROW - 1)
    def _():
        signal(relay_sem, place(RELAY + 1 - ROW, 0))

    at_start = 1 - (row + (ROW - 1)) // ROW
    last = place(ROW - 1 - RELAY, 0)
    for m in FAR_FIRST:
        source, slot = send_y if m[0] == 0 else send_x, cell(*m)
        if m[0] == -1:
            there = slot + at_start * (10 + m[1] - slot)
            target = place(-1 - at_start * (ROW - 1 - RELAY), m[1])
            copy(0, source, recv_a.at[there], target, 3 * at_start).start()
        else:
            copy(0, source, recv_a.at[slot], place(*m)).start()

    (migrants_ref,) = loaded("migrants")
    slots = jnp.concatenate([migrants_ref[...]] * 16, axis=1)
    valid = slots >= 0
    at = jnp.where(valid, slots, 0)
    field = lane // 8
    gain = 0.5 * TIME_STEP * inv_mass
    out = jnp.where(field == 7, 1.0, jnp.zeros((8, 128), F32))
    fields = [coords[0:1], coords[1:2], coords[2:3]]
    fields += [halfway[0:1], halfway[1:2], halfway[2:3], species_row, None, gain]
    for number, value in enumerate(fields):
        if value is not None:
            out = jnp.where(field == number, lanes_at(jnp.broadcast_to(value, (8, 128)), at), out)
    dx_col = row_const([BOX_SIDE * m[0] for m in MOVES], (8, 128))
    dy_col = row_const([BOX_SIDE * m[1] for m in MOVES], (8, 128))
    out = out - jnp.where(field == 0, dx_col, jnp.where(field == 1, dy_col, 0.0))
    out = jnp.where(valid, out, 0.0)
    send_m[...] = jnp.where(field == 9, slots.astype(F32), out)
    leave = [
        copy(1, send_m.at[pl.ds(c, 1)], recv_m.at[pl.ds(c, 1)], place(*m))
        for c, m in enumerate(MOVES)
    ]
    for m, c in zip(MOVES, leave):
        if m[0] == -1:
            pl.when(row > 0)(c.start)
        else:
            c.start()

    neighbor_ref, center_ref = loaded("neighbor", "center")
    neighbor = neighbor_ref[...].reshape(1, 256)
    center = center_ref[...].reshape(1, 256)
    live = iota((1, 256), 1) < count_ref[0]
    place_n = jnp.where(
        neighbor < 128,
        neighbor,
        jnp.where(neighbor < 192, ((neighbor - 128) ^ 32) + 128, ((neighbor - 192) ^ 64) + 256),
    )
    hot_n = (iota((384, 256), 0) == place_n).astype(F32)
    hot_c = (iota((128, 256), 0) == center).astype(F32)
    hot_owned = (hot_n[:128] - hot_c).astype(BF16)
    hot_y = hot_n[256:].astype(BF16)
    ghost = place_n - 128
    in_x = (ghost >= 0) & (ghost < 64)
    at_x = jnp.where(in_x, jnp.where(ghost < 32, 32, 128) + ghost, -1)
    face_rows = jnp.concatenate([owned_y, lower, upper], axis=1)
    hot_f = (iota((128, 384), 0) == face_rows).astype(F32).astype(BF16)
    c_live = center.astype(F32)
    rows_e = iota((8, 256), 0)
    left_c = jnp.where(rows_e == 0, jnp.where(live, c_live, -1.0), jnp.where(rows_e == 1, 1.0, 0.0))
    right_c = jnp.where(rows_e == 0, 1.0, jnp.where(rows_e == 1, jnp.where(live, -c_live, 2.0), 0.0))
    same = dot(left_c.astype(BF16), right_c.astype(BF16), (0, 0)) == 0.0
    k0 = same.astype(F32).astype(BF16)

    def merged(tensor_ref, mix_ref):
        tensor = tensor_ref[...]
        width = tensor.shape[1]
        high, low = halves(
            jnp.concatenate(
                [
                    lax.dot_general(
                        tensor,
                        mix_ref[pl.ds(width * deg, width), :],
                        (((1,), (0,)), ((), ())),
                        precision=lax.Precision.HIGHEST,
                        preferred_element_type=F32,
                    )
                    for deg in range(3)
                ],
                axis=1,
            )
        )
        return doubled(high, low)

    tensor1_ref, mix1_ref, tensor2_ref, mix2_ref = loaded("tensor1", "mix1", "tensor2", "mix2")
    final_ref, radial_ref, emb_c_ref, emb_n_ref = loaded("final", "radial", "emb_c", "emb_n")
    (eout_ref,) = loaded("eout")
    layers = (merged(tensor1_ref, mix1_ref), merged(tensor2_ref, mix2_ref))
    final_forward, final_backward = doubled(*halves(final_ref[...]))
    pad3 = jnp.zeros((3, 128), F32)
    table = jnp.concatenate([radial_ref[...], emb_c_ref[...], pad3, emb_n_ref[...], pad3], axis=0)
    table_h, table_l = halves_f32(table)
    table_cat = jnp.concatenate(
        [table_h, table_l, table_h[:8], jnp.zeros((8, 128), F32)], axis=0
    ).astype(BF16)
    rad_h, rad_l = table_h[:8], table_l[:8]
    rad_cat = jnp.concatenate([rad_h, rad_l], axis=0).astype(BF16)

    @pl.when(row == RELAY)
    def _():
        all_of(3, recv_a, 3).wait_recv()
        pl.semaphore_wait(relay_sem, 1)
        for dy in (-1, 0, 1):
            copy(3, recv_a.at[10 + dy], recv_a.at[cell(-1, dy)], last, 0).start()

    all_of(0, recv_a, 8).wait_recv()

    @pl.when(row == 0)
    def _():
        signal(known_sem, place(1, 0))
        signal(known_sem, place(1, 1))
        for m, c in zip(MOVES, leave):
            if m[0] == -1:
                c.start()

    def pick4(tiles):
        quarter = lane // 32
        result = tiles[3]
        for q in (2, 1, 0):
            result = jnp.where(quarter == q, tiles[q], result)
        return result

    x_shift = jnp.where(rows == 0, jnp.where(low_x, BOX_SIDE, -BOX_SIDE), 0.0)
    y_shift = jnp.where(rows == 1, jnp.where(low_y, BOX_SIDE, -BOX_SIDE), 0.0)
    ghost_x = jnp.where(low_x, recv_a[cell(-1, 0)], recv_a[cell(1, 0)]) + x_shift
    far_x = (
        pick4(
            [recv_a[cell(-1, -1)], recv_a[cell(1, -1)], recv_a[cell(-1, 1)], recv_a[cell(1, 1)]]
        )
        + x_shift
    )
    ghost_y = jnp.where(low_y, recv_a[cell(0, -1)], recv_a[cell(0, 1)])
    listed = ghost_y[4:5].astype(jnp.int32)
    via_x = listed >= 128
    far_lane = jnp.where(via_x, ((listed - 128) ^ 32) + jnp.where(low_y, 0, 64), 0)
    ghost_y = jnp.where(via_x, lanes_at(far_x, far_lane), ghost_y) + y_shift
    far_at = (far_lane + 96 * ((far_lane // 32) % 2)).astype(F32)
    ghost_y = jnp.where(rows == 4, jnp.where(via_x, far_at, -1.0), ghost_y)

    def edge_side(tiles, index):
        parts = []
        for half in range(2):
            at = index[:, 128 * half : 128 * half + 128]
            result = lanes_at(tiles[0], at & 127)
            for number in range(1, len(tiles)):
                result = jnp.where(
                    at >= 128 * number, lanes_at(tiles[number], at & 127), result
                )
            parts.append(result)
        return jnp.concatenate(parts, axis=1)

    near = edge_side([record, ghost_x, ghost_y], place_n)
    own = edge_side([record], center)
    side = iota((256, 256), 0)
    hot_x = (side == jnp.where(in_x, at_x, near[4:5].astype(jnp.int32))).astype(F32).astype(BF16)

    offset = (near - own) * (1.0 / CUTOFF)
    ux, uy, uz = offset[0:1], offset[1:2], offset[2:3]
    squared = ux * ux + uy * uy + uz * uz
    tees = jnp.concatenate(
        [
            ux,
            uy,
            uz,
            ux * uy,
            uy * uz,
            uz * ux,
            0.5 * (ux * ux - uy * uy),
            (2.0 * uz * uz - ux * ux - uy * uy) * Y20,
        ],
        axis=0,
    )
    minus_inv_w = row_const([-1.0 / w for w in WIDTHS], (8, 256))
    radial = jnp.exp(squared * minus_inv_w)
    hot_sc = (rows_e == own[3:4].astype(jnp.int32)).astype(F32)
    hot_sn = (rows_e == near[3:4].astype(jnp.int32)).astype(F32)
    radial_h, radial_l = halves_f32(radial)
    features = jnp.concatenate(
        [radial_h, hot_sc, hot_sn, radial_h, hot_sc, hot_sn, radial_l, jnp.zeros((8, 256), F32)],
        axis=0,
    ).astype(BF16)
    hidden_pre = dot(features, table_cat, (0, 0))

    tees_h, tees_l = halves_f32(tees)
    tees_r = jnp.concatenate([tees_h, tees_l, tees_h, jnp.zeros((8, 256), F32)], axis=0).astype(BF16)

    def degree(mask):
        left = jnp.concatenate([tees_h, tees_h, tees_l, jnp.zeros((8, 256), F32)], axis=0)
        left = jnp.where(mask, left, 0.0).astype(BF16)
        return halves(jnp.where(same, dot(left, tees_r, (0, 0)), 0.0))

    row32 = iota((32, 256), 0) % 8
    k1_h, k1_l = degree(row32 < 3)
    k2_h, k2_l = degree(row32 >= 3)

    k_wide = jnp.concatenate([k0, k1_h, k2_h], axis=1)
    k_wide_l = jnp.concatenate([k1_l, k2_l], axis=1)
    k_tall = jnp.concatenate([k0, k1_h, k2_h], axis=0)
    k_tall_l = jnp.concatenate([k1_l, k2_l], axis=0)

    sig = sigmoid(hidden_pre)
    hidden = hidden_pre * sig
    slope0 = sig * (1.0 + hidden_pre * (1.0 - sig))
    slopes, values = [], []
    for forward, _ in layers:
        hid_h, hid_l = halves(hidden)
        pair = dot(jnp.concatenate([hid_h, hid_l], axis=1), forward)
        value = pair[:, :384] + pair[:, 384:]
        val_h, val_l = halves(value)
        values.append((val_h, val_l))
        both = dot(
            k_wide,
            jnp.concatenate(
                [
                    jnp.concatenate([val_h[:, 128 * d : 128 * d + 128], val_l[:, 128 * d : 128 * d + 128]], axis=1)
                    for d in range(3)
                ],
                axis=0,
            ),
        )
        rest = dot(k_wide_l, jnp.concatenate([val_h[:, 128:256], val_h[:, 256:384]], axis=0))
        pre = both[:, :128] + both[:, 128:] + rest
        sig = sigmoid(pre)
        hidden = hidden + pre * sig
        slopes.append(sig * (1.0 + pre * (1.0 - sig)))

    hid_h, hid_l = halves(hidden)
    pre = dot(jnp.concatenate([hid_h, hid_l], axis=1), final_forward)
    pre = pre[:, :128] + pre[:, 128:]
    sig = sigmoid(pre)
    back = eout_ref[...].reshape(1, 128) * (sig * (1.0 + pre * (1.0 - sig)))
    back_h, back_l = halves(back)
    grad = dot(jnp.concatenate([back_h, back_l], axis=1), final_backward, (1, 1))
    grad = grad[:, :128] + grad[:, 128:]
    downs = []
    for index in (1, 0):
        _, backward = layers[index]
        down_h, down_l = halves(grad * slopes[index])
        downs.append((down_h, down_l))
        both = dot(k_tall, jnp.concatenate([down_h, down_l], axis=1))
        rest = dot(k_tall_l, down_h)
        parts = [both[:256, :128] + both[:256, 128:]]
        for d in (1, 2):
            at = slice(256 * d, 256 * d + 256)
            parts.append(both[at, :128] + both[at, 128:] + rest[256 * d - 256 : 256 * d])
        dv_h, dv_l = halves(jnp.concatenate(parts, axis=1))
        both = dot(jnp.concatenate([dv_h, dv_l], axis=1), backward, (1, 1))
        grad = grad + (both[:, :128] + both[:, 128:])
    (d2_h, d2_l), (d1_h, d1_l) = downs
    (v1_h, v1_l), (v2_h, v2_l) = values
    outer_left = jnp.concatenate([d1_h, d2_h, d1_l, d2_l, d1_h, d2_h], axis=1)
    moved = []
    for d in (1, 2):
        at = slice(128 * d, 128 * d + 128)
        outer = dot(
            outer_left,
            jnp.concatenate(
                [v1_h[:, at], v2_h[:, at], v1_h[:, at], v2_h[:, at], v1_l[:, at], v2_l[:, at]],
                axis=1,
            ),
            (1, 1),
        )
        out_h, out_l = halves(jnp.where(same, outer, 0.0))
        pair = jnp.concatenate([tees_h, tees_l], axis=0).astype(BF16)
        high_t = tees_h.astype(BF16)
        first_part = dot(pair, out_h) + dot(pair, out_h, (1, 1))
        second_part = dot(high_t, out_l) + dot(high_t, out_l, (1, 1))
        moved.append(first_part[:8] + first_part[8:] + second_part)
    d_tees = jnp.where(rows_e < 3, moved[0], moved[1])

    g_h, g_l = halves(grad * slope0)
    d_radial = dot(rad_cat, g_h, (1, 1))
    d_radial = d_radial[:8] + d_radial[8:] + dot(rad_cat[:8], g_l, (1, 1))
    d_squared = 2.0 * jnp.sum(d_radial * radial * minus_inv_w, axis=0, keepdims=True)
    dxy, dyz, dzx = d_tees[3:4], d_tees[4:5], d_tees[5:6]
    dxx, dzz = d_tees[6:7], (2.0 * Y20) * d_tees[7:8]
    dux = d_tees[0:1] + ux * (d_squared + dxx - dzz) + uy * dxy + uz * dzx
    duy = d_tees[1:2] + uy * (d_squared - dxx - dzz) + ux * dxy + uz * dyz
    duz = d_tees[2:3] + uz * (d_squared + 2.0 * dzz) + uy * dyz + ux * dzx
    d_edge = jnp.concatenate([dux, duy, duz, jnp.zeros((5, 256), F32)], axis=0)
    d_edge = jnp.where(live, d_edge * (1.0 / CUTOFF), 0.0)
    d_edge_h, d_edge_l = halves_f32(d_edge)
    d_pair = jnp.concatenate([d_edge_h, d_edge_l], axis=0).astype(BF16)

    spread = dot(d_pair, jnp.concatenate([hot_owned, hot_y, hot_x], axis=0), (1, 1))
    spread = spread[:4] + spread[8:12]
    mine = (spread[:, 384:], spread[:, :128], spread[:, 128:256], spread[:, 256:384])
    for number, value in enumerate(mine):
        send_c[number] = value

    def seat(ox, oy):
        return (ox + 2) * n_gy + oy % n_gy

    second = []
    for mx in (2, 1, -2, -1, 0):
        for my in (2, -1, 1, 0):
            if (mx, my) != (0, 0):
                slot = seat(-mx, -my)
                used = {-2: (0, 1), -1: (0, 3), 0: (0, 4), 1: (1, 3), 2: (3, 1)}[mx]
                c = copy(2, send_c.at[pl.ds(*used)], recv_c.at[slot, pl.ds(*used)], place(mx, my))
                second.append(c)
                if mx == -2:
                    pl.when(row != 1)(c.start)
                else:
                    c.start()

    @pl.when(row == 1)
    def _():
        pl.semaphore_wait(known_sem, 2)
        for c in second[2 * n_gy : 3 * n_gy]:
            c.start()

    all_of(1, recv_m, 8).wait_recv()
    arriving = recv_m[...]
    slot_lane = lane % 8
    gains = lanes_at(arriving, 64 + slot_lane)
    listed = lanes_at(arriving, 72 + slot_lane)
    listed_row = jnp.sum(jnp.where(rows == field, listed, 0.0), axis=0, keepdims=True)
    listed_at = jnp.maximum(listed_row, 0.0).astype(jnp.int32)
    spots = iota((64, 128), 0)
    arriving_lists = jnp.where(field == 9, arriving, 0.0).astype(BF16)
    from_source = (iota((64, 8), 0) // 8 == iota((64, 8), 1)).astype(F32).astype(BF16)
    listed_col = jnp.sum(
        jnp.where(
            iota((64, 128), 1) == 72 + spots % 8, dot(from_source, arriving_lists), 0.0
        ),
        axis=1,
        keepdims=True,
    )
    spot_source = iota((64, 384), 0) // 8
    hot_spots = []
    for c, m in enumerate(MOVES):
        tile = recv_a[cell(*m)]
        faces = jnp.concatenate([tile[5:6], tile[6:7], tile[7:8]], axis=1)
        hit = jnp.where(spot_source == c, faces, -2.0) == listed_col
        hot_spots.append(hit.astype(F32).astype(BF16))
    hot_spots = jnp.concatenate(hot_spots, axis=1)

    all_of(2, recv_c, 3 * n_gy - 1).wait_recv()

    def part(ox, oy, tile):
        if (ox, oy) == (0, 0):
            return mine[tile]
        return recv_c[seat(ox, oy), tile]

    third = lane // 32

    def inward(bx, by):
        sides = [jnp.where(low_y, part(bx, by - 1, 2), part(bx, by + 1, 2))]
        for ox, tile in ((bx - 1, 3), (bx + 1, 0)):
            above, beside = part(ox, by - 1, tile), part(ox, by, tile)
            below = part(ox, by + 1, tile)
            sides.append(jnp.where(third == 0, above, jnp.where(third == 1, beside, below)))
        high, low = halves_f32(jnp.concatenate(sides, axis=1))
        return jnp.concatenate([high, low, jnp.zeros((8, 384), F32)], axis=0).astype(BF16)

    def force_of(owned, back):
        return -(owned[:3] + back[:3] + back[4:7])

    force = force_of(mine[1], dot(inward(0, 0), hot_f, (1, 1)))
    new_frc_ref[...] = force
    new_vel_ref[...] = halfway + gain * force

    owned = jnp.zeros((8, 128), F32)
    for c, m in enumerate(MOVES):
        tile = jnp.concatenate([part(-m[0], -m[1], 1)] * 2, axis=0)
        owned = jnp.where(field == c, lanes_at(tile, listed_at), owned)
    back = dot(
        jnp.concatenate([inward(-m[0], -m[1]) for m in MOVES], axis=1), hot_spots, (1, 1)
    )
    back = jnp.concatenate([back, jnp.zeros((16, 64), F32)], axis=1)
    arriving_force = force_of(owned, back)
    push = jnp.zeros((8, 128), F32)
    for axis in range(3):
        value = jnp.broadcast_to(arriving_force[axis : axis + 1], (8, 128))
        push = jnp.where(field == 3 + axis, lanes_at(value, rows * 8 + slot_lane), push)
    result = arriving + gains * push
    for a in range(3):
        arr_ref[a] = jnp.concatenate(
            [
                jnp.zeros((1, 64), F32)
                if (a, b) == (1, 1)
                else result[MOVES.index((a - 1, b - 1)), 0:64].reshape(1, 64)
                for b in range(3)
            ],
            axis=0,
        )
    all_of(0, recv_a, 8).wait_send()
    all_of(1, recv_m, 8).wait_send()
    all_of(2, recv_c, 3 * n_gy - 1).wait_send()

    @pl.when(row == RELAY)
    def _():
        all_of(3, recv_a, 3).wait_send()


def store(*refs):
    copies = [pltpu.make_async_copy(refs[i], refs[4 + i], refs[8].at[i]) for i in range(4)]
    for c in copies:
        c.start()
    for c in copies:
        c.wait()


def solution(mesh):
    n_gx, n_gy = mesh.shape["gx"], mesh.shape["gy"]
    vmem = pl.BlockSpec(memory_space=pltpu.VMEM)
    smem = pl.BlockSpec(memory_space=pltpu.SMEM)
    hbm = pl.BlockSpec(memory_space=pltpu.HBM)

    def hold(name, arg):
        return arg if name == "count" else pltpu.with_memory_space_constraint(arg, pltpu.HBM)

    def body(*args):
        def whole(*refs):
            kernel(n_gx, n_gy, *refs)

        atoms = jax.ShapeDtypeStruct(args[0].shape, F32)
        outs = (atoms, atoms, atoms, jax.ShapeDtypeStruct((3, 3, 64), F32))
        tile = pltpu.VMEM((8, 128), F32)
        scalars = ("inv_mass", "count")
        results = pl.pallas_call(
            whole,
            out_shape=outs,
            in_specs=[smem if name == "count" else hbm for name in INPUTS],
            out_specs=(vmem,) * 4,
            scratch_shapes=[
                (pltpu.SMEM if name in scalars else pltpu.VMEM)(arg.shape, arg.dtype)
                for name, arg in zip(INPUTS, args)
            ]
            + [tile, tile, pltpu.VMEM((12, 8, 128), F32), tile, tile]
            + [
                pltpu.VMEM((4, 4, 128), F32),
                pltpu.VMEM((5 * n_gy, 4, 4, 128), F32),
                pltpu.SemaphoreType.DMA((len(args),)),
                pltpu.SemaphoreType.DMA((4,)),
                pltpu.SemaphoreType.DMA((4,)),
                pltpu.SemaphoreType.REGULAR,
                pltpu.SemaphoreType.REGULAR,
            ],
            compiler_params=pltpu.CompilerParams(
                collective_id=0, has_side_effects=True, vmem_limit_bytes=VMEM_BYTES
            ),
        )(*(hold(name, arg) for name, arg in zip(INPUTS, args)))
        return pl.pallas_call(
            store,
            out_shape=outs,
            in_specs=[vmem] * 4,
            out_specs=(hbm,) * 4,
            scratch_shapes=[pltpu.SemaphoreType.DMA((4,))],
            compiler_params=pltpu.CompilerParams(vmem_limit_bytes=VMEM_BYTES),
        )(*results)

    bricks = ("gx", "gy")
    atoms_spec = P(None, bricks)
    in_specs = (
        (atoms_spec,) * 3
        + (P(bricks), P())
        + (P(bricks),) * 5
        + (P(bricks, None),)
        + (P(),) * 9
    )
    return jax.shard_map(
        body,
        mesh=mesh,
        in_specs=in_specs,
        out_specs=(atoms_spec,) * 3 + (P("gx", "gy", None),),
        check_vma=False,
    )
```

```python
import jax
import jax.numpy as jnp
from jax import lax
from jax.experimental import pallas as pl
from jax.experimental.pallas import tpu as pltpu
from jax.sharding import PartitionSpec as P

BOX_SIDE = 2.0
CUTOFF = 2.0
TIME_STEP = 0.05
WIDTHS = tuple((0.1 * 20.0 ** (k / 7.0) for k in range(8)))
Y20 = 0.28867513459481287
MESH = pl.DeviceIdType.MESH
F32 = jnp.float32
BF16 = jnp.bfloat16
VMEM_BYTES = 32 * 1024 * 1024

MOVES = tuple((a, b) for a in (-1, 0, 1) for b in (-1, 0, 1) if (a, b) != (0, 0))
ROW = 32
RELAY = 3
FAR_FIRST = tuple(sorted(MOVES, key=lambda move: -abs(move[0])))


INPUTS = (
    "pos",
    "vel",
    "frc",
    "spec",
    "inv_mass",
    "xface",
    "yface",
    "center",
    "neighbor",
    "count",
    "migrants",
    "emb_c",
    "emb_n",
    "radial",
    "tensor1",
    "mix1",
    "tensor2",
    "mix2",
    "final",
    "eout",
)
FIRST = ("spec", "inv_mass", "frc", "vel", "pos", "xface", "yface")
LOAD_ORDER = FIRST + tuple(name for name in INPUTS if name not in FIRST and name != "count")


def cell(dx, dy):
    return (dx + 1) * 3 + dy + 1


def iota(shape, dim):
    return lax.broadcasted_iota(jnp.int32, shape, dim)


def halves(value):
    high = value.astype(BF16)
    low = (value - high.astype(F32)).astype(BF16)
    return high, low


def halves_f32(value):
    high = value.astype(BF16).astype(F32)
    return high, value - high


def doubled(high, low):
    return (
        jnp.concatenate([jnp.concatenate([high, low], axis=1)] * 2, axis=0),
        jnp.concatenate([jnp.concatenate([high] * 2, axis=1), jnp.concatenate([low] * 2, axis=1)], axis=0),
    )


def dot(left, right, contract=(1, 0)):
    return lax.dot_general(
        left, right, (((contract[0],), (contract[1],)), ((), ())), preferred_element_type=F32
    )


def lanes_at(tile, index):
    return jnp.take_along_axis(
        tile, jnp.broadcast_to(index, tile.shape), axis=1, mode="promise_in_bounds"
    )


def sigmoid(value):
    return 0.5 + 0.5 * jnp.tanh(0.5 * value)


def row_const(values, shape):
    rows = iota(shape, 0)
    result = jnp.zeros(shape, F32)
    for index, value in enumerate(values):
        result = jnp.where(rows == index, F32(value), result)
    return result


def kernel(n_gx, n_gy, *refs):
    count = len(INPUTS)
    sources, refs = refs[:count], refs[count:]
    (new_pos_ref, new_vel_ref, new_frc_ref, arr_ref), refs = refs[:4], refs[4:]
    local, refs = refs[:count], refs[count:]
    send_x, send_y, recv_a, send_m, recv_m, send_c, recv_c, load_sems, sems_out, sems_in = refs[:10]
    relay_sem, known_sem = refs[10:]
    gx = lax.axis_index("gx")
    gy = lax.axis_index("gy")
    row = lax.rem(gx, ROW)

    def place(dx, dy):
        return (lax.rem(gx + (dx + n_gx), n_gx), lax.rem(gy + (dy + n_gy), n_gy))

    def signal(semaphore, target):
        pl.semaphore_signal(semaphore, inc=1, device_id=target, device_id_type=MESH)

    barrier = pltpu.get_barrier_semaphore()

    @pl.when(row == RELAY)
    def _():
        signal(barrier, place(ROW - 1 - RELAY, 0))
        for dy in (-1, 0, 1):
            signal(barrier, place(ROW - RELAY, dy))

    @pl.when(row < ROW - 1)
    def _():
        for dy in (-1, 0, 1):
            signal(barrier, place(1, dy))

    for move in FAR_FIRST:
        if move[0] != 1:
            signal(barrier, place(*move))

    loads = {
        name: pltpu.make_async_copy(sources[i], local[i], load_sems.at[i])
        for i, name in enumerate(INPUTS)
        if name != "count"
    }
    refs_of = dict(zip(INPUTS, local))
    count_ref = sources[INPUTS.index("count")]
    for name in LOAD_ORDER:
        loads[name].start()

    def loaded(*wanted):
        for name in wanted:
            loads[name].wait()
        return [refs_of[name] for name in wanted]

    def copy(phase, source, target, device, arrive=None):
        return pltpu.make_async_remote_copy(
            src_ref=source,
            dst_ref=target,
            send_sem=sems_out.at[phase],
            recv_sem=sems_in.at[phase if arrive is None else arrive],
            device_id=device,
            device_id_type=MESH,
        )

    def all_of(phase, ref, tiles):
        whole = ref.at[pl.ds(0, tiles)]
        return copy(phase, whole, whole, place(1, 0))

    lane = iota((1, 128), 1)
    rows = iota((8, 128), 0)
    low_x = (lane % 64) < 32
    low_y = lane < 64

    spec_ref, inv_mass_ref, frc_ref, vel_ref, pos_ref, xface_ref, yface_ref = loaded(*FIRST)
    species = spec_ref[...].reshape(1, 128)
    inv_mass = jnp.zeros((1, 128), F32)
    for k in range(inv_mass_ref.shape[0]):
        inv_mass = jnp.where(species == k, inv_mass_ref[k], inv_mass)
    halfway = vel_ref[...] + 0.5 * TIME_STEP * frc_ref[...] * inv_mass
    coords = pos_ref[...] + TIME_STEP * halfway
    new_pos_ref[...] = coords
    species_row = species.astype(F32)
    minus = jnp.full((1, 128), -1.0, F32)
    record = jnp.concatenate([coords, species_row, minus, jnp.zeros((3, 128), F32)], axis=0)

    xface = xface_ref[...].reshape(1, 64)
    xface2 = jnp.concatenate([xface, xface], axis=1)
    yface = yface_ref[...].reshape(1, 128)
    y_owned = yface < 128
    blank = jnp.full((1, 32), -1, jnp.int32)
    lower = jnp.concatenate([xface[:, :32]] * 3 + [blank], axis=1)
    upper = jnp.concatenate([xface[:, 32:]] * 3 + [blank], axis=1)
    owned_y = jnp.where(y_owned, yface, -1)
    lists = jnp.concatenate(
        [
            jnp.zeros((4, 128), F32),
            yface.astype(F32),
            owned_y.astype(F32),
            lower.astype(F32),
            upper.astype(F32),
        ],
        axis=0,
    )
    send_x[...] = jnp.where(rows < 5, lanes_at(record, xface2), lists)
    send_y[...] = jnp.where(rows < 4, lanes_at(record, jnp.where(y_owned, yface, 0)), lists)
    pl.semaphore_wait(barrier, len(MOVES) + row // (ROW - 1))

    @pl.when(row == ROW - 1)
    def _():
        signal(relay_sem, place(RELAY + 1 - ROW, 0))

    at_start = 1 - (row + (ROW - 1)) // ROW
    last = place(ROW - 1 - RELAY, 0)
    for m in FAR_FIRST:
        source, slot = send_y if m[0] == 0 else send_x, cell(*m)
        if m[0] == -1:
            there = slot + at_start * (10 + m[1] - slot)
            target = place(-1 - at_start * (ROW - 1 - RELAY), m[1])
            copy(0, source, recv_a.at[there], target, 3 * at_start).start()
        else:
            copy(0, source, recv_a.at[slot], place(*m)).start()

    (migrants_ref,) = loaded("migrants")
    slots = jnp.concatenate([migrants_ref[...]] * 16, axis=1)
    valid = slots >= 0
    at = jnp.where(valid, slots, 0)
    field = lane // 8
    gain = 0.5 * TIME_STEP * inv_mass
    out = jnp.where(field == 7, 1.0, jnp.zeros((8, 128), F32))
    fields = [coords[0:1], coords[1:2], coords[2:3]]
    fields += [halfway[0:1], halfway[1:2], halfway[2:3], species_row, None, gain]
    for number, value in enumerate(fields):
        if value is not None:
            out = jnp.where(field == number, lanes_at(jnp.broadcast_to(value, (8, 128)), at), out)
    dx_col = row_const([BOX_SIDE * m[0] for m in MOVES], (8, 128))
    dy_col = row_const([BOX_SIDE * m[1] for m in MOVES], (8, 128))
    out = out - jnp.where(field == 0, dx_col, jnp.where(field == 1, dy_col, 0.0))
    out = jnp.where(valid, out, 0.0)
    send_m[...] = jnp.where(field == 9, slots.astype(F32), out)
    leave = [
        copy(1, send_m.at[pl.ds(c, 1)], recv_m.at[pl.ds(c, 1)], place(*m))
        for c, m in enumerate(MOVES)
    ]
    for m, c in zip(MOVES, leave):
        if m[0] == -1:
            pl.when(row > 0)(c.start)
        else:
            c.start()

    neighbor_ref, center_ref = loaded("neighbor", "center")
    neighbor = neighbor_ref[...].reshape(1, 256)
    center = center_ref[...].reshape(1, 256)
    live = iota((1, 256), 1) < count_ref[0]
    place_n = jnp.where(
        neighbor < 128,
        neighbor,
        jnp.where(neighbor < 192, ((neighbor - 128) ^ 32) + 128, ((neighbor - 192) ^ 64) + 256),
    )

    def edge_side(tile, index):
        return jnp.concatenate(
            [lanes_at(tile, index[:, 128 * h : 128 * h + 128] & 127) for h in range(2)], axis=1
        )

    own = edge_side(record, center)
    near_owned = edge_side(record, place_n)
    hot_n = (iota((384, 256), 0) == place_n).astype(F32)
    hot_c = (iota((128, 256), 0) == center).astype(F32)
    hot_owned = (hot_n[:128] - hot_c).astype(BF16)
    hot_y = hot_n[256:].astype(BF16)
    ghost = place_n - 128
    in_x = (ghost >= 0) & (ghost < 64)
    at_x = jnp.where(in_x, jnp.where(ghost < 32, 32, 128) + ghost, -1)
    face_rows = jnp.concatenate([owned_y, lower, upper], axis=1)
    hot_f = (iota((128, 384), 0) == face_rows).astype(F32).astype(BF16)
    c_live = center.astype(F32)
    rows_e = iota((8, 256), 0)
    left_c = jnp.where(rows_e == 0, jnp.where(live, c_live, -1.0), jnp.where(rows_e == 1, 1.0, 0.0))
    right_c = jnp.where(rows_e == 0, 1.0, jnp.where(rows_e == 1, jnp.where(live, -c_live, 2.0), 0.0))
    same = dot(left_c.astype(BF16), right_c.astype(BF16), (0, 0)) == 0.0
    k0 = same.astype(F32).astype(BF16)

    def merged(tensor_ref, mix_ref):
        tensor = tensor_ref[...]
        width = tensor.shape[1]
        high, low = halves(
            jnp.concatenate(
                [
                    lax.dot_general(
                        tensor,
                        mix_ref[pl.ds(width * deg, width), :],
                        (((1,), (0,)), ((), ())),
                        precision=lax.Precision.HIGHEST,
                        preferred_element_type=F32,
                    )
                    for deg in range(3)
                ],
                axis=1,
            )
        )
        blocks = [
            doubled(high[:, 128 * d : 128 * d + 128], low[:, 128 * d : 128 * d + 128])
            for d in range(3)
        ]
        return tuple(jnp.concatenate(each, axis=1) for each in zip(*blocks))

    tensor1_ref, mix1_ref, tensor2_ref, mix2_ref = loaded("tensor1", "mix1", "tensor2", "mix2")
    final_ref, radial_ref, emb_c_ref, emb_n_ref = loaded("final", "radial", "emb_c", "emb_n")
    (eout_ref,) = loaded("eout")
    layers = (merged(tensor1_ref, mix1_ref), merged(tensor2_ref, mix2_ref))
    final_forward, final_backward = doubled(*halves(final_ref[...]))
    pad3 = jnp.zeros((3, 128), F32)
    table = jnp.concatenate([radial_ref[...], emb_c_ref[...], pad3, emb_n_ref[...], pad3], axis=0)
    table_h, table_l = halves_f32(table)
    table_cat = jnp.concatenate(
        [table_h, table_l, table_h[:8], jnp.zeros((8, 128), F32)], axis=0
    ).astype(BF16)
    rad_h, rad_l = table_h[:8], table_l[:8]
    rad_cat = jnp.concatenate([rad_h, rad_l], axis=0).astype(BF16)

    @pl.when(row == RELAY)
    def _():
        all_of(3, recv_a, 3).wait_recv()
        pl.semaphore_wait(relay_sem, 1)
        for dy in (-1, 0, 1):
            copy(3, recv_a.at[10 + dy], recv_a.at[cell(-1, dy)], last, 0).start()

    all_of(0, recv_a, 8).wait_recv()

    @pl.when(row == 0)
    def _():
        signal(known_sem, place(1, 0))
        signal(known_sem, place(1, 1))
        for m, c in zip(MOVES, leave):
            if m[0] == -1:
                c.start()

    def pick4(tiles):
        quarter = lane // 32
        result = tiles[3]
        for q in (2, 1, 0):
            result = jnp.where(quarter == q, tiles[q], result)
        return result

    x_shift = jnp.where(rows == 0, jnp.where(low_x, BOX_SIDE, -BOX_SIDE), 0.0)
    y_shift = jnp.where(rows == 1, jnp.where(low_y, BOX_SIDE, -BOX_SIDE), 0.0)
    ghost_x = jnp.where(low_x, recv_a[cell(-1, 0)], recv_a[cell(1, 0)]) + x_shift
    far_x = (
        pick4(
            [recv_a[cell(-1, -1)], recv_a[cell(1, -1)], recv_a[cell(-1, 1)], recv_a[cell(1, 1)]]
        )
        + x_shift
    )
    ghost_y = jnp.where(low_y, recv_a[cell(0, -1)], recv_a[cell(0, 1)])
    listed = ghost_y[4:5].astype(jnp.int32)
    via_x = listed >= 128
    far_lane = jnp.where(via_x, ((listed - 128) ^ 32) + jnp.where(low_y, 0, 64), 0)
    ghost_y = jnp.where(via_x, lanes_at(far_x, far_lane), ghost_y) + y_shift
    far_at = (far_lane + 96 * ((far_lane // 32) % 2)).astype(F32)
    ghost_y = jnp.where(rows == 4, jnp.where(via_x, far_at, -1.0), ghost_y)

    near = jnp.where(
        place_n < 128,
        near_owned,
        jnp.where(place_n < 256, edge_side(ghost_x, place_n), edge_side(ghost_y, place_n)),
    )
    side = iota((256, 256), 0)
    hot_x = (side == jnp.where(in_x, at_x, near[4:5].astype(jnp.int32))).astype(F32).astype(BF16)

    offset = (near - own) * (1.0 / CUTOFF)
    ux, uy, uz = offset[0:1], offset[1:2], offset[2:3]
    squared = ux * ux + uy * uy + uz * uz
    tees = jnp.concatenate(
        [
            ux,
            uy,
            uz,
            ux * uy,
            uy * uz,
            uz * ux,
            0.5 * (ux * ux - uy * uy),
            (2.0 * uz * uz - ux * ux - uy * uy) * Y20,
        ],
        axis=0,
    )
    minus_inv_w = row_const([-1.0 / w for w in WIDTHS], (8, 256))
    radial = jnp.exp(squared * minus_inv_w)
    hot_sc = (rows_e == own[3:4].astype(jnp.int32)).astype(F32)
    hot_sn = (rows_e == near[3:4].astype(jnp.int32)).astype(F32)
    radial_h, radial_l = halves_f32(radial)
    features = jnp.concatenate(
        [radial_h, hot_sc, hot_sn, radial_h, hot_sc, hot_sn, radial_l, jnp.zeros((8, 256), F32)],
        axis=0,
    ).astype(BF16)
    hidden_pre = dot(features, table_cat, (0, 0))

    tees_h, tees_l = halves_f32(tees)
    tees_r = jnp.concatenate([tees_h, tees_l, tees_h, jnp.zeros((8, 256), F32)], axis=0).astype(BF16)

    def degree(mask):
        left = jnp.concatenate([tees_h, tees_h, tees_l, jnp.zeros((8, 256), F32)], axis=0)
        left = jnp.where(mask, left, 0.0).astype(BF16)
        return halves(jnp.where(same, dot(left, tees_r, (0, 0)), 0.0))

    row32 = iota((32, 256), 0) % 8
    k1_h, k1_l = degree(row32 < 3)
    k2_h, k2_l = degree(row32 >= 3)

    k_wide = jnp.concatenate([k0, k1_h, k2_h], axis=1)
    k_wide_l = jnp.concatenate([k1_l, k2_l], axis=1)
    k_tall = jnp.concatenate([k0, k1_h, k2_h], axis=0)
    k_tall_l = jnp.concatenate([k1_l, k2_l], axis=0)

    sig = sigmoid(hidden_pre)
    hidden = hidden_pre * sig
    slope0 = sig * (1.0 + hidden_pre * (1.0 - sig))
    slopes, values = [], []
    for forward, _ in layers:
        hid_h, hid_l = halves(hidden)
        pair = dot(jnp.concatenate([hid_h, hid_l], axis=1), forward)
        split = [
            halves(pair[:, 256 * d : 256 * d + 128] + pair[:, 256 * d + 128 : 256 * d + 256])
            for d in range(3)
        ]
        values.append(split)
        both = sum(dot(k, jnp.concatenate(split[d], axis=1)) for d, k in enumerate((k0, k1_h, k2_h)))
        rest = dot(k1_l, split[1][0]) + dot(k2_l, split[2][0])
        pre = both[:, :128] + both[:, 128:] + rest
        sig = sigmoid(pre)
        hidden = hidden + pre * sig
        slopes.append(sig * (1.0 + pre * (1.0 - sig)))

    hid_h, hid_l = halves(hidden)
    pre = dot(jnp.concatenate([hid_h, hid_l], axis=1), final_forward)
    pre = pre[:, :128] + pre[:, 128:]
    sig = sigmoid(pre)
    back = eout_ref[...].reshape(1, 128) * (sig * (1.0 + pre * (1.0 - sig)))
    back_h, back_l = halves(back)
    grad = dot(jnp.concatenate([back_h, back_l], axis=1), final_backward, (1, 1))
    grad = grad[:, :128] + grad[:, 128:]
    downs = []
    for index in (1, 0):
        _, backward = layers[index]
        down_h, down_l = halves(grad * slopes[index])
        downs.append((down_h, down_l))
        both = dot(k_tall, jnp.concatenate([down_h, down_l], axis=1))
        rest = dot(k_tall_l, down_h)
        parts = [both[:256, :128] + both[:256, 128:]]
        for d in (1, 2):
            at = slice(256 * d, 256 * d + 256)
            parts.append(both[at, :128] + both[at, 128:] + rest[256 * d - 256 : 256 * d])
        both = dot(
            jnp.concatenate([half for part in parts for half in halves(part)], axis=1),
            backward,
            (1, 1),
        )
        grad = grad + (both[:, :128] + both[:, 128:])
    (d2_h, d2_l), (d1_h, d1_l) = downs
    outer_left = jnp.concatenate([d1_h, d2_h, d1_l, d2_l, d1_h, d2_h], axis=1)
    moved = []
    for d in (1, 2):
        (v1_h, v1_l), (v2_h, v2_l) = values[0][d], values[1][d]
        outer = dot(
            outer_left, jnp.concatenate([v1_h, v2_h, v1_h, v2_h, v1_l, v2_l], axis=1), (1, 1)
        )
        turned = jnp.where(same, outer, 0.0)
        out_h, out_l = halves(turned + turned.T)
        pair = jnp.concatenate([tees_h, tees_l], axis=0).astype(BF16)
        high_t = tees_h.astype(BF16)
        first_part = dot(pair, out_h)
        moved.append(first_part[:8] + first_part[8:] + dot(high_t, out_l))
    d_tees = jnp.where(rows_e < 3, moved[0], moved[1])

    g_h, g_l = halves(grad * slope0)
    d_radial = dot(rad_cat, g_h, (1, 1))
    d_radial = d_radial[:8] + d_radial[8:] + dot(rad_cat[:8], g_l, (1, 1))
    d_squared = 2.0 * jnp.sum(d_radial * radial * minus_inv_w, axis=0, keepdims=True)
    dxy, dyz, dzx = d_tees[3:4], d_tees[4:5], d_tees[5:6]
    dxx, dzz = d_tees[6:7], (2.0 * Y20) * d_tees[7:8]
    dux = d_tees[0:1] + ux * (d_squared + dxx - dzz) + uy * dxy + uz * dzx
    duy = d_tees[1:2] + uy * (d_squared - dxx - dzz) + ux * dxy + uz * dyz
    duz = d_tees[2:3] + uz * (d_squared + 2.0 * dzz) + uy * dyz + ux * dzx
    d_edge = jnp.concatenate([dux, duy, duz, jnp.zeros((5, 256), F32)], axis=0)
    d_edge = jnp.where(live, d_edge * (1.0 / CUTOFF), 0.0)
    d_edge_h, d_edge_l = halves_f32(d_edge)
    d_pair = jnp.concatenate([d_edge_h, d_edge_l], axis=0).astype(BF16)

    spread = dot(d_pair, jnp.concatenate([hot_owned, hot_y, hot_x], axis=0), (1, 1))
    spread = spread[:4] + spread[8:12]
    mine = (spread[:, 384:], spread[:, :128], spread[:, 128:256], spread[:, 256:384])
    for number, value in enumerate(mine):
        send_c[number] = value

    def seat(ox, oy):
        return (ox + 2) * n_gy + oy % n_gy

    second = []
    for mx in (2, 1, -2, -1, 0):
        for my in (2, -1, 1, 0):
            if (mx, my) != (0, 0):
                slot = seat(-mx, -my)
                used = {-2: (0, 1), -1: (0, 3), 0: (0, 4), 1: (1, 3), 2: (3, 1)}[mx]
                c = copy(2, send_c.at[pl.ds(*used)], recv_c.at[slot, pl.ds(*used)], place(mx, my))
                second.append(c)
                if mx == -2:
                    pl.when(row != 1)(c.start)
                else:
                    c.start()

    @pl.when(row == 1)
    def _():
        pl.semaphore_wait(known_sem, 2)
        for c in second[2 * n_gy : 3 * n_gy]:
            c.start()

    all_of(1, recv_m, 8).wait_recv()
    arriving = recv_m[...]
    slot_lane = lane % 8
    gains = lanes_at(arriving, 64 + slot_lane)
    listed = lanes_at(arriving, 72 + slot_lane)
    listed_row = jnp.sum(jnp.where(rows == field, listed, 0.0), axis=0, keepdims=True)
    listed_at = jnp.maximum(listed_row, 0.0).astype(jnp.int32)
    spots = iota((64, 128), 0)
    arriving_lists = jnp.where(field == 9, arriving, 0.0).astype(BF16)
    from_source = (iota((64, 8), 0) // 8 == iota((64, 8), 1)).astype(F32).astype(BF16)
    listed_col = jnp.sum(
        jnp.where(
            iota((64, 128), 1) == 72 + spots % 8, dot(from_source, arriving_lists), 0.0
        ),
        axis=1,
        keepdims=True,
    )
    spot_source = iota((64, 384), 0) // 8
    hot_spots = []
    for c, m in enumerate(MOVES):
        tile = recv_a[cell(*m)]
        faces = jnp.concatenate([tile[5:6], tile[6:7], tile[7:8]], axis=1)
        hit = jnp.where(spot_source == c, faces, -2.0) == listed_col
        hot_spots.append(hit.astype(F32).astype(BF16))
    hot_spots = jnp.concatenate(hot_spots, axis=1)

    all_of(2, recv_c, 3 * n_gy - 1).wait_recv()

    def part(ox, oy, tile):
        if (ox, oy) == (0, 0):
            return mine[tile]
        return recv_c[seat(ox, oy), tile]

    third = lane // 32

    def inward(bx, by):
        sides = [jnp.where(low_y, part(bx, by - 1, 2), part(bx, by + 1, 2))]
        for ox, tile in ((bx - 1, 3), (bx + 1, 0)):
            above, beside = part(ox, by - 1, tile), part(ox, by, tile)
            below = part(ox, by + 1, tile)
            sides.append(jnp.where(third == 0, above, jnp.where(third == 1, beside, below)))
        high, low = halves_f32(jnp.concatenate(sides, axis=1))
        return jnp.concatenate([high, low, jnp.zeros((8, 384), F32)], axis=0).astype(BF16)

    def force_of(owned, back):
        return -(owned[:3] + back[:3] + back[4:7])

    force = force_of(mine[1], dot(inward(0, 0), hot_f, (1, 1)))
    new_frc_ref[...] = force
    new_vel_ref[...] = halfway + gain * force

    owned = jnp.zeros((8, 128), F32)
    for c, m in enumerate(MOVES):
        tile = jnp.concatenate([part(-m[0], -m[1], 1)] * 2, axis=0)
        owned = jnp.where(field == c, lanes_at(tile, listed_at), owned)
    back = dot(
        jnp.concatenate([inward(-m[0], -m[1]) for m in MOVES], axis=1), hot_spots, (1, 1)
    )
    back = jnp.concatenate([back, jnp.zeros((16, 64), F32)], axis=1)
    arriving_force = force_of(owned, back)
    push = jnp.zeros((8, 128), F32)
    for axis in range(3):
        value = jnp.broadcast_to(arriving_force[axis : axis + 1], (8, 128))
        push = jnp.where(field == 3 + axis, lanes_at(value, rows * 8 + slot_lane), push)
    result = arriving + gains * push
    for a in range(3):
        arr_ref[a] = jnp.concatenate(
            [
                jnp.zeros((1, 64), F32)
                if (a, b) == (1, 1)
                else result[MOVES.index((a - 1, b - 1)), 0:64].reshape(1, 64)
                for b in range(3)
            ],
            axis=0,
        )
    all_of(0, recv_a, 8).wait_send()
    all_of(1, recv_m, 8).wait_send()
    all_of(2, recv_c, 3 * n_gy - 1).wait_send()

    @pl.when(row == RELAY)
    def _():
        all_of(3, recv_a, 3).wait_send()


def store(*refs):
    copies = [pltpu.make_async_copy(refs[i], refs[4 + i], refs[8].at[i]) for i in range(4)]
    for c in copies:
        c.start()
    for c in copies:
        c.wait()


def solution(mesh):
    n_gx, n_gy = mesh.shape["gx"], mesh.shape["gy"]
    vmem = pl.BlockSpec(memory_space=pltpu.VMEM)
    smem = pl.BlockSpec(memory_space=pltpu.SMEM)
    hbm = pl.BlockSpec(memory_space=pltpu.HBM)

    def hold(name, arg):
        return arg if name == "count" else pltpu.with_memory_space_constraint(arg, pltpu.HBM)

    def body(*args):
        def whole(*refs):
            kernel(n_gx, n_gy, *refs)

        atoms = jax.ShapeDtypeStruct(args[0].shape, F32)
        outs = (atoms, atoms, atoms, jax.ShapeDtypeStruct((3, 3, 64), F32))
        tile = pltpu.VMEM((8, 128), F32)
        scalars = ("inv_mass", "count")
        results = pl.pallas_call(
            whole,
            out_shape=outs,
            in_specs=[smem if name == "count" else hbm for name in INPUTS],
            out_specs=(vmem,) * 4,
            scratch_shapes=[
                (pltpu.SMEM if name in scalars else pltpu.VMEM)(arg.shape, arg.dtype)
                for name, arg in zip(INPUTS, args)
            ]
            + [tile, tile, pltpu.VMEM((12, 8, 128), F32), tile, tile]
            + [
                pltpu.VMEM((4, 4, 128), F32),
                pltpu.VMEM((5 * n_gy, 4, 4, 128), F32),
                pltpu.SemaphoreType.DMA((len(args),)),
                pltpu.SemaphoreType.DMA((4,)),
                pltpu.SemaphoreType.DMA((4,)),
                pltpu.SemaphoreType.REGULAR,
                pltpu.SemaphoreType.REGULAR,
            ],
            compiler_params=pltpu.CompilerParams(
                collective_id=0, has_side_effects=True, vmem_limit_bytes=VMEM_BYTES
            ),
        )(*(hold(name, arg) for name, arg in zip(INPUTS, args)))
        return pl.pallas_call(
            store,
            out_shape=outs,
            in_specs=[vmem] * 4,
            out_specs=(hbm,) * 4,
            scratch_shapes=[pltpu.SemaphoreType.DMA((4,))],
            compiler_params=pltpu.CompilerParams(vmem_limit_bytes=VMEM_BYTES),
        )(*results)

    bricks = ("gx", "gy")
    atoms_spec = P(None, bricks)
    in_specs = (
        (atoms_spec,) * 3
        + (P(bricks), P())
        + (P(bricks),) * 5
        + (P(bricks, None),)
        + (P(),) * 9
    )
    return jax.shard_map(
        body,
        mesh=mesh,
        in_specs=in_specs,
        out_specs=(atoms_spec,) * 3 + (P("gx", "gy", None),),
        check_vma=False,
    )
```

```python
import jax
import jax.numpy as jnp
from jax import lax
from jax.experimental import pallas as pl
from jax.experimental.pallas import tpu as pltpu
from jax.sharding import PartitionSpec as P

BOX_SIDE = 2.0
CUTOFF = 2.0
TIME_STEP = 0.05
WIDTHS = tuple((0.1 * 20.0 ** (k / 7.0) for k in range(8)))
Y20 = 0.28867513459481287
MESH = pl.DeviceIdType.MESH
F32 = jnp.float32
BF16 = jnp.bfloat16
VMEM_BYTES = 32 * 1024 * 1024

MOVES = tuple((a, b) for a in (-1, 0, 1) for b in (-1, 0, 1) if (a, b) != (0, 0))
ROW = 32
RELAY = 3
FAR_FIRST = tuple(sorted(MOVES, key=lambda move: (-abs(move[0]), -move[0])))


INPUTS = (
    "pos",
    "vel",
    "frc",
    "spec",
    "inv_mass",
    "xface",
    "yface",
    "center",
    "neighbor",
    "count",
    "migrants",
    "emb_c",
    "emb_n",
    "radial",
    "tensor1",
    "mix1",
    "tensor2",
    "mix2",
    "final",
    "eout",
)
FIRST = ("spec", "inv_mass", "frc", "vel", "pos", "xface", "yface")
LOAD_ORDER = FIRST + tuple(name for name in INPUTS if name not in FIRST and name != "count")


def cell(dx, dy):
    return (dx + 1) * 3 + dy + 1


def iota(shape, dim):
    return lax.broadcasted_iota(jnp.int32, shape, dim)


def halves(value):
    high = value.astype(BF16)
    low = (value - high.astype(F32)).astype(BF16)
    return high, low


def halves_f32(value):
    high = value.astype(BF16).astype(F32)
    return high, value - high


def doubled(high, low):
    return (
        jnp.concatenate([jnp.concatenate([high, low], axis=1)] * 2, axis=0),
        jnp.concatenate([jnp.concatenate([high] * 2, axis=1), jnp.concatenate([low] * 2, axis=1)], axis=0),
    )


def dot(left, right, contract=(1, 0)):
    return lax.dot_general(
        left, right, (((contract[0],), (contract[1],)), ((), ())), preferred_element_type=F32
    )


def lanes_at(tile, index):
    return jnp.take_along_axis(
        tile, jnp.broadcast_to(index, tile.shape), axis=1, mode="promise_in_bounds"
    )


def sigmoid(value):
    return 0.5 + 0.5 * jnp.tanh(0.5 * value)


def row_const(values, shape):
    rows = iota(shape, 0)
    result = jnp.zeros(shape, F32)
    for index, value in enumerate(values):
        result = jnp.where(rows == index, F32(value), result)
    return result


def kernel(n_gx, n_gy, *refs):
    count = len(INPUTS)
    sources, refs = refs[:count], refs[count:]
    (new_pos_ref, new_vel_ref, new_frc_ref, arr_ref), refs = refs[:4], refs[4:]
    local, refs = refs[:count], refs[count:]
    send_x, send_y, recv_a, send_m, recv_m, send_c, recv_c, load_sems, sems_out, sems_in = refs[:10]
    relay_sem, known_sem = refs[10:]
    gx = lax.axis_index("gx")
    gy = lax.axis_index("gy")
    row = lax.rem(gx, ROW)

    near_x = {dx: lax.rem(gx + (dx + n_gx), n_gx) for dx in (-2, -1, 0, 1, 2)}
    near_y = {dy: lax.rem(gy + (dy + n_gy), n_gy) for dy in (-1, 0, 1, 2)}

    def place(dx, dy):
        if isinstance(dx, int) and dx in near_x:
            return near_x[dx], near_y[dy]
        return lax.rem(gx + (dx + n_gx), n_gx), near_y[dy]

    def signal(semaphore, target):
        pl.semaphore_signal(semaphore, inc=1, device_id=target, device_id_type=MESH)

    barrier = pltpu.get_barrier_semaphore()

    @pl.when(row == RELAY)
    def _():
        signal(barrier, place(ROW - 1 - RELAY, 0))
        for dy in (-1, 0, 1):
            signal(barrier, place(ROW - RELAY, dy))

    @pl.when(row < ROW - 1)
    def _():
        for dy in (-1, 0, 1):
            signal(barrier, place(1, dy))

    for move in FAR_FIRST:
        if move[0] != 1:
            signal(barrier, place(*move))

    loads = {
        name: pltpu.make_async_copy(sources[i], local[i], load_sems.at[i])
        for i, name in enumerate(INPUTS)
        if name != "count"
    }
    refs_of = dict(zip(INPUTS, local))
    count_ref = sources[INPUTS.index("count")]
    for name in LOAD_ORDER:
        loads[name].start()

    def loaded(*wanted):
        for name in wanted:
            loads[name].wait()
        return [refs_of[name] for name in wanted]

    def copy(phase, source, target, device, arrive=None):
        return pltpu.make_async_remote_copy(
            src_ref=source,
            dst_ref=target,
            send_sem=sems_out.at[phase],
            recv_sem=sems_in.at[phase if arrive is None else arrive],
            device_id=device,
            device_id_type=MESH,
        )

    def all_of(phase, ref, tiles):
        whole = ref.at[pl.ds(0, tiles)]
        return copy(phase, whole, whole, place(1, 0))

    lane = iota((1, 128), 1)
    rows = iota((8, 128), 0)
    low_x = (lane % 64) < 32
    low_y = lane < 64

    spec_ref, inv_mass_ref, frc_ref, vel_ref, pos_ref, xface_ref, yface_ref = loaded(*FIRST)
    species = spec_ref[...].reshape(1, 128)
    inv_mass = jnp.zeros((1, 128), F32)
    for k in range(inv_mass_ref.shape[0]):
        inv_mass = jnp.where(species == k, inv_mass_ref[k], inv_mass)
    halfway = vel_ref[...] + 0.5 * TIME_STEP * frc_ref[...] * inv_mass
    coords = pos_ref[...] + TIME_STEP * halfway
    new_pos_ref[...] = coords
    species_row = species.astype(F32)
    minus = jnp.full((1, 128), -1.0, F32)
    record = jnp.concatenate([coords, species_row, minus, jnp.zeros((3, 128), F32)], axis=0)

    xface = xface_ref[...].reshape(1, 64)
    xface2 = jnp.concatenate([xface, xface], axis=1)
    yface = yface_ref[...].reshape(1, 128)
    y_owned = yface < 128
    blank = jnp.full((1, 32), -1, jnp.int32)
    lower = jnp.concatenate([xface[:, :32]] * 3 + [blank], axis=1)
    upper = jnp.concatenate([xface[:, 32:]] * 3 + [blank], axis=1)
    owned_y = jnp.where(y_owned, yface, -1)
    lists = jnp.concatenate(
        [
            jnp.zeros((4, 128), F32),
            yface.astype(F32),
            owned_y.astype(F32),
            lower.astype(F32),
            upper.astype(F32),
        ],
        axis=0,
    )
    send_x[...] = jnp.where(rows < 5, lanes_at(record, xface2), lists)
    send_y[...] = jnp.where(rows < 4, lanes_at(record, jnp.where(y_owned, yface, 0)), lists)
    pl.semaphore_wait(barrier, len(MOVES) + row // (ROW - 1))

    @pl.when(row == ROW - 1)
    def _():
        signal(relay_sem, place(RELAY + 1 - ROW, 0))

    at_start = 1 - (row + (ROW - 1)) // ROW
    last = place(ROW - 1 - RELAY, 0)
    for m in FAR_FIRST:
        source, slot = send_y if m[0] == 0 else send_x, cell(*m)
        if m[0] == -1:
            there = slot + at_start * (10 + m[1] - slot)
            target = place(-1 - at_start * (ROW - 1 - RELAY), m[1])
            copy(0, source, recv_a.at[there], target, 3 * at_start).start()
        else:
            copy(0, source, recv_a.at[slot], place(*m)).start()

    (migrants_ref,) = loaded("migrants")
    slots = jnp.concatenate([migrants_ref[...]] * 16, axis=1)
    valid = slots >= 0
    at = jnp.where(valid, slots, 0)
    field = lane // 8
    gain = 0.5 * TIME_STEP * inv_mass
    out = jnp.where(field == 7, 1.0, jnp.zeros((8, 128), F32))
    fields = [coords[0:1], coords[1:2], coords[2:3]]
    fields += [halfway[0:1], halfway[1:2], halfway[2:3], species_row, None, gain]
    for number, value in enumerate(fields):
        if value is not None:
            out = jnp.where(field == number, lanes_at(jnp.broadcast_to(value, (8, 128)), at), out)
    dx_col = row_const([BOX_SIDE * m[0] for m in MOVES], (8, 128))
    dy_col = row_const([BOX_SIDE * m[1] for m in MOVES], (8, 128))
    out = out - jnp.where(field == 0, dx_col, jnp.where(field == 1, dy_col, 0.0))
    out = jnp.where(valid, out, 0.0)
    send_m[...] = jnp.where(field == 9, slots.astype(F32), out)
    leave = [
        copy(1, send_m.at[pl.ds(c, 1)], recv_m.at[pl.ds(c, 1)], place(*m))
        for c, m in enumerate(MOVES)
    ]
    leave_back = [c for m, c in zip(MOVES, leave) if m[0] == -1]
    for m, c in zip(MOVES, leave):
        if m[0] != -1:
            c.start()

    @pl.when(row > 0)
    def _():
        for c in leave_back:
            c.start()

    neighbor_ref, center_ref = loaded("neighbor", "center")
    neighbor = neighbor_ref[...].reshape(1, 256)
    center = center_ref[...].reshape(1, 256)
    live = iota((1, 256), 1) < count_ref[0]
    place_n = jnp.where(
        neighbor < 128,
        neighbor,
        jnp.where(neighbor < 192, ((neighbor - 128) ^ 32) + 128, ((neighbor - 192) ^ 64) + 256),
    )

    def edge_side(tile, index):
        return jnp.concatenate(
            [lanes_at(tile, index[:, 128 * h : 128 * h + 128] & 127) for h in range(2)], axis=1
        )

    own = edge_side(record, center)
    near_owned = edge_side(record, place_n)
    hot_n = (iota((384, 256), 0) == place_n).astype(F32)
    hot_c = (iota((128, 256), 0) == center).astype(F32)
    hot_owned = (hot_n[:128] - hot_c).astype(BF16)
    hot_y = hot_n[256:].astype(BF16)
    ghost = place_n - 128
    in_x = (ghost >= 0) & (ghost < 64)
    at_x = jnp.where(in_x, jnp.where(ghost < 32, 32, 128) + ghost, -1)
    face_rows = jnp.concatenate([owned_y, lower, upper], axis=1)
    hot_f = (iota((128, 384), 0) == face_rows).astype(F32).astype(BF16)
    c_live = center.astype(F32)
    rows_e = iota((8, 256), 0)
    left_c = jnp.where(rows_e == 0, jnp.where(live, c_live, -1.0), jnp.where(rows_e == 1, 1.0, 0.0))
    right_c = jnp.where(rows_e == 0, 1.0, jnp.where(rows_e == 1, jnp.where(live, -c_live, 2.0), 0.0))
    same = dot(left_c.astype(BF16), right_c.astype(BF16), (0, 0)) == 0.0
    k0 = same.astype(F32).astype(BF16)

    def merged(tensor_ref, mix_ref):
        tensor = tensor_ref[...]
        width = tensor.shape[1]
        high, low = halves(
            jnp.concatenate(
                [
                    lax.dot_general(
                        tensor,
                        mix_ref[pl.ds(width * deg, width), :],
                        (((1,), (0,)), ((), ())),
                        precision=lax.Precision.HIGHEST,
                        preferred_element_type=F32,
                    )
                    for deg in range(3)
                ],
                axis=1,
            )
        )
        blocks = [
            doubled(high[:, 128 * d : 128 * d + 128], low[:, 128 * d : 128 * d + 128])
            for d in range(3)
        ]
        return tuple(jnp.concatenate(each, axis=1) for each in zip(*blocks))

    tensor1_ref, mix1_ref, tensor2_ref, mix2_ref = loaded("tensor1", "mix1", "tensor2", "mix2")
    final_ref, radial_ref, emb_c_ref, emb_n_ref = loaded("final", "radial", "emb_c", "emb_n")
    (eout_ref,) = loaded("eout")
    layers = (merged(tensor1_ref, mix1_ref), merged(tensor2_ref, mix2_ref))
    final_forward, final_backward = doubled(*halves(final_ref[...]))
    pad3 = jnp.zeros((3, 128), F32)
    table = jnp.concatenate([radial_ref[...], emb_c_ref[...], pad3, emb_n_ref[...], pad3], axis=0)
    table_h, table_l = halves_f32(table)
    table_cat = jnp.concatenate(
        [table_h, table_l, table_h[:8], jnp.zeros((8, 128), F32)], axis=0
    ).astype(BF16)
    rad_h, rad_l = table_h[:8], table_l[:8]
    rad_cat = jnp.concatenate([rad_h, rad_l], axis=0).astype(BF16)

    @pl.when(row == RELAY)
    def _():
        all_of(3, recv_a, 3).wait_recv()
        pl.semaphore_wait(relay_sem, 1)
        for dy in (-1, 0, 1):
            copy(3, recv_a.at[10 + dy], recv_a.at[cell(-1, dy)], last, 0).start()

    all_of(0, recv_a, 8).wait_recv()

    @pl.when(row == 0)
    def _():
        signal(known_sem, place(1, 0))
        signal(known_sem, place(1, 1))
        for c in leave_back:
            c.start()

    def pick4(tiles):
        quarter = lane // 32
        result = tiles[3]
        for q in (2, 1, 0):
            result = jnp.where(quarter == q, tiles[q], result)
        return result

    x_shift = jnp.where(rows == 0, jnp.where(low_x, BOX_SIDE, -BOX_SIDE), 0.0)
    y_shift = jnp.where(rows == 1, jnp.where(low_y, BOX_SIDE, -BOX_SIDE), 0.0)
    ghost_x = jnp.where(low_x, recv_a[cell(-1, 0)], recv_a[cell(1, 0)]) + x_shift
    far_x = (
        pick4(
            [recv_a[cell(-1, -1)], recv_a[cell(1, -1)], recv_a[cell(-1, 1)], recv_a[cell(1, 1)]]
        )
        + x_shift
    )
    ghost_y = jnp.where(low_y, recv_a[cell(0, -1)], recv_a[cell(0, 1)])
    listed = ghost_y[4:5].astype(jnp.int32)
    via_x = listed >= 128
    far_lane = jnp.where(via_x, ((listed - 128) ^ 32) + jnp.where(low_y, 0, 64), 0)
    ghost_y = jnp.where(via_x, lanes_at(far_x, far_lane), ghost_y) + y_shift
    far_at = (far_lane + 96 * ((far_lane // 32) % 2)).astype(F32)
    ghost_y = jnp.where(rows == 4, jnp.where(via_x, far_at, -1.0), ghost_y)

    near = jnp.where(
        place_n < 128,
        near_owned,
        jnp.where(place_n < 256, edge_side(ghost_x, place_n), edge_side(ghost_y, place_n)),
    )
    side = iota((256, 256), 0)
    hot_x = (side == jnp.where(in_x, at_x, near[4:5].astype(jnp.int32))).astype(F32).astype(BF16)

    offset = (near - own) * (1.0 / CUTOFF)
    ux, uy, uz = offset[0:1], offset[1:2], offset[2:3]
    squared = ux * ux + uy * uy + uz * uz
    tees = jnp.concatenate(
        [
            ux,
            uy,
            uz,
            ux * uy,
            uy * uz,
            uz * ux,
            0.5 * (ux * ux - uy * uy),
            (2.0 * uz * uz - ux * ux - uy * uy) * Y20,
        ],
        axis=0,
    )
    minus_inv_w = row_const([-1.0 / w for w in WIDTHS], (8, 256))
    radial = jnp.exp(squared * minus_inv_w)
    hot_sc = (rows_e == own[3:4].astype(jnp.int32)).astype(F32)
    hot_sn = (rows_e == near[3:4].astype(jnp.int32)).astype(F32)
    radial_h, radial_l = halves_f32(radial)
    features = jnp.concatenate(
        [radial_h, hot_sc, hot_sn, radial_h, hot_sc, hot_sn, radial_l, jnp.zeros((8, 256), F32)],
        axis=0,
    ).astype(BF16)
    hidden_pre = dot(features, table_cat, (0, 0))

    tees_h, tees_l = halves_f32(tees)
    tees_r = jnp.concatenate([tees_h, tees_l, tees_h, jnp.zeros((8, 256), F32)], axis=0).astype(BF16)

    def degree(mask):
        left = jnp.concatenate([tees_h, tees_h, tees_l, jnp.zeros((8, 256), F32)], axis=0)
        left = jnp.where(mask, left, 0.0).astype(BF16)
        return halves(jnp.where(same, dot(left, tees_r, (0, 0)), 0.0))

    row32 = iota((32, 256), 0) % 8
    k1_h, k1_l = degree(row32 < 3)
    k2_h, k2_l = degree(row32 >= 3)

    k_wide = jnp.concatenate([k0, k1_h, k2_h], axis=1)
    k_wide_l = jnp.concatenate([k1_l, k2_l], axis=1)
    k_tall = jnp.concatenate([k0, k1_h, k2_h], axis=0)
    k_tall_l = jnp.concatenate([k1_l, k2_l], axis=0)

    sig = sigmoid(hidden_pre)
    hidden = hidden_pre * sig
    slope0 = sig * (1.0 + hidden_pre * (1.0 - sig))
    slopes, values = [], []
    for forward, _ in layers:
        hid_h, hid_l = halves(hidden)
        hid = jnp.concatenate([hid_h, hid_l], axis=1)
        split = []
        for d in range(3):
            pair = dot(hid, forward[:, 256 * d : 256 * d + 256])
            split.append(halves(pair[:, :128] + pair[:, 128:]))
        values.append(split)
        both = sum(dot(k, jnp.concatenate(split[d], axis=1)) for d, k in enumerate((k0, k1_h, k2_h)))
        rest = dot(k1_l, split[1][0]) + dot(k2_l, split[2][0])
        pre = both[:, :128] + both[:, 128:] + rest
        sig = sigmoid(pre)
        hidden = hidden + pre * sig
        slopes.append(sig * (1.0 + pre * (1.0 - sig)))

    hid_h, hid_l = halves(hidden)
    pre = dot(jnp.concatenate([hid_h, hid_l], axis=1), final_forward)
    pre = pre[:, :128] + pre[:, 128:]
    sig = sigmoid(pre)
    back = eout_ref[...].reshape(1, 128) * (sig * (1.0 + pre * (1.0 - sig)))
    back_h, back_l = halves(back)
    grad = dot(jnp.concatenate([back_h, back_l], axis=1), final_backward, (1, 1))
    grad = grad[:, :128] + grad[:, 128:]
    downs = []
    for index in (1, 0):
        _, backward = layers[index]
        down_h, down_l = halves(grad * slopes[index])
        downs.append((down_h, down_l))
        both = dot(k_tall, jnp.concatenate([down_h, down_l], axis=1))
        rest = dot(k_tall_l, down_h)
        parts = [both[:256, :128] + both[:256, 128:]]
        for d in (1, 2):
            at = slice(256 * d, 256 * d + 256)
            parts.append(both[at, :128] + both[at, 128:] + rest[256 * d - 256 : 256 * d])
        both = dot(
            jnp.concatenate([half for part in parts for half in halves(part)], axis=1),
            backward,
            (1, 1),
        )
        grad = grad + (both[:, :128] + both[:, 128:])
    (d2_h, d2_l), (d1_h, d1_l) = downs
    outer_left = jnp.concatenate([d1_h, d2_h, d1_l, d2_l, d1_h, d2_h], axis=1)
    moved = []
    for d in (1, 2):
        (v1_h, v1_l), (v2_h, v2_l) = values[0][d], values[1][d]
        outer = dot(
            outer_left, jnp.concatenate([v1_h, v2_h, v1_h, v2_h, v1_l, v2_l], axis=1), (1, 1)
        )
        turned = jnp.where(same, outer, 0.0)
        out_h, out_l = halves(turned + turned.T)
        pair = jnp.concatenate([tees_h, tees_l], axis=0).astype(BF16)
        high_t = tees_h.astype(BF16)
        first_part = dot(pair, out_h)
        moved.append(first_part[:8] + first_part[8:] + dot(high_t, out_l))
    d_tees = jnp.where(rows_e < 3, moved[0], moved[1])

    g_h, g_l = halves(grad * slope0)
    d_radial = dot(rad_cat, g_h, (1, 1))
    d_radial = d_radial[:8] + d_radial[8:] + dot(rad_cat[:8], g_l, (1, 1))
    d_squared = 2.0 * jnp.sum(d_radial * radial * minus_inv_w, axis=0, keepdims=True)
    dxy, dyz, dzx = d_tees[3:4], d_tees[4:5], d_tees[5:6]
    dxx, dzz = d_tees[6:7], (2.0 * Y20) * d_tees[7:8]
    dux = d_tees[0:1] + ux * (d_squared + dxx - dzz) + uy * dxy + uz * dzx
    duy = d_tees[1:2] + uy * (d_squared - dxx - dzz) + ux * dxy + uz * dyz
    duz = d_tees[2:3] + uz * (d_squared + 2.0 * dzz) + uy * dyz + ux * dzx
    d_edge = jnp.concatenate([dux, duy, duz, jnp.zeros((5, 256), F32)], axis=0)
    d_edge = jnp.where(live, d_edge * (1.0 / CUTOFF), 0.0)
    d_edge_h, d_edge_l = halves_f32(d_edge)
    d_pair = jnp.concatenate([d_edge_h, d_edge_l], axis=0).astype(BF16)

    spread = dot(d_pair, jnp.concatenate([hot_owned, hot_y, hot_x], axis=0), (1, 1))
    spread = spread[:4] + spread[8:12]
    mine = (spread[:, 384:], spread[:, :128], spread[:, 128:256], spread[:, 256:384])
    for number, value in enumerate(mine):
        send_c[number] = value

    def seat(ox, oy):
        return (ox + 2) * n_gy + oy % n_gy

    second = {}
    for mx, used in ((2, (3, 1)), (1, (1, 3)), (-2, (0, 1)), (-1, (0, 3)), (0, (0, 4))):
        second[mx] = [
            copy(2, send_c.at[pl.ds(*used)], recv_c.at[seat(-mx, -my), pl.ds(*used)], place(mx, my))
            for my in (2, -1, 1, 0)
            if (mx, my) != (0, 0)
        ]
    for c in second[2] + second[1]:
        c.start()

    @pl.when(row != 1)
    def _():
        for c in second[-2]:
            c.start()

    for c in second[-1] + second[0]:
        c.start()

    @pl.when(row == 1)
    def _():
        pl.semaphore_wait(known_sem, 2)
        for c in second[-2]:
            c.start()

    all_of(1, recv_m, 8).wait_recv()
    arriving = recv_m[...]
    slot_lane = lane % 8
    gains = lanes_at(arriving, 64 + slot_lane)
    listed = lanes_at(arriving, 72 + slot_lane)
    listed_row = jnp.sum(jnp.where(rows == field, listed, 0.0), axis=0, keepdims=True)
    listed_at = jnp.maximum(listed_row, 0.0).astype(jnp.int32)
    spots = iota((64, 128), 0)
    arriving_lists = jnp.where(field == 9, arriving, 0.0).astype(BF16)
    from_source = (iota((64, 8), 0) // 8 == iota((64, 8), 1)).astype(F32).astype(BF16)
    listed_col = jnp.sum(
        jnp.where(
            iota((64, 128), 1) == 72 + spots % 8, dot(from_source, arriving_lists), 0.0
        ),
        axis=1,
        keepdims=True,
    )
    spot_source = iota((64, 384), 0) // 8
    hot_spots = []
    for c, m in enumerate(MOVES):
        tile = recv_a[cell(*m)]
        faces = jnp.concatenate([tile[5:6], tile[6:7], tile[7:8]], axis=1)
        hit = jnp.where(spot_source == c, faces, -2.0) == listed_col
        hot_spots.append(hit.astype(F32).astype(BF16))
    hot_spots = jnp.concatenate(hot_spots, axis=1)

    all_of(0, recv_a, 8).wait_send()
    all_of(1, recv_m, 8).wait_send()

    @pl.when(row == RELAY)
    def _():
        all_of(3, recv_a, 3).wait_send()

    all_of(2, recv_c, 3 * n_gy - 1).wait_send()
    all_of(2, recv_c, 3 * n_gy - 1).wait_recv()

    def part(ox, oy, tile):
        if (ox, oy) == (0, 0):
            return mine[tile]
        return recv_c[seat(ox, oy), tile]

    third = lane // 32

    def inward(bx, by):
        sides = [jnp.where(low_y, part(bx, by - 1, 2), part(bx, by + 1, 2))]
        for ox, tile in ((bx - 1, 3), (bx + 1, 0)):
            above, beside = part(ox, by - 1, tile), part(ox, by, tile)
            below = part(ox, by + 1, tile)
            sides.append(jnp.where(third == 0, above, jnp.where(third == 1, beside, below)))
        high, low = halves_f32(jnp.concatenate(sides, axis=1))
        return jnp.concatenate([high, low, jnp.zeros((8, 384), F32)], axis=0).astype(BF16)

    def force_of(owned, back):
        return -(owned[:3] + back[:3] + back[4:7])

    force = force_of(mine[1], dot(inward(0, 0), hot_f, (1, 1)))
    new_frc_ref[...] = force
    new_vel_ref[...] = halfway + gain * force

    owned = jnp.zeros((8, 128), F32)
    for c, m in enumerate(MOVES):
        tile = jnp.concatenate([part(-m[0], -m[1], 1)] * 2, axis=0)
        owned = jnp.where(field == c, lanes_at(tile, listed_at), owned)
    back = dot(
        jnp.concatenate([inward(-m[0], -m[1]) for m in MOVES], axis=1), hot_spots, (1, 1)
    )
    back = jnp.concatenate([back, jnp.zeros((16, 64), F32)], axis=1)
    arriving_force = force_of(owned, back)
    push = jnp.zeros((8, 128), F32)
    for axis in range(3):
        value = jnp.broadcast_to(arriving_force[axis : axis + 1], (8, 128))
        push = jnp.where(field == 3 + axis, lanes_at(value, rows * 8 + slot_lane), push)
    result = arriving + gains * push
    for a in range(3):
        arr_ref[a] = jnp.concatenate(
            [
                jnp.zeros((1, 64), F32)
                if (a, b) == (1, 1)
                else result[MOVES.index((a - 1, b - 1)), 0:64].reshape(1, 64)
                for b in range(3)
            ],
            axis=0,
        )


def store(*refs):
    copies = [pltpu.make_async_copy(refs[i], refs[4 + i], refs[8].at[i]) for i in range(4)]
    for c in copies:
        c.start()
    for c in copies:
        c.wait()


def solution(mesh):
    n_gx, n_gy = mesh.shape["gx"], mesh.shape["gy"]
    vmem = pl.BlockSpec(memory_space=pltpu.VMEM)
    smem = pl.BlockSpec(memory_space=pltpu.SMEM)
    hbm = pl.BlockSpec(memory_space=pltpu.HBM)

    def hold(name, arg):
        return arg if name == "count" else pltpu.with_memory_space_constraint(arg, pltpu.HBM)

    def body(*args):
        def whole(*refs):
            kernel(n_gx, n_gy, *refs)

        atoms = jax.ShapeDtypeStruct(args[0].shape, F32)
        outs = (atoms, atoms, atoms, jax.ShapeDtypeStruct((3, 3, 64), F32))
        tile = pltpu.VMEM((8, 128), F32)
        scalars = ("inv_mass", "count")
        results = pl.pallas_call(
            whole,
            out_shape=outs,
            in_specs=[smem if name == "count" else hbm for name in INPUTS],
            out_specs=(vmem,) * 4,
            scratch_shapes=[
                (pltpu.SMEM if name in scalars else pltpu.VMEM)(arg.shape, arg.dtype)
                for name, arg in zip(INPUTS, args)
            ]
            + [tile, tile, pltpu.VMEM((12, 8, 128), F32), tile, tile]
            + [
                pltpu.VMEM((4, 4, 128), F32),
                pltpu.VMEM((5 * n_gy, 4, 4, 128), F32),
                pltpu.SemaphoreType.DMA((len(args),)),
                pltpu.SemaphoreType.DMA((4,)),
                pltpu.SemaphoreType.DMA((4,)),
                pltpu.SemaphoreType.REGULAR,
                pltpu.SemaphoreType.REGULAR,
            ],
            compiler_params=pltpu.CompilerParams(
                collective_id=0, has_side_effects=True, vmem_limit_bytes=VMEM_BYTES
            ),
        )(*(hold(name, arg) for name, arg in zip(INPUTS, args)))
        return pl.pallas_call(
            store,
            out_shape=outs,
            in_specs=[vmem] * 4,
            out_specs=(hbm,) * 4,
            scratch_shapes=[pltpu.SemaphoreType.DMA((4,))],
            compiler_params=pltpu.CompilerParams(vmem_limit_bytes=VMEM_BYTES),
        )(*results)

    bricks = ("gx", "gy")
    atoms_spec = P(None, bricks)
    in_specs = (
        (atoms_spec,) * 3
        + (P(bricks), P())
        + (P(bricks),) * 5
        + (P(bricks, None),)
        + (P(),) * 9
    )
    return jax.shard_map(
        body,
        mesh=mesh,
        in_specs=in_specs,
        out_specs=(atoms_spec,) * 3 + (P("gx", "gy", None),),
        check_vma=False,
    )
```

```python
import jax
import jax.numpy as jnp
from jax import lax
from jax.experimental import pallas as pl
from jax.experimental.pallas import tpu as pltpu
from jax.sharding import PartitionSpec as P

BOX_SIDE = 2.0
CUTOFF = 2.0
TIME_STEP = 0.05
WIDTHS = tuple((0.1 * 20.0 ** (k / 7.0) for k in range(8)))
Y20 = 0.28867513459481287
MESH = pl.DeviceIdType.MESH
F32 = jnp.float32
BF16 = jnp.bfloat16
VMEM_BYTES = 32 * 1024 * 1024

MOVES = tuple((a, b) for a in (-1, 0, 1) for b in (-1, 0, 1) if (a, b) != (0, 0))
ROW = 32
RELAY = 3
FAR_FIRST = tuple(sorted(MOVES, key=lambda move: -abs(move[0])))


INPUTS = (
    "pos",
    "vel",
    "frc",
    "spec",
    "inv_mass",
    "xface",
    "yface",
    "center",
    "neighbor",
    "count",
    "migrants",
    "emb_c",
    "emb_n",
    "radial",
    "tensor1",
    "mix1",
    "tensor2",
    "mix2",
    "final",
    "eout",
)
FIRST = ("spec", "inv_mass", "frc", "vel", "pos", "xface", "yface")
LOAD_ORDER = FIRST + tuple(name for name in INPUTS if name not in FIRST and name != "count")


def cell(dx, dy):
    return (dx + 1) * 3 + dy + 1


def iota(shape, dim):
    return lax.broadcasted_iota(jnp.int32, shape, dim)


def halves(value):
    high = value.astype(BF16)
    low = (value - high.astype(F32)).astype(BF16)
    return high, low


def halves_f32(value):
    high = value.astype(BF16).astype(F32)
    return high, value - high


def doubled(high, low):
    return (
        jnp.concatenate([jnp.concatenate([high, low], axis=1)] * 2, axis=0),
        jnp.concatenate([jnp.concatenate([high] * 2, axis=1), jnp.concatenate([low] * 2, axis=1)], axis=0),
    )


def dot(left, right, contract=(1, 0)):
    return lax.dot_general(
        left, right, (((contract[0],), (contract[1],)), ((), ())), preferred_element_type=F32
    )


def lanes_at(tile, index):
    return jnp.take_along_axis(
        tile, jnp.broadcast_to(index, tile.shape), axis=1, mode="promise_in_bounds"
    )


def sigmoid(value):
    return 0.5 + 0.5 * jnp.tanh(0.5 * value)


def row_const(values, shape):
    rows = iota(shape, 0)
    result = jnp.zeros(shape, F32)
    for index, value in enumerate(values):
        result = jnp.where(rows == index, F32(value), result)
    return result


def kernel(n_gx, n_gy, *refs):
    count = len(INPUTS)
    sources, refs = refs[:count], refs[count:]
    (new_pos_ref, new_vel_ref, new_frc_ref, arr_ref), refs = refs[:4], refs[4:]
    local, refs = refs[:count], refs[count:]
    send_x, send_y, recv_a, send_m, recv_m, send_c, recv_c, load_sems, sems_out, sems_in = refs[:10]
    relay_sem, known_sem = refs[10:]
    gx = lax.axis_index("gx")
    gy = lax.axis_index("gy")
    row = lax.rem(gx, ROW)

    def place(dx, dy):
        return (lax.rem(gx + (dx + n_gx), n_gx), lax.rem(gy + (dy + n_gy), n_gy))

    def signal(semaphore, target):
        pl.semaphore_signal(semaphore, inc=1, device_id=target, device_id_type=MESH)

    barrier = pltpu.get_barrier_semaphore()

    @pl.when(row == RELAY)
    def _():
        signal(barrier, place(ROW - 1 - RELAY, 0))
        for dy in (-1, 0, 1):
            signal(barrier, place(ROW - RELAY, dy))

    @pl.when(row < ROW - 1)
    def _():
        for dy in (-1, 0, 1):
            signal(barrier, place(1, dy))

    for move in FAR_FIRST:
        if move[0] != 1:
            signal(barrier, place(*move))

    loads = {
        name: pltpu.make_async_copy(sources[i], local[i], load_sems.at[i])
        for i, name in enumerate(INPUTS)
        if name != "count"
    }
    refs_of = dict(zip(INPUTS, local))
    count_ref = sources[INPUTS.index("count")]
    for name in LOAD_ORDER:
        loads[name].start()

    def loaded(*wanted):
        for name in wanted:
            loads[name].wait()
        return [refs_of[name] for name in wanted]

    def copy(phase, source, target, device, arrive=None):
        return pltpu.make_async_remote_copy(
            src_ref=source,
            dst_ref=target,
            send_sem=sems_out.at[phase],
            recv_sem=sems_in.at[phase if arrive is None else arrive],
            device_id=device,
            device_id_type=MESH,
        )

    def all_of(phase, ref, tiles):
        whole = ref.at[pl.ds(0, tiles)]
        return copy(phase, whole, whole, place(1, 0))

    lane = iota((1, 128), 1)
    rows = iota((8, 128), 0)
    low_x = (lane % 64) < 32
    low_y = lane < 64

    spec_ref, inv_mass_ref, frc_ref, vel_ref, pos_ref, xface_ref, yface_ref = loaded(*FIRST)
    species = spec_ref[...].reshape(1, 128)
    inv_mass = jnp.zeros((1, 128), F32)
    for k in range(inv_mass_ref.shape[0]):
        inv_mass = jnp.where(species == k, inv_mass_ref[k], inv_mass)
    halfway = vel_ref[...] + 0.5 * TIME_STEP * frc_ref[...] * inv_mass
    coords = pos_ref[...] + TIME_STEP * halfway
    new_pos_ref[...] = coords
    species_row = species.astype(F32)
    minus = jnp.full((1, 128), -1.0, F32)
    record = jnp.concatenate([coords, species_row, minus, jnp.zeros((3, 128), F32)], axis=0)

    xface = xface_ref[...].reshape(1, 64)
    xface2 = jnp.concatenate([xface, xface], axis=1)
    yface = yface_ref[...].reshape(1, 128)
    y_owned = yface < 128
    blank = jnp.full((1, 32), -1, jnp.int32)
    lower = jnp.concatenate([xface[:, :32]] * 3 + [blank], axis=1)
    upper = jnp.concatenate([xface[:, 32:]] * 3 + [blank], axis=1)
    owned_y = jnp.where(y_owned, yface, -1)
    lists = jnp.concatenate(
        [
            jnp.zeros((4, 128), F32),
            yface.astype(F32),
            owned_y.astype(F32),
            lower.astype(F32),
            upper.astype(F32),
        ],
        axis=0,
    )
    send_x[...] = jnp.where(rows < 5, lanes_at(record, xface2), lists)
    send_y[...] = jnp.where(rows < 4, lanes_at(record, jnp.where(y_owned, yface, 0)), lists)
    pl.semaphore_wait(barrier, len(MOVES) + row // (ROW - 1))

    @pl.when(row == ROW - 1)
    def _():
        signal(relay_sem, place(RELAY + 1 - ROW, 0))

    at_start = 1 - (row + (ROW - 1)) // ROW
    last = place(ROW - 1 - RELAY, 0)
    for m in FAR_FIRST:
        source, slot = send_y if m[0] == 0 else send_x, cell(*m)
        if m[0] == -1:
            there = slot + at_start * (10 + m[1] - slot)
            target = place(-1 - at_start * (ROW - 1 - RELAY), m[1])
            copy(0, source, recv_a.at[there], target, 3 * at_start).start()
        else:
            copy(0, source, recv_a.at[slot], place(*m)).start()

    (migrants_ref,) = loaded("migrants")
    slots = jnp.concatenate([migrants_ref[...]] * 16, axis=1)
    valid = slots >= 0
    at = jnp.where(valid, slots, 0)
    field = lane // 8
    gain = 0.5 * TIME_STEP * inv_mass
    out = jnp.where(field == 7, 1.0, jnp.zeros((8, 128), F32))
    fields = [coords[0:1], coords[1:2], coords[2:3]]
    fields += [halfway[0:1], halfway[1:2], halfway[2:3], species_row, None, gain]
    for number, value in enumerate(fields):
        if value is not None:
            out = jnp.where(field == number, lanes_at(jnp.broadcast_to(value, (8, 128)), at), out)
    dx_col = row_const([BOX_SIDE * m[0] for m in MOVES], (8, 128))
    dy_col = row_const([BOX_SIDE * m[1] for m in MOVES], (8, 128))
    out = out - jnp.where(field == 0, dx_col, jnp.where(field == 1, dy_col, 0.0))
    out = jnp.where(valid, out, 0.0)
    send_m[...] = jnp.where(field == 9, slots.astype(F32), out)
    leave = [
        copy(1, send_m.at[pl.ds(c, 1)], recv_m.at[pl.ds(c, 1)], place(*m))
        for c, m in enumerate(MOVES)
    ]
    for m, c in zip(MOVES, leave):
        if m[0] == -1:
            pl.when(row > 0)(c.start)
        else:
            c.start()

    neighbor_ref, center_ref = loaded("neighbor", "center")
    neighbor = neighbor_ref[...].reshape(1, 256)
    center = center_ref[...].reshape(1, 256)
    live = iota((1, 256), 1) < count_ref[0]
    place_n = jnp.where(
        neighbor < 128,
        neighbor,
        jnp.where(neighbor < 192, ((neighbor - 128) ^ 32) + 128, ((neighbor - 192) ^ 64) + 256),
    )

    def edge_side(tile, index):
        return jnp.concatenate(
            [lanes_at(tile, index[:, 128 * h : 128 * h + 128] & 127) for h in range(2)], axis=1
        )

    own = edge_side(record, center)
    near_owned = edge_side(record, place_n)
    hot_n = (iota((384, 256), 0) == place_n).astype(F32)
    hot_c = (iota((128, 256), 0) == center).astype(F32)
    hot_owned = (hot_n[:128] - hot_c).astype(BF16)
    hot_y = hot_n[256:].astype(BF16)
    ghost = place_n - 128
    in_x = (ghost >= 0) & (ghost < 64)
    at_x = jnp.where(in_x, jnp.where(ghost < 32, 32, 128) + ghost, -1)
    face_rows = jnp.concatenate([owned_y, lower, upper], axis=1)
    hot_f = (iota((128, 384), 0) == face_rows).astype(F32).astype(BF16)
    c_live = center.astype(F32)
    rows_e = iota((8, 256), 0)
    left_c = jnp.where(rows_e == 0, jnp.where(live, c_live, -1.0), jnp.where(rows_e == 1, 1.0, 0.0))
    right_c = jnp.where(rows_e == 0, 1.0, jnp.where(rows_e == 1, jnp.where(live, -c_live, 2.0), 0.0))
    same = dot(left_c.astype(BF16), right_c.astype(BF16), (0, 0)) == 0.0
    k0 = same.astype(F32).astype(BF16)

    def merged(tensor_ref, mix_ref):
        tensor = tensor_ref[...]
        width = tensor.shape[1]
        high, low = halves(
            jnp.concatenate(
                [
                    lax.dot_general(
                        tensor,
                        mix_ref[pl.ds(width * deg, width), :],
                        (((1,), (0,)), ((), ())),
                        precision=lax.Precision.HIGHEST,
                        preferred_element_type=F32,
                    )
                    for deg in range(3)
                ],
                axis=1,
            )
        )
        blocks = [
            doubled(high[:, 128 * d : 128 * d + 128], low[:, 128 * d : 128 * d + 128])
            for d in range(3)
        ]
        return tuple(jnp.concatenate(each, axis=1) for each in zip(*blocks))

    tensor1_ref, mix1_ref, tensor2_ref, mix2_ref = loaded("tensor1", "mix1", "tensor2", "mix2")
    final_ref, radial_ref, emb_c_ref, emb_n_ref = loaded("final", "radial", "emb_c", "emb_n")
    (eout_ref,) = loaded("eout")
    layers = (merged(tensor1_ref, mix1_ref), merged(tensor2_ref, mix2_ref))
    final_forward, final_backward = doubled(*halves(final_ref[...]))
    pad3 = jnp.zeros((3, 128), F32)
    table = jnp.concatenate([radial_ref[...], emb_c_ref[...], pad3, emb_n_ref[...], pad3], axis=0)
    table_h, table_l = halves_f32(table)
    table_cat = jnp.concatenate(
        [table_h, table_l, table_h[:8], jnp.zeros((8, 128), F32)], axis=0
    ).astype(BF16)
    rad_h, rad_l = table_h[:8], table_l[:8]
    rad_cat = jnp.concatenate([rad_h, rad_l], axis=0).astype(BF16)

    @pl.when(row == RELAY)
    def _():
        all_of(3, recv_a, 3).wait_recv()
        pl.semaphore_wait(relay_sem, 1)
        for dy in (-1, 0, 1):
            copy(3, recv_a.at[10 + dy], recv_a.at[cell(-1, dy)], last, 0).start()

    all_of(0, recv_a, 8).wait_recv()

    @pl.when(row == 0)
    def _():
        signal(known_sem, place(1, 0))
        signal(known_sem, place(1, 1))
        for m, c in zip(MOVES, leave):
            if m[0] == -1:
                c.start()

    def pick4(tiles):
        quarter = lane // 32
        result = tiles[3]
        for q in (2, 1, 0):
            result = jnp.where(quarter == q, tiles[q], result)
        return result

    x_shift = jnp.where(rows == 0, jnp.where(low_x, BOX_SIDE, -BOX_SIDE), 0.0)
    y_shift = jnp.where(rows == 1, jnp.where(low_y, BOX_SIDE, -BOX_SIDE), 0.0)
    ghost_x = jnp.where(low_x, recv_a[cell(-1, 0)], recv_a[cell(1, 0)]) + x_shift
    far_x = (
        pick4(
            [recv_a[cell(-1, -1)], recv_a[cell(1, -1)], recv_a[cell(-1, 1)], recv_a[cell(1, 1)]]
        )
        + x_shift
    )
    ghost_y = jnp.where(low_y, recv_a[cell(0, -1)], recv_a[cell(0, 1)])
    listed = ghost_y[4:5].astype(jnp.int32)
    via_x = listed >= 128
    far_lane = jnp.where(via_x, ((listed - 128) ^ 32) + jnp.where(low_y, 0, 64), 0)
    ghost_y = jnp.where(via_x, lanes_at(far_x, far_lane), ghost_y) + y_shift
    far_at = (far_lane + 96 * ((far_lane // 32) % 2)).astype(F32)
    ghost_y = jnp.where(rows == 4, jnp.where(via_x, far_at, -1.0), ghost_y)

    near = jnp.where(
        place_n < 128,
        near_owned,
        jnp.where(place_n < 256, edge_side(ghost_x, place_n), edge_side(ghost_y, place_n)),
    )
    side = iota((256, 256), 0)
    hot_x = (side == jnp.where(in_x, at_x, near[4:5].astype(jnp.int32))).astype(F32).astype(BF16)

    offset = (near - own) * (1.0 / CUTOFF)
    ux, uy, uz = offset[0:1], offset[1:2], offset[2:3]
    squared = ux * ux + uy * uy + uz * uz
    tees = jnp.concatenate(
        [
            ux,
            uy,
            uz,
            ux * uy,
            uy * uz,
            uz * ux,
            0.5 * (ux * ux - uy * uy),
            (2.0 * uz * uz - ux * ux - uy * uy) * Y20,
        ],
        axis=0,
    )
    minus_inv_w = row_const([-1.0 / w for w in WIDTHS], (8, 256))
    radial = jnp.exp(squared * minus_inv_w)
    hot_sc = (rows_e == own[3:4].astype(jnp.int32)).astype(F32)
    hot_sn = (rows_e == near[3:4].astype(jnp.int32)).astype(F32)
    radial_h, radial_l = halves_f32(radial)
    features = jnp.concatenate(
        [radial_h, hot_sc, hot_sn, radial_h, hot_sc, hot_sn, radial_l, jnp.zeros((8, 256), F32)],
        axis=0,
    ).astype(BF16)
    hidden_pre = dot(features, table_cat, (0, 0))

    tees_h, tees_l = halves_f32(tees)
    tees_r = jnp.concatenate([tees_h, tees_l, tees_h, jnp.zeros((8, 256), F32)], axis=0).astype(BF16)

    def degree(mask):
        left = jnp.concatenate([tees_h, tees_h, tees_l, jnp.zeros((8, 256), F32)], axis=0)
        left = jnp.where(mask, left, 0.0).astype(BF16)
        return halves(jnp.where(same, dot(left, tees_r, (0, 0)), 0.0))

    row32 = iota((32, 256), 0) % 8
    k1_h, k1_l = degree(row32 < 3)
    k2_h, k2_l = degree(row32 >= 3)

    k_wide = jnp.concatenate([k0, k1_h, k2_h], axis=1)
    k_wide_l = jnp.concatenate([k1_l, k2_l], axis=1)
    k_tall = jnp.concatenate([k0, k1_h, k2_h], axis=0)
    k_tall_l = jnp.concatenate([k1_l, k2_l], axis=0)

    sig = sigmoid(hidden_pre)
    hidden = hidden_pre * sig
    slope0 = sig * (1.0 + hidden_pre * (1.0 - sig))
    slopes, values = [], []
    for forward, _ in layers:
        hid_h, hid_l = halves(hidden)
        hid = jnp.concatenate([hid_h, hid_l], axis=1)
        split = []
        for d in range(3):
            pair = dot(hid, forward[:, 256 * d : 256 * d + 256])
            split.append(halves(pair[:, :128] + pair[:, 128:]))
        values.append(split)
        both = sum(dot(k, jnp.concatenate(split[d], axis=1)) for d, k in enumerate((k0, k1_h, k2_h)))
        rest = dot(k1_l, split[1][0]) + dot(k2_l, split[2][0])
        pre = both[:, :128] + both[:, 128:] + rest
        sig = sigmoid(pre)
        hidden = hidden + pre * sig
        slopes.append(sig * (1.0 + pre * (1.0 - sig)))

    hid_h, hid_l = halves(hidden)
    pre = dot(jnp.concatenate([hid_h, hid_l], axis=1), final_forward)
    pre = pre[:, :128] + pre[:, 128:]
    sig = sigmoid(pre)
    back = eout_ref[...].reshape(1, 128) * (sig * (1.0 + pre * (1.0 - sig)))
    back_h, back_l = halves(back)
    grad = dot(jnp.concatenate([back_h, back_l], axis=1), final_backward, (1, 1))
    grad = grad[:, :128] + grad[:, 128:]
    downs = []
    for index in (1, 0):
        _, backward = layers[index]
        down_h, down_l = halves(grad * slopes[index])
        downs.append((down_h, down_l))
        both = dot(k_tall, jnp.concatenate([down_h, down_l], axis=1))
        rest = dot(k_tall_l, down_h)
        parts = [both[:256, :128] + both[:256, 128:]]
        for d in (1, 2):
            at = slice(256 * d, 256 * d + 256)
            parts.append(both[at, :128] + both[at, 128:] + rest[256 * d - 256 : 256 * d])
        both = dot(
            jnp.concatenate([half for part in parts for half in halves(part)], axis=1),
            backward,
            (1, 1),
        )
        grad = grad + (both[:, :128] + both[:, 128:])
    (d2_h, d2_l), (d1_h, d1_l) = downs
    outer_left = jnp.concatenate([d1_h, d2_h, d1_l, d2_l, d1_h, d2_h], axis=1)
    moved = []
    for d in (1, 2):
        (v1_h, v1_l), (v2_h, v2_l) = values[0][d], values[1][d]
        outer = (
            dot(jnp.concatenate([d2_h, d2_l], axis=1), jnp.concatenate([v2_h, v2_h], axis=1), (1, 1))
            + dot(jnp.concatenate([d1_h, d1_l], axis=1), jnp.concatenate([v1_h, v1_h], axis=1), (1, 1))
            + dot(jnp.concatenate([d1_h, d2_h], axis=1), jnp.concatenate([v1_l, v2_l], axis=1), (1, 1))
        )
        turned = jnp.where(same, outer, 0.0)
        out_h, out_l = halves(turned + turned.T)
        pair = jnp.concatenate([tees_h, tees_l], axis=0).astype(BF16)
        high_t = tees_h.astype(BF16)
        first_part = dot(pair, out_h)
        moved.append(first_part[:8] + first_part[8:] + dot(high_t, out_l))
    d_tees = jnp.where(rows_e < 3, moved[0], moved[1])

    g_h, g_l = halves(grad * slope0)
    d_radial = dot(rad_cat, g_h, (1, 1))
    d_radial = d_radial[:8] + d_radial[8:] + dot(rad_cat[:8], g_l, (1, 1))
    d_squared = 2.0 * jnp.sum(d_radial * radial * minus_inv_w, axis=0, keepdims=True)
    dxy, dyz, dzx = d_tees[3:4], d_tees[4:5], d_tees[5:6]
    dxx, dzz = d_tees[6:7], (2.0 * Y20) * d_tees[7:8]
    dux = d_tees[0:1] + ux * (d_squared + dxx - dzz) + uy * dxy + uz * dzx
    duy = d_tees[1:2] + uy * (d_squared - dxx - dzz) + ux * dxy + uz * dyz
    duz = d_tees[2:3] + uz * (d_squared + 2.0 * dzz) + uy * dyz + ux * dzx
    d_edge = jnp.concatenate([dux, duy, duz, jnp.zeros((5, 256), F32)], axis=0)
    d_edge = jnp.where(live, d_edge * (1.0 / CUTOFF), 0.0)
    d_edge_h, d_edge_l = halves_f32(d_edge)
    d_pair = jnp.concatenate([d_edge_h, d_edge_l], axis=0).astype(BF16)

    spread = dot(d_pair, jnp.concatenate([hot_owned, hot_y, hot_x], axis=0), (1, 1))
    spread = spread[:4] + spread[8:12]
    mine = (spread[:, 384:], spread[:, :128], spread[:, 128:256], spread[:, 256:384])
    for number, value in enumerate(mine):
        send_c[number] = value

    def seat(ox, oy):
        return (ox + 2) * n_gy + oy % n_gy

    second = []
    for mx in (2, 1, -2, -1, 0):
        for my in (2, -1, 1, 0):
            if (mx, my) != (0, 0):
                slot = seat(-mx, -my)
                used = {-2: (0, 1), -1: (0, 3), 0: (0, 4), 1: (1, 3), 2: (3, 1)}[mx]
                c = copy(2, send_c.at[pl.ds(*used)], recv_c.at[slot, pl.ds(*used)], place(mx, my))
                second.append(c)
                if mx == -2:
                    pl.when(row != 1)(c.start)
                else:
                    c.start()

    @pl.when(row == 1)
    def _():
        pl.semaphore_wait(known_sem, 2)
        for c in second[2 * n_gy : 3 * n_gy]:
            c.start()

    all_of(1, recv_m, 8).wait_recv()
    arriving = recv_m[...]
    slot_lane = lane % 8
    gains = lanes_at(arriving, 64 + slot_lane)
    listed = lanes_at(arriving, 72 + slot_lane)
    listed_row = jnp.sum(jnp.where(rows == field, listed, 0.0), axis=0, keepdims=True)
    listed_at = jnp.maximum(listed_row, 0.0).astype(jnp.int32)
    spots = iota((64, 128), 0)
    arriving_lists = jnp.where(field == 9, arriving, 0.0).astype(BF16)
    from_source = (iota((64, 8), 0) // 8 == iota((64, 8), 1)).astype(F32).astype(BF16)
    listed_col = jnp.sum(
        jnp.where(
            iota((64, 128), 1) == 72 + spots % 8, dot(from_source, arriving_lists), 0.0
        ),
        axis=1,
        keepdims=True,
    )
    spot_source = iota((64, 384), 0) // 8
    hot_spots = []
    for c, m in enumerate(MOVES):
        tile = recv_a[cell(*m)]
        faces = jnp.concatenate([tile[5:6], tile[6:7], tile[7:8]], axis=1)
        hit = jnp.where(spot_source == c, faces, -2.0) == listed_col
        hot_spots.append(hit.astype(F32).astype(BF16))
    hot_spots = jnp.concatenate(hot_spots, axis=1)

    all_of(2, recv_c, 3 * n_gy - 1).wait_recv()

    def part(ox, oy, tile):
        if (ox, oy) == (0, 0):
            return mine[tile]
        return recv_c[seat(ox, oy), tile]

    third = lane // 32

    def inward(bx, by):
        sides = [jnp.where(low_y, part(bx, by - 1, 2), part(bx, by + 1, 2))]
        for ox, tile in ((bx - 1, 3), (bx + 1, 0)):
            above, beside = part(ox, by - 1, tile), part(ox, by, tile)
            below = part(ox, by + 1, tile)
            sides.append(jnp.where(third == 0, above, jnp.where(third == 1, beside, below)))
        high, low = halves_f32(jnp.concatenate(sides, axis=1))
        return jnp.concatenate([high, low, jnp.zeros((8, 384), F32)], axis=0).astype(BF16)

    def force_of(owned, back):
        return -(owned[:3] + back[:3] + back[4:7])

    force = force_of(mine[1], dot(inward(0, 0), hot_f, (1, 1)))
    new_frc_ref[...] = force
    new_vel_ref[...] = halfway + gain * force

    owned = jnp.zeros((8, 128), F32)
    for c, m in enumerate(MOVES):
        tile = jnp.concatenate([part(-m[0], -m[1], 1)] * 2, axis=0)
        owned = jnp.where(field == c, lanes_at(tile, listed_at), owned)
    back = dot(
        jnp.concatenate([inward(-m[0], -m[1]) for m in MOVES], axis=1), hot_spots, (1, 1)
    )
    back = jnp.concatenate([back, jnp.zeros((16, 64), F32)], axis=1)
    arriving_force = force_of(owned, back)
    push = jnp.zeros((8, 128), F32)
    for axis in range(3):
        value = jnp.broadcast_to(arriving_force[axis : axis + 1], (8, 128))
        push = jnp.where(field == 3 + axis, lanes_at(value, rows * 8 + slot_lane), push)
    result = arriving + gains * push
    for a in range(3):
        arr_ref[a] = jnp.concatenate(
            [
                jnp.zeros((1, 64), F32)
                if (a, b) == (1, 1)
                else result[MOVES.index((a - 1, b - 1)), 0:64].reshape(1, 64)
                for b in range(3)
            ],
            axis=0,
        )
    all_of(0, recv_a, 8).wait_send()
    all_of(1, recv_m, 8).wait_send()
    all_of(2, recv_c, 3 * n_gy - 1).wait_send()

    @pl.when(row == RELAY)
    def _():
        all_of(3, recv_a, 3).wait_send()


def store(*refs):
    copies = [pltpu.make_async_copy(refs[i], refs[4 + i], refs[8].at[i]) for i in range(4)]
    for c in copies:
        c.start()
    for c in copies:
        c.wait()


def solution(mesh):
    n_gx, n_gy = mesh.shape["gx"], mesh.shape["gy"]
    vmem = pl.BlockSpec(memory_space=pltpu.VMEM)
    smem = pl.BlockSpec(memory_space=pltpu.SMEM)
    hbm = pl.BlockSpec(memory_space=pltpu.HBM)

    def hold(name, arg):
        return arg if name == "count" else pltpu.with_memory_space_constraint(arg, pltpu.HBM)

    def body(*args):
        def whole(*refs):
            kernel(n_gx, n_gy, *refs)

        atoms = jax.ShapeDtypeStruct(args[0].shape, F32)
        outs = (atoms, atoms, atoms, jax.ShapeDtypeStruct((3, 3, 64), F32))
        tile = pltpu.VMEM((8, 128), F32)
        scalars = ("inv_mass", "count")
        results = pl.pallas_call(
            whole,
            out_shape=outs,
            in_specs=[smem if name == "count" else hbm for name in INPUTS],
            out_specs=(vmem,) * 4,
            scratch_shapes=[
                (pltpu.SMEM if name in scalars else pltpu.VMEM)(arg.shape, arg.dtype)
                for name, arg in zip(INPUTS, args)
            ]
            + [tile, tile, pltpu.VMEM((12, 8, 128), F32), tile, tile]
            + [
                pltpu.VMEM((4, 4, 128), F32),
                pltpu.VMEM((5 * n_gy, 4, 4, 128), F32),
                pltpu.SemaphoreType.DMA((len(args),)),
                pltpu.SemaphoreType.DMA((4,)),
                pltpu.SemaphoreType.DMA((4,)),
                pltpu.SemaphoreType.REGULAR,
                pltpu.SemaphoreType.REGULAR,
            ],
            compiler_params=pltpu.CompilerParams(
                collective_id=0, has_side_effects=True, vmem_limit_bytes=VMEM_BYTES
            ),
        )(*(hold(name, arg) for name, arg in zip(INPUTS, args)))
        return pl.pallas_call(
            store,
            out_shape=outs,
            in_specs=[vmem] * 4,
            out_specs=(hbm,) * 4,
            scratch_shapes=[pltpu.SemaphoreType.DMA((4,))],
            compiler_params=pltpu.CompilerParams(vmem_limit_bytes=VMEM_BYTES),
        )(*results)

    bricks = ("gx", "gy")
    atoms_spec = P(None, bricks)
    in_specs = (
        (atoms_spec,) * 3
        + (P(bricks), P())
        + (P(bricks),) * 5
        + (P(bricks, None),)
        + (P(),) * 9
    )
    return jax.shard_map(
        body,
        mesh=mesh,
        in_specs=in_specs,
        out_specs=(atoms_spec,) * 3 + (P("gx", "gy", None),),
        check_vma=False,
    )
```
